256 devices in a mesh: seq: 64 (over z, x, core), head: 4 (over y).
Axes of the slice: x: 4, y: 4, z: 8, core: 2. Of those that a mesh axis runs over, the one named last changes fastest.
Arguments:
- query: bfloat16 [32768, 4096], P(('seq', 'head')), may hold values from -256 to 256
- keys: bfloat16 [32768, 1024], P(('seq', 'head')), may hold values from -6 to 6
- values: bfloat16 [32768, 1024], P(('seq', 'head')), may hold values from -6 to 6
- chosen: int32 [64, 8, 3], P('seq', 'head'), may hold values from -1 to 62, as said below
Outputs:
- attended: bfloat16 [32768, 4096], P(('seq', 'head'))
The draws below stay inside these ranges and needn't reach their ends.
Inputs may be any that keep to these rules, and one draw needn't show every extreme that they name: `chosen`: for query block b every entry is -1 or one of the blocks b - 12 to b - 1. For each head shard s, the 8 / 4 key heads s * (8 / 4) to (s + 1) * (8 / 4) - 1 together never name one block twice. Block b - 1 is named by one of them for every b >= 1; query block b names min(b, 3 * 8 / 4) blocks over those heads.
All inputs are finite; a program needn't handle non-finite values.
Results may differ from the reference program's by a relative error of at most 0.0035.
Values may be sent and summed in bfloat16 or wider, within the bound.
A program may use at most 128 MiB of HBM per device.

```python
import math
import jax
import jax.numpy as jnp
from jax import lax

HQ = 32
HK = 8
DH = 128
BLK = 512
TOPK = 3
NBLK = 64
LENGTH = 32768
WIN = 12
N_HEAD = 4


def shared_keys(key):
    return jnp.clip(jax.random.normal(key, (LENGTH, HK * DH), jnp.float32), -6.0, 6.0)


def draw_keys(key, part):
    base = shared_keys(key)
    return base.astype(jnp.bfloat16)


def draw_query(key, part):
    key = jax.random.fold_in(key, 2)
    drawn = 2.0 * jnp.clip(jax.random.normal(key, (LENGTH, HQ * DH), jnp.float32), -6.0, 6.0)
    return drawn.astype(jnp.bfloat16)


def draw_chosen(key, part):
    key = jax.random.fold_in(key, 11)
    first, second, third = jax.random.split(key, 3)
    nblk = NBLK
    per_shard = HK // N_HEAD * TOPK
    noise = jax.random.randint(first, (nblk, N_HEAD, nblk), 0, 1 << 16)
    coin = jax.random.randint(second, (nblk, N_HEAD, 1), 0, 2)
    row = jnp.arange(nblk)[:, None, None]
    col = jnp.arange(nblk)[None, None, :]
    score = noise * nblk + col + (col == row - 1).astype(jnp.int32) * (1 << 27) + (col == row - WIN).astype(jnp.int32) * coin * (1 << 26)
    score = jnp.where((col < row) & (col >= row - WIN), score, -1)
    top_vals, top_idx = lax.top_k(score, per_shard)
    entry = jnp.where(top_vals >= 0, top_idx, -1).astype(jnp.int32)
    shuffle = jax.random.randint(third, (nblk, N_HEAD, per_shard), 0, 1 << 20) * per_shard + jnp.arange(per_shard)
    order = jnp.argsort(shuffle, axis=-1, stable=True)
    entry = jnp.take_along_axis(entry, order, axis=-1)
    return entry.reshape(nblk, HK, TOPK).astype(jnp.int32)


def block_scale(own_key, dims, cuts, low, largest):
    def one(axis_at, shards_of):
        draws = jax.random.uniform(jax.random.fold_in(jax.random.fold_in(own_key, 6), axis_at), (shards_of,), jnp.float32, low / len(cuts), largest / len(cuts))
        return jnp.repeat(jnp.exp(draws), dims[axis_at] // shards_of).reshape((-1,) + (1,) * (len(dims) - axis_at - 1))

    level = one(*cuts[0])
    for cut in cuts[1:]:
        level = level * one(*cut)
    return level


def scatter_about(own_key, extent, scale, reach, cuts=(), kind=jnp.bfloat16):
    drawn = jax.random.normal(own_key, extent, jnp.float32) * scale
    if len(cuts) > 0:
        drawn = block_scale(own_key, extent, cuts, -0.22, 0.18) * drawn
    return jnp.clip(drawn, min=-reach, max=reach).astype(kind)


def setup_inputs(seed: int = 0) -> dict:
    streams_of = jax.random.split(jax.random.key(seed), 5)
    query = draw_query(jax.random.fold_in(streams_of[4], 71), 0)
    keys = draw_keys(jax.random.fold_in(streams_of[4], 71), 0)
    values = scatter_about(streams_of[2], (LENGTH, HK * DH), 1.0, 6.0, ((0, 256),))
    chosen = draw_chosen(jax.random.fold_in(streams_of[4], 71), 0)
    return {"query": query, "keys": keys, "values": values, "chosen": chosen}


def reference(query, keys, values, chosen):
    nblk = query.shape[0] // BLK
    grp = HQ // HK
    scale = 1.0 / math.sqrt(DH)
    qb = query.reshape(nblk, BLK, HK, grp, DH)
    kt = keys.reshape(nblk, BLK, HK, DH).transpose(0, 2, 1, 3)
    vt = values.reshape(nblk, BLK, HK, DH).transpose(0, 2, 1, 3)
    lower = jnp.arange(BLK)[:, None] >= jnp.arange(BLK)[None, :]
    heads = jnp.arange(HK)[:, None]

    def one_block(b):
        qf = qb[b].astype(jnp.float32).transpose(1, 2, 0, 3)
        idx = chosen[b]
        valid = idx >= 0
        safe = jnp.maximum(idx, 0)
        key_cat = jnp.concatenate([kt[b][:, None], kt[safe, heads]], axis=1).reshape(HK, (TOPK + 1) * BLK, DH)
        val_cat = jnp.concatenate([vt[b][:, None], vt[safe, heads]], axis=1).reshape(HK, (TOPK + 1) * BLK, DH)
        own_mask = jnp.broadcast_to(lower[None], (HK, BLK, BLK))
        far_mask = jnp.broadcast_to(valid[:, None, :, None], (HK, BLK, TOPK, BLK)).reshape(HK, BLK, TOPK * BLK)
        mask = jnp.concatenate([own_mask, far_mask], axis=2)[:, None]
        score = jnp.einsum('hgqd,hkd->hgqk', qf, key_cat.astype(jnp.float32)) * scale
        score = jnp.where(mask, score, -1e+30)
        top = lax.optimization_barrier(jnp.max(score, axis=-1, keepdims=True))
        expo = jnp.where(mask, jnp.exp(score - top), 0.0)
        total = lax.optimization_barrier(jnp.sum(expo, axis=-1, keepdims=True))
        weight = expo.astype(jnp.bfloat16).astype(jnp.float32)
        summed = jnp.einsum('hgqk,hkd->hgqd', weight, val_cat.astype(jnp.float32))
        result = summed / total
        return result.transpose(2, 0, 1, 3).reshape(BLK, HQ * DH).astype(jnp.bfloat16)
    return lax.map(one_block, jnp.arange(nblk)).reshape(nblk * BLK, HQ * DH)
```

```python
import math

import jax
import jax.numpy as jnp
from jax import lax
from jax.experimental import pallas as pl
from jax.experimental.pallas import tpu as pltpu
from jax.sharding import PartitionSpec as P

HQ = 32
HK = 8
DH = 128
BLK = 512
TOPK = 3
GRP = HQ // HK
NHEAD = 4
HLOC = HK // NHEAD
TOK = BLK // NHEAD
NX = 4
SLOTS = 13
GROUPS = 2 * HLOC
PARTS = 2
PIECES = GROUPS * PARTS
ROWS = BLK // PARTS
WIDE = GRP * DH
NEG = -1e30
RATE = math.log2(math.e) / math.sqrt(DH)
MESH = pl.DeviceIdType.MESH


def kernel(nseq, chosen, query, keys, values, out, kv0, kv1, kv2, kv3, qbuf, obuf, scores, weights, totals,
           own_send, own_recv, q_send, q_recv, win_send, win_recv, sib_send, sib_recv,
           out_send, out_recv, local_sem):
    kv = (kv0, kv1, kv2, kv3)
    nz = nseq // (2 * NX)
    seq = lax.axis_index("seq")
    y = lax.axis_index("head")
    core = lax.rem(seq, 2)
    x = lax.rem(seq // 2, NX)
    z = seq // (2 * NX)

    def at(zz, xx):
        return ((zz * NX + xx) * 2 + core, y)

    up = at(lax.rem(z + 1, nz), x)
    down = at(lax.rem(z + nz - 1, nz), x)
    right = at(z, lax.rem(x + 1, NX))
    left = at(z, lax.rem(x + NX - 1, NX))
    sibling = (seq + 1 - 2 * core, y)

    def partner(o):
        return (seq, lax.rem(y + o, NHEAD))

    barrier = pltpu.get_barrier_semaphore()
    for who in [up, down, right, left, sibling, partner(1), partner(2), partner(3)]:
        pl.semaphore_signal(barrier, inc=1, device_id=who, device_id_type=MESH)
    pl.semaphore_wait(barrier, 8)

    def columns(start, width):
        return pl.ds(pl.multiple_of(start, DH), width)

    def remote(src, dst, send, recv, to):
        return pltpu.make_async_remote_copy(
            src_ref=src, dst_ref=dst, send_sem=send, recv_sem=recv, device_id=to, device_id_type=MESH)

    own_rows = pl.ds(pl.multiple_of(y * TOK, TOK), TOK)

    def kv_source(g, to_y):
        return (keys, values)[g % 2].at[:, columns((to_y * HLOC + g // 2) * DH, DH)]

    def kv_copy(o, g):
        to = partner(o)
        return remote(kv_source(g, to[1]), kv[g].at[0, own_rows], own_send.at[g], own_recv.at[g], to)

    def kv_local(g):
        return pltpu.make_async_copy(kv_source(g, y), kv[g].at[0, own_rows], local_sem.at[g])

    def q_source(h, to_y):
        return query.at[:, columns((to_y * HLOC + h) * WIDE, WIDE)]

    def q_copy(o, h):
        to = partner(o)
        return remote(q_source(h, to[1]), qbuf.at[h, y], q_send.at[h], q_recv.at[h], to)

    def q_local(h):
        return pltpu.make_async_copy(q_source(h, y), qbuf.at[h, y], local_sem.at[GROUPS + h])

    def out_place(to_y, h):
        return out.at[:, columns((to_y * HLOC + h) * WIDE, WIDE)]

    def out_copy(o, h):
        to = partner(o)
        return remote(obuf.at[h, to[1]], out_place(y, h), out_send.at[h], out_recv.at[h], to)

    def out_local(h):
        return pltpu.make_async_copy(obuf.at[h, y], out_place(y, h), local_sem.at[GROUPS + HLOC + h])

    def three(ref, send, recv):
        return remote(ref, ref, send, recv, sibling)

    def kv_three(g):
        return three(kv[g].at[0, pl.ds(0, 3 * TOK)], own_send.at[g], own_recv.at[g])

    def q_three(h):
        return three(qbuf.at[h, pl.ds(0, 3)], q_send.at[h], q_recv.at[h])

    def out_three(h):
        return three(obuf.at[h, pl.ds(0, 3)], out_send.at[h], out_recv.at[h])

    def send_q(h):
        for o in (2, 1, 3):
            q_copy(o, h).start()
        q_local(h).start()

    def piece(m, slot):
        return kv[m // PARTS].at[slot, pl.ds((m % PARTS) * ROWS, ROWS)]

    def forward(m, to, r, into):
        remote(piece(m, 2 * r), piece(m, 2 * into),
               win_send.at[m // PARTS], win_recv.at[m, into - 1], to).start()

    def arrived(m, r):
        remote(piece(m, 2 * r), piece(m, 2 * r), win_send.at[m // PARTS], win_recv.at[m, r - 1], up).wait_recv()

    def share(m, r):
        g = m // PARTS

        def go():
            remote(piece(m, 2 * r), piece(m, 2 * r + 1 - 2 * core), sib_send.at[g], sib_recv.at[g], sibling).start()

        if r == 0:
            pl.when(core == 0)(go)
        elif r == 6:
            pl.when(core == 1)(go)
        else:
            go()

    def when(cond, *args):
        pl.when(cond)(lambda: forward(*args))

    def lag0(m):
        if m % PARTS == 0:
            kv_three(m // PARTS).wait_recv()
            kv_local(m // PARTS).wait()
        forward(m, up, 0, 4)
        when(x < 3, m, right, 0, 1)
        when(x == 0, m, left, 0, 3)
        share(m, 0)

    def lag1(m):
        arrived(m, 4)
        when(x > 0, m, left, 4, 3)
        when(x == 3, m, right, 4, 1)
        when(x < 2, m, right, 4, 5)
        share(m, 4)

        @pl.when(x == 3)
        def _():
            arrived(m, 3)
            forward(m, left, 3, 2)
            share(m, 3)

        @pl.when(x > 0)
        def _():
            arrived(m, 1)
            when(x == 2, m, right, 1, 2)
            when(x == 3, m, up, 1, 5)
            share(m, 1)

    def lag2(m):
        @pl.when(x == 0)
        def _():
            arrived(m, 1)
            share(m, 1)

        @pl.when(x < 3)
        def _():
            arrived(m, 3)
            when(x == 0, m, left, 3, 6)
            when(x == 2, m, left, 3, 2)
            share(m, 3)

        @pl.when(x == 3)
        def _():
            arrived(m, 5)
            forward(m, right, 5, 2)
            share(m, 5)
            arrived(m, 2)
            share(m, 2)

        @pl.when(x == 2)
        def _():
            arrived(m, 2)
            forward(m, up, 2, 6)
            share(m, 2)

        @pl.when((x == 1) | (x == 2))
        def _():
            arrived(m, 5)
            share(m, 5)

    def lag3(m):
        @pl.when(x < 2)
        def _():
            arrived(m, 2)
            forward(m, up, 2, 6)
            share(m, 2)

        @pl.when(x >= 2)
        def _():
            arrived(m, 6)
            share(m, 6)

    def lag4(m):
        @pl.when(x < 2)
        def _():
            arrived(m, 6)
            when(x == 1, m, left, 6, 5)
            share(m, 6)

    def lag5(m):
        @pl.when(x == 0)
        def _():
            arrived(m, 5)
            share(m, 5)

    lags = [lag0, lag1, lag2, lag3, lag4, lag5]

    def step(n):
        for lag, event in enumerate(lags):
            if 0 <= n - lag < PIECES:
                event(n - lag)

    for g in range(GROUPS):
        for o in (2, 1, 3):
            kv_copy(o, g).start()
        kv_local(g).start()

    done = PARTS - 1 + len(lags) - 1
    for n in range(done + 1):
        step(n)
        if n == 1:
            send_q(0)
        if n == 4:
            send_q(1)

    token = lax.rem(lax.broadcasted_iota(jnp.int32, (GRP * TOK, BLK), 0), TOK)
    key_at = lax.broadcasted_iota(jnp.int32, (GRP * TOK, BLK), 1)

    def whole(g):
        ref = kv[g].at[pl.ds(0, 6)]
        return remote(ref, ref, sib_send.at[g], sib_recv.at[g], sibling)

    def picks(h):
        valid, slot = [None], [0]
        for t in range(TOPK):
            pick = chosen[0, h, t]
            valid.append(pick >= 0)
            slot.append(jnp.where(pick >= 0, jnp.clip(seq - pick, 0, SLOTS - 1), 0))
        return valid, slot

    def weigh(h, c):
        wide = qbuf[h, c]
        q = jnp.concatenate([wide[:, g * DH:(g + 1) * DH] for g in range(GRP)], axis=0)
        valid, slot = picks(h)
        top = None
        for t in range(TOPK + 1):
            s = lax.dot_general(q, kv[2 * h][slot[t]], (((1,), (1,)), ((), ())),
                                preferred_element_type=jnp.float32)
            if t == 0:
                s = jnp.where(token + c * TOK >= key_at, s, NEG)
            scores[t] = s
            high = jnp.max(s, axis=1, keepdims=True)
            top = high if t == 0 else jnp.maximum(top, jnp.where(valid[t], high, NEG))
        total = None
        for t in range(TOPK + 1):
            shift = top if t == 0 else jnp.where(valid[t], top, -NEG)
            p = jnp.exp2((scores[t] - shift) * RATE)
            add = jnp.sum(p, axis=1, keepdims=True)
            weights[c, t] = p.astype(jnp.bfloat16)
            total = add if t == 0 else total + add
        totals[c] = jnp.broadcast_to(total, (GRP * TOK, DH))

    def attend(h, c, o):
        _, slot = picks(h)
        acc = None
        for t in range(TOPK + 1):
            part = lax.dot_general(weights[c, t], kv[2 * h + 1][slot[t]], (((1,), (0,)), ((), ())),
                                   preferred_element_type=jnp.float32)
            acc = part if t == 0 else acc + part
        res = (acc / totals[c]).astype(jnp.bfloat16)
        for g in range(GRP):
            obuf[h, c, :, g * DH:(g + 1) * DH] = res[g * TOK:(g + 1) * TOK]
        for k in (1, 2, 3):
            pl.when(o == k)(lambda: out_copy(k, h).start())
        pl.when(o == 0)(lambda: out_local(h).start())

    def phase(h, work, steps):
        def body(j, _):
            o = lax.rem(j + 1, NHEAD)
            work(h, lax.rem(y + o, NHEAD), o)
            for after, n in steps:
                pl.when(j == after)(lambda: step(n))
            return 0

        lax.fori_loop(0, NHEAD, body, 0)

    def weigh_phase(h, steps):
        whole(2 * h).wait_recv()
        q_three(h).wait_recv()
        q_local(h).wait()
        phase(h, lambda h, c, o: weigh(h, c), steps)

    def attend_phase(h, steps):
        whole(2 * h + 1).wait_recv()
        phase(h, attend, steps)

    weigh_phase(0, [(0, done + 1), (2, done + 2)])
    attend_phase(0, [(1, done + 3), (3, done + 4)])
    weigh_phase(1, [(0, done + 5), (2, done + 6)])
    attend_phase(1, [])

    for g in range(GROUPS):
        kv_three(g).wait_send()
        whole(g).wait_send()
        ref = kv[g].at[pl.ds(0, 6)]
        remote(ref, ref, win_send.at[g], sib_recv.at[g], up).wait_send()
    for h in range(HLOC):
        q_three(h).wait_send()
        out_three(h).wait()
        out_local(h).wait()


def on_device(query, keys, values, chosen):
    nseq = lax.axis_size("seq")
    dma = pltpu.SemaphoreType.DMA
    any_spec = pl.BlockSpec(memory_space=pl.ANY)

    def body(*refs):
        kernel(nseq, *refs)

    return pl.pallas_call(
        body,
        out_shape=jax.ShapeDtypeStruct(query.shape, jnp.bfloat16),
        in_specs=[pl.BlockSpec(memory_space=pltpu.SMEM), any_spec, any_spec, any_spec],
        out_specs=any_spec,
        scratch_shapes=[pltpu.VMEM((SLOTS, BLK, DH), jnp.bfloat16)] * GROUPS + [
            pltpu.VMEM((HLOC, NHEAD, TOK, WIDE), jnp.bfloat16),
            pltpu.VMEM((HLOC, NHEAD, TOK, WIDE), jnp.bfloat16),
            pltpu.VMEM((TOPK + 1, GRP * TOK, BLK), jnp.float32),
            pltpu.VMEM((NHEAD, TOPK + 1, GRP * TOK, BLK), jnp.bfloat16),
            pltpu.VMEM((NHEAD, GRP * TOK, DH), jnp.float32),
            dma((GROUPS,)), dma((GROUPS,)),
            dma((HLOC,)), dma((HLOC,)),
            dma((GROUPS,)), dma((PIECES, 6)),
            dma((GROUPS,)), dma((GROUPS,)),
            dma((HLOC,)), dma((HLOC,)),
            dma((GROUPS + 2 * HLOC,)),
        ],
        compiler_params=pltpu.CompilerParams(
            collective_id=0, has_side_effects=True, vmem_limit_bytes=56 * 1024 * 1024),
        cost_estimate=pl.CostEstimate(
            flops=4 * BLK * HLOC * GRP * BLK * 4 * DH, bytes_accessed=4 * 1024 * 1024,
            transcendentals=HLOC * GRP * BLK * BLK * 4),
        name="window_attention",
    )(chosen, query, keys, values)


def solution(mesh):
    in_specs = (
        P(("seq", "head"), None),
        P(("seq", "head"), None),
        P(("seq", "head"), None),
        P("seq", "head", None),
    )
    return jax.shard_map(
        on_device, mesh=mesh, in_specs=in_specs, out_specs=P(("seq", "head"), None), check_vma=False
    )
```

```python
import math

import jax
import jax.numpy as jnp
from jax import lax
from jax.experimental import pallas as pl
from jax.experimental.pallas import tpu as pltpu
from jax.sharding import PartitionSpec as P

HQ = 32
HK = 8
DH = 128
BLK = 512
TOPK = 3
GRP = HQ // HK
NHEAD = 4
HLOC = HK // NHEAD
TOK = BLK // NHEAD
NX = 4
SLOTS = 13
GROUPS = 2 * HLOC
PARTS = 2
PIECES = GROUPS * PARTS
ROWS = BLK // PARTS
WIDE = GRP * DH
TILE = 256
TILES = (TOPK + 1) * BLK // TILE
BAND = GRP * TOK // TILES
NEG = -1e30
RATE = math.log2(math.e) / math.sqrt(DH)
MESH = pl.DeviceIdType.MESH


def kernel(nseq, chosen, query, keys, values, out, kv0, kv1, kv2, kv3, qbuf, obuf, scores_a, scores_b, weights, totals,
           own_send, own_recv, q_send, q_recv, win_send, win_recv, sib_send, sib_recv,
           out_send, out_recv, local_sem):
    kv = (kv0, kv1, kv2, kv3)
    nz = nseq // (2 * NX)
    seq = lax.axis_index("seq")
    y = lax.axis_index("head")
    core = lax.rem(seq, 2)
    x = lax.rem(seq // 2, NX)
    z = seq // (2 * NX)

    def at(zz, xx):
        return ((zz * NX + xx) * 2 + core, y)

    up = at(lax.rem(z + 1, nz), x)
    down = at(lax.rem(z + nz - 1, nz), x)
    right = at(z, lax.rem(x + 1, NX))
    left = at(z, lax.rem(x + NX - 1, NX))
    sibling = (seq + 1 - 2 * core, y)

    def partner(o):
        return (seq, lax.rem(y + o, NHEAD))

    barrier = pltpu.get_barrier_semaphore()
    for who in [up, down, right, left, sibling, partner(1), partner(2), partner(3)]:
        pl.semaphore_signal(barrier, inc=1, device_id=who, device_id_type=MESH)
    pl.semaphore_wait(barrier, 8)

    def columns(start, width):
        return pl.ds(pl.multiple_of(start, DH), width)

    def remote(src, dst, send, recv, to):
        return pltpu.make_async_remote_copy(
            src_ref=src, dst_ref=dst, send_sem=send, recv_sem=recv, device_id=to, device_id_type=MESH)

    own_rows = pl.ds(pl.multiple_of(y * TOK, TOK), TOK)

    def kv_source(g, to_y):
        return (keys, values)[g % 2].at[:, columns((to_y * HLOC + g // 2) * DH, DH)]

    def kv_copy(o, g):
        to = partner(o)
        return remote(kv_source(g, to[1]), kv[g].at[0, own_rows], own_send.at[g], own_recv.at[g], to)

    def kv_local(g):
        return pltpu.make_async_copy(kv_source(g, y), kv[g].at[0, own_rows], local_sem.at[g])

    def q_source(h, to_y):
        return query.at[:, columns((to_y * HLOC + h) * WIDE, WIDE)]

    def q_copy(o, h):
        to = partner(o)
        return remote(q_source(h, to[1]), qbuf.at[h, y], q_send.at[h], q_recv.at[h], to)

    def q_local(h):
        return pltpu.make_async_copy(q_source(h, y), qbuf.at[h, y], local_sem.at[GROUPS + h])

    def out_place(to_y, h):
        return out.at[:, columns((to_y * HLOC + h) * WIDE, WIDE)]

    def out_copy(o, h):
        to = partner(o)
        return remote(obuf.at[h, to[1]], out_place(y, h), out_send.at[h], out_recv.at[h], to)

    def out_local(h):
        return pltpu.make_async_copy(obuf.at[h, y], out_place(y, h), local_sem.at[GROUPS + HLOC + h])

    def three(ref, send, recv):
        return remote(ref, ref, send, recv, sibling)

    def kv_three(g):
        return three(kv[g].at[0, pl.ds(0, 3 * TOK)], own_send.at[g], own_recv.at[g])

    def q_three(h):
        return three(qbuf.at[h, pl.ds(0, 3)], q_send.at[h], q_recv.at[h])

    def out_three(h):
        return three(obuf.at[h, pl.ds(0, 3)], out_send.at[h], out_recv.at[h])

    def send_q(h):
        for o in (2, 1, 3):
            q_copy(o, h).start()
        q_local(h).start()

    def piece(m, slot):
        return kv[m // PARTS].at[slot, pl.ds((m % PARTS) * ROWS, ROWS)]

    def forward(m, to, r, into):
        remote(piece(m, 2 * r), piece(m, 2 * into),
               win_send.at[m // PARTS], win_recv.at[m, into - 1], to).start()

    def arrived(m, r):
        remote(piece(m, 2 * r), piece(m, 2 * r), win_send.at[m // PARTS], win_recv.at[m, r - 1], up).wait_recv()

    def share(m, r):
        g = m // PARTS

        def go():
            remote(piece(m, 2 * r), piece(m, 2 * r + 1 - 2 * core), sib_send.at[g], sib_recv.at[g], sibling).start()

        if r == 0:
            pl.when(core == 0)(go)
        elif r == 6:
            pl.when(core == 1)(go)
        else:
            go()

    def when(cond, *args):
        pl.when(cond)(lambda: forward(*args))

    def lag0(m):
        if m % PARTS == 0:
            kv_three(m // PARTS).wait_recv()
            kv_local(m // PARTS).wait()
        forward(m, up, 0, 4)
        when(x < 3, m, right, 0, 1)
        when(x == 0, m, left, 0, 3)
        share(m, 0)

    def lag1(m):
        arrived(m, 4)
        when(x > 0, m, left, 4, 3)
        when(x == 3, m, right, 4, 1)
        when(x < 2, m, right, 4, 5)
        share(m, 4)

        @pl.when(x == 3)
        def _():
            arrived(m, 3)
            forward(m, left, 3, 2)
            share(m, 3)

        @pl.when(x > 0)
        def _():
            arrived(m, 1)
            when(x == 2, m, right, 1, 2)
            when(x == 3, m, up, 1, 5)
            share(m, 1)

    def lag2(m):
        @pl.when(x == 0)
        def _():
            arrived(m, 1)
            share(m, 1)

        @pl.when(x < 3)
        def _():
            arrived(m, 3)
            when(x == 0, m, left, 3, 6)
            when(x == 2, m, left, 3, 2)
            share(m, 3)

        @pl.when(x == 3)
        def _():
            arrived(m, 5)
            forward(m, right, 5, 2)
            share(m, 5)
            arrived(m, 2)
            share(m, 2)

        @pl.when(x == 2)
        def _():
            arrived(m, 2)
            forward(m, up, 2, 6)
            share(m, 2)

        @pl.when((x == 1) | (x == 2))
        def _():
            arrived(m, 5)
            share(m, 5)

    def lag3(m):
        @pl.when(x < 2)
        def _():
            arrived(m, 2)
            forward(m, up, 2, 6)
            share(m, 2)

        @pl.when(x >= 2)
        def _():
            arrived(m, 6)
            share(m, 6)

    def lag4(m):
        @pl.when(x < 2)
        def _():
            arrived(m, 6)
            when(x == 1, m, left, 6, 5)
            share(m, 6)

    def lag5(m):
        @pl.when(x == 0)
        def _():
            arrived(m, 5)
            share(m, 5)

    lags = [lag0, lag1, lag2, lag3, lag4, lag5]

    def step(n):
        for lag, event in enumerate(lags):
            if 0 <= n - lag < PIECES:
                event(n - lag)

    for g in range(GROUPS):
        for o in (2, 1, 3):
            kv_copy(o, g).start()
        kv_local(g).start()

    done = PARTS - 1 + len(lags) - 1
    for n in range(done + 1):
        step(n)
        if n == 1:
            send_q(0)
        if n == 4:
            send_q(1)

    def whole(g):
        ref = kv[g].at[pl.ds(0, 6)]
        return remote(ref, ref, sib_send.at[g], sib_recv.at[g], sibling)

    def offset(j):
        return (j + 1) % NHEAD

    def chunk(j):
        return lax.rem(y + offset(j), NHEAD)

    def pick(h, t):
        named = chosen[0, h, t]
        return named >= 0, jnp.where(named >= 0, jnp.clip(seq - named, 0, SLOTS - 1), 0)

    ahead = (lax.broadcasted_iota(jnp.int32, (BAND, TILE), 0)
             - lax.broadcasted_iota(jnp.int32, (BAND, TILE), 1))

    def multiply(h, j, i, into):
        wide = qbuf[h, chunk(j)]
        q = jnp.concatenate([wide[:, g * DH:(g + 1) * DH] for g in range(GRP)], axis=0)
        t = i // 2
        slot = jnp.where(t == 0, 0, pick(h, jnp.maximum(t - 1, 0))[1])
        k = kv[2 * h][slot, pl.ds(pl.multiple_of(lax.rem(i, 2) * TILE, TILE), TILE)]
        into[i] = lax.dot_general(q, k, (((1,), (1,)), ((), ())), preferred_element_type=jnp.float32)

    def normalize(h, j, i, source):
        c = chunk(j)
        rows = pl.ds(pl.multiple_of(i * BAND, BAND), BAND)
        first = c * TOK + lax.rem(i * BAND, TOK)

        def tile(u):
            s = source[u, rows]
            if u * TILE < BLK:
                s = jnp.where(ahead >= u * TILE - first, s, NEG)
            return s

        valid = [None] + [pick(h, t)[0] for t in range(TOPK)]
        top = None
        for t in range(TOPK + 1):
            high = None
            for u in (2 * t, 2 * t + 1):
                s = tile(u)
                s = jnp.maximum(s[:, :DH], s[:, DH:])
                high = s if high is None else jnp.maximum(high, s)
            top = high if t == 0 else jnp.maximum(top, jnp.where(valid[t], high, NEG))
        top = jnp.max(top, axis=1, keepdims=True)
        total = None
        for t in range(TOPK + 1):
            shift = top if t == 0 else jnp.where(valid[t], top, -NEG)
            for u in (2 * t, 2 * t + 1):
                p = jnp.exp2((tile(u) - shift) * RATE)
                weights[c, rows, u * TILE:(u + 1) * TILE] = p.astype(jnp.bfloat16)
                p = p[:, :DH] + p[:, DH:]
                total = p if total is None else total + p
        totals[c, rows] = jnp.broadcast_to(jnp.sum(total, axis=1, keepdims=True), (BAND, DH))

    def attend(h, j):
        c = chunk(j)
        acc = None
        for t in range(TOPK + 1):
            slot = 0 if t == 0 else pick(h, t - 1)[1]
            part = lax.dot_general(weights[c, :, t * BLK:(t + 1) * BLK], kv[2 * h + 1][slot],
                                   (((1,), (0,)), ((), ())), preferred_element_type=jnp.float32)
            acc = part if t == 0 else acc + part
        res = (acc / totals[c]).astype(jnp.bfloat16)
        for g in range(GRP):
            obuf[h, c, :, g * DH:(g + 1) * DH] = res[g * TOK:(g + 1) * TOK]
        if offset(j) == 0:
            out_local(h).start()
        else:
            out_copy(offset(j), h).start()

    sides = (scores_a, scores_b)

    def weigh_phase(h, steps):
        whole(2 * h).wait_recv()
        q_three(h).wait_recv()
        q_local(h).wait()
        for j in range(NHEAD + 1):
            def body(i, _):
                if j > 0:
                    normalize(h, j - 1, i, sides[(j - 1) % 2])
                if j < NHEAD:
                    multiply(h, j, i, sides[j % 2])
                return 0

            lax.fori_loop(0, TILES, body, 0)
            if j in steps:
                step(steps[j])

    def attend_phase(h, steps):
        whole(2 * h + 1).wait_recv()
        for j in range(NHEAD):
            attend(h, j)
            if j in steps:
                step(steps[j])

    weigh_phase(0, {0: done + 1, 2: done + 2})
    attend_phase(0, {1: done + 3, 3: done + 4})
    weigh_phase(1, {0: done + 5, 2: done + 6})
    attend_phase(1, {})

    for g in range(GROUPS):
        kv_three(g).wait_send()
        whole(g).wait_send()
        ref = kv[g].at[pl.ds(0, 6)]
        remote(ref, ref, win_send.at[g], sib_recv.at[g], up).wait_send()
    for h in range(HLOC):
        q_three(h).wait_send()
        out_three(h).wait()
        out_local(h).wait()


def on_device(query, keys, values, chosen):
    nseq = lax.axis_size("seq")
    dma = pltpu.SemaphoreType.DMA
    any_spec = pl.BlockSpec(memory_space=pl.ANY)

    def body(*refs):
        kernel(nseq, *refs)

    return pl.pallas_call(
        body,
        out_shape=pltpu.VMEM(query.shape, jnp.bfloat16),
        in_specs=[pl.BlockSpec(memory_space=pltpu.SMEM), any_spec, any_spec, any_spec],
        out_specs=pl.BlockSpec(memory_space=pltpu.VMEM),
        scratch_shapes=[pltpu.VMEM((SLOTS, BLK, DH), jnp.bfloat16)] * GROUPS + [
            pltpu.VMEM((HLOC, NHEAD, TOK, WIDE), jnp.bfloat16),
            pltpu.VMEM((HLOC, NHEAD, TOK, WIDE), jnp.bfloat16),
            pltpu.VMEM((TILES, GRP * TOK, TILE), jnp.float32),
            pltpu.VMEM((TILES, GRP * TOK, TILE), jnp.float32),
            pltpu.VMEM((NHEAD, GRP * TOK, (TOPK + 1) * BLK), jnp.bfloat16),
            pltpu.VMEM((NHEAD, GRP * TOK, DH), jnp.float32),
            dma((GROUPS,)), dma((GROUPS,)),
            dma((HLOC,)), dma((HLOC,)),
            dma((GROUPS,)), dma((PIECES, 6)),
            dma((GROUPS,)), dma((GROUPS,)),
            dma((HLOC,)), dma((HLOC,)),
            dma((GROUPS + 2 * HLOC,)),
        ],
        compiler_params=pltpu.CompilerParams(
            collective_id=0, has_side_effects=True, vmem_limit_bytes=56 * 1024 * 1024),
        cost_estimate=pl.CostEstimate(
            flops=4 * BLK * HLOC * GRP * BLK * 4 * DH, bytes_accessed=4 * 1024 * 1024,
            transcendentals=HLOC * GRP * BLK * BLK * 4),
        name="window_attention",
    )(chosen, query, keys, values)


def solution(mesh):
    in_specs = (
        P(("seq", "head"), None),
        P(("seq", "head"), None),
        P(("seq", "head"), None),
        P("seq", "head", None),
    )
    return jax.shard_map(
        on_device, mesh=mesh, in_specs=in_specs, out_specs=P(("seq", "head"), None), check_vma=False
    )
```

```python
import math

import jax
import jax.numpy as jnp
from jax import lax
from jax.experimental import pallas as pl
from jax.experimental.pallas import tpu as pltpu
from jax.sharding import PartitionSpec as P

HQ = 32
HK = 8
DH = 128
BLK = 512
TOPK = 3
GRP = HQ // HK
NHEAD = 4
HLOC = HK // NHEAD
TOK = BLK // NHEAD
NX = 4
SLOTS = 13
GROUPS = 2 * HLOC
PARTS = 2
PIECES = GROUPS * PARTS
ROWS = BLK // PARTS
WIDE = GRP * DH
NEG = -1e30
RATE = math.log2(math.e) / math.sqrt(DH)
MESH = pl.DeviceIdType.MESH


def kernel(nseq, chosen, query, keys, values, out, kv0, kv1, kv2, kv3, qbuf, obuf, scores, weights, totals, flipped,
           own_send, own_recv, q_send, q_recv, win_send, win_recv, sib_send, sib_recv,
           out_send, out_recv, local_sem):
    kv = (kv0, kv1, kv2, kv3)
    nz = nseq // (2 * NX)
    seq = lax.axis_index("seq")
    y = lax.axis_index("head")
    core = lax.rem(seq, 2)
    x = lax.rem(seq // 2, NX)
    z = seq // (2 * NX)

    def at(zz, xx):
        return ((zz * NX + xx) * 2 + core, y)

    up = at(lax.rem(z + 1, nz), x)
    down = at(lax.rem(z + nz - 1, nz), x)
    right = at(z, lax.rem(x + 1, NX))
    left = at(z, lax.rem(x + NX - 1, NX))
    sibling = (seq + 1 - 2 * core, y)

    def partner(o):
        return (seq, lax.rem(y + o, NHEAD))

    barrier = pltpu.get_barrier_semaphore()
    for who in [up, down, right, left, sibling, partner(1), partner(2), partner(3)]:
        pl.semaphore_signal(barrier, inc=1, device_id=who, device_id_type=MESH)
    pl.semaphore_wait(barrier, 8)

    def columns(start, width):
        return pl.ds(pl.multiple_of(start, DH), width)

    def remote(src, dst, send, recv, to):
        return pltpu.make_async_remote_copy(
            src_ref=src, dst_ref=dst, send_sem=send, recv_sem=recv, device_id=to, device_id_type=MESH)

    own_rows = pl.ds(pl.multiple_of(y * TOK, TOK), TOK)

    def kv_source(g, to_y):
        return (keys, values)[g % 2].at[:, columns((to_y * HLOC + g // 2) * DH, DH)]

    def kv_copy(o, g):
        to = partner(o)
        return remote(kv_source(g, to[1]), kv[g].at[0, own_rows], own_send.at[g], own_recv.at[g], to)

    def kv_local(g):
        return pltpu.make_async_copy(kv_source(g, y), kv[g].at[0, own_rows], local_sem.at[g])

    def q_source(h, to_y):
        return query.at[:, columns((to_y * HLOC + h) * WIDE, WIDE)]

    def q_copy(o, h):
        to = partner(o)
        return remote(q_source(h, to[1]), qbuf.at[h, y], q_send.at[h], q_recv.at[h], to)

    def q_local(h):
        return pltpu.make_async_copy(q_source(h, y), qbuf.at[h, y], local_sem.at[GROUPS + h])

    def out_place(to_y, h):
        return out.at[:, columns((to_y * HLOC + h) * WIDE, WIDE)]

    def out_copy(o, h):
        to = partner(o)
        return remote(obuf.at[h, to[1]], out_place(y, h), out_send.at[h], out_recv.at[h], to)

    def out_local(h):
        return pltpu.make_async_copy(obuf.at[h, y], out_place(y, h), local_sem.at[GROUPS + HLOC + h])

    def three(ref, send, recv):
        return remote(ref, ref, send, recv, sibling)

    def kv_three(g):
        return three(kv[g].at[0, pl.ds(0, 3 * TOK)], own_send.at[g], own_recv.at[g])

    def q_three(h):
        return three(qbuf.at[h, pl.ds(0, 3)], q_send.at[h], q_recv.at[h])

    def out_three(h):
        return three(obuf.at[h, pl.ds(0, 3)], out_send.at[h], out_recv.at[h])

    def send_q(h):
        for o in (2, 1, 3):
            q_copy(o, h).start()
        q_local(h).start()

    def piece(m, slot):
        return kv[m // PARTS].at[slot, pl.ds((m % PARTS) * ROWS, ROWS)]

    def forward(m, to, r, into):
        remote(piece(m, 2 * r), piece(m, 2 * into),
               win_send.at[m // PARTS], win_recv.at[m, into - 1], to).start()

    def arrived(m, r):
        remote(piece(m, 2 * r), piece(m, 2 * r), win_send.at[m // PARTS], win_recv.at[m, r - 1], up).wait_recv()

    def share(m, r):
        g = m // PARTS

        def go():
            remote(kv[g].at[2 * r], kv[g].at[2 * r + 1 - 2 * core], sib_send.at[g], sib_recv.at[g], sibling).start()

        if m % PARTS < PARTS - 1:
            return
        if r == 0:
            pl.when(core == 0)(go)
        elif r == 6:
            pl.when(core == 1)(go)
        else:
            go()

    def when(cond, *args):
        pl.when(cond)(lambda: forward(*args))

    def lag0(m):
        if m % PARTS == 0:
            kv_three(m // PARTS).wait_recv()
            kv_local(m // PARTS).wait()
        forward(m, up, 0, 4)
        when(x < 3, m, right, 0, 1)
        when(x == 0, m, left, 0, 3)
        share(m, 0)

    def lag1(m):
        arrived(m, 4)
        when(x > 0, m, left, 4, 3)
        when(x == 3, m, right, 4, 1)
        when(x < 2, m, right, 4, 5)
        share(m, 4)

        @pl.when(x == 3)
        def _():
            arrived(m, 3)
            forward(m, left, 3, 2)
            share(m, 3)

        @pl.when(x > 0)
        def _():
            arrived(m, 1)
            when(x == 2, m, right, 1, 2)
            when(x == 3, m, up, 1, 5)
            share(m, 1)

    def lag2(m):
        @pl.when(x == 0)
        def _():
            arrived(m, 1)
            share(m, 1)

        @pl.when(x < 3)
        def _():
            arrived(m, 3)
            when(x == 0, m, left, 3, 6)
            when(x == 2, m, left, 3, 2)
            share(m, 3)

        @pl.when(x == 3)
        def _():
            arrived(m, 5)
            forward(m, right, 5, 2)
            share(m, 5)
            arrived(m, 2)
            share(m, 2)

        @pl.when(x == 2)
        def _():
            arrived(m, 2)
            forward(m, up, 2, 6)
            share(m, 2)

        @pl.when((x == 1) | (x == 2))
        def _():
            arrived(m, 5)
            share(m, 5)

    def lag3(m):
        @pl.when(x < 2)
        def _():
            arrived(m, 2)
            forward(m, up, 2, 6)
            share(m, 2)

        @pl.when(x >= 2)
        def _():
            arrived(m, 6)
            share(m, 6)

    def lag4(m):
        @pl.when(x < 2)
        def _():
            arrived(m, 6)
            when(x == 1, m, left, 6, 5)
            share(m, 6)

    def lag5(m):
        @pl.when(x == 0)
        def _():
            arrived(m, 5)
            share(m, 5)

    lags = [lag0, lag1, lag2, lag3, lag4, lag5]

    def step(n):
        for lag, event in enumerate(lags):
            if 0 <= n - lag < PIECES:
                event(n - lag)

    for g in range(GROUPS):
        for o in (2, 1, 3):
            kv_copy(o, g).start()
        kv_local(g).start()

    done = PARTS - 1 + len(lags) - 1
    for n in range(done + 1):
        step(n)
        if n == 1:
            send_q(0)
        if n == 4:
            send_q(1)

    key_at = lax.broadcasted_iota(jnp.int32, (BLK, GRP * TOK), 0)
    token = lax.rem(lax.broadcasted_iota(jnp.int32, (BLK, GRP * TOK), 1), TOK)

    def whole(g):
        ref = kv[g].at[pl.ds(0, 6)]
        return remote(ref, ref, sib_send.at[g], sib_recv.at[g], sibling)

    def picks(h):
        valid, slot = [None], [0]
        for t in range(TOPK):
            pick = chosen[0, h, t]
            valid.append(pick >= 0)
            slot.append(jnp.where(pick >= 0, jnp.clip(seq - pick, 0, SLOTS - 1), 0))
        return valid, slot

    def weigh(h, c):
        wide = qbuf[h, c]
        q = jnp.concatenate([wide[:, g * DH:(g + 1) * DH] for g in range(GRP)], axis=0)
        valid, slot = picks(h)
        top = None
        for t in range(TOPK + 1):
            s = lax.dot_general(kv[2 * h][slot[t]], q, (((1,), (1,)), ((), ())),
                                preferred_element_type=jnp.float32)
            if t == 0:
                s = jnp.where(token + c * TOK >= key_at, s, NEG)
            scores[t] = s
            high = jnp.max(s, axis=0, keepdims=True)
            top = high if t == 0 else jnp.maximum(top, jnp.where(valid[t], high, NEG))
        total = None
        for t in range(TOPK + 1):
            shift = top if t == 0 else jnp.where(valid[t], top, -NEG)
            p = jnp.exp2((scores[t] - shift) * RATE)
            add = jnp.sum(p, axis=0, keepdims=True)
            weights[c, t] = p.astype(jnp.bfloat16)
            total = add if t == 0 else total + add
        totals[c] = jnp.broadcast_to(total, (8, GRP * TOK))

    def flip(h):
        _, slot = picks(h)
        for t in range(TOPK + 1):
            flipped[t] = kv[2 * h + 1][slot[t]].T

    def attend(h, c, o):
        acc = None
        for t in range(TOPK + 1):
            part = lax.dot_general(flipped[t], weights[c, t], (((1,), (0,)), ((), ())),
                                   preferred_element_type=jnp.float32)
            acc = part if t == 0 else acc + part
        res = acc / totals[c, 0:1]
        for g in range(GRP):
            obuf[h, c, :, g * DH:(g + 1) * DH] = res[:, g * TOK:(g + 1) * TOK].T.astype(jnp.bfloat16)
        for k in (1, 2, 3):
            pl.when(o == k)(lambda: out_copy(k, h).start())
        pl.when(o == 0)(lambda: out_local(h).start())

    def phase(h, work, steps):
        def body(j, _):
            o = lax.rem(j + 1, NHEAD)
            work(h, lax.rem(y + o, NHEAD), o)
            for after, n in steps:
                pl.when(j == after)(lambda: step(n))
            return 0

        lax.fori_loop(0, NHEAD, body, 0)

    def weigh_phase(h, steps):
        whole(2 * h).wait_recv()
        q_three(h).wait_recv()
        q_local(h).wait()
        phase(h, lambda h, c, o: weigh(h, c), steps)

    def attend_phase(h, steps):
        whole(2 * h + 1).wait_recv()
        flip(h)
        phase(h, attend, steps)

    weigh_phase(0, [(0, done + 1), (2, done + 2)])
    attend_phase(0, [(1, done + 3), (3, done + 4)])
    weigh_phase(1, [(0, done + 5), (2, done + 6)])
    attend_phase(1, [])

    for g in range(GROUPS):
        kv_three(g).wait_send()
        whole(g).wait_send()
        ref = kv[g].at[pl.ds(0, 6)]
        remote(ref, ref, win_send.at[g], sib_recv.at[g], up).wait_send()
    for h in range(HLOC):
        q_three(h).wait_send()
        out_three(h).wait()
        out_local(h).wait()


def on_device(query, keys, values, chosen):
    nseq = lax.axis_size("seq")
    dma = pltpu.SemaphoreType.DMA
    any_spec = pl.BlockSpec(memory_space=pl.ANY)

    def body(*refs):
        kernel(nseq, *refs)

    return pl.pallas_call(
        body,
        out_shape=pltpu.VMEM(query.shape, jnp.bfloat16),
        in_specs=[pl.BlockSpec(memory_space=pltpu.SMEM), any_spec, any_spec, any_spec],
        out_specs=pl.BlockSpec(memory_space=pltpu.VMEM),
        scratch_shapes=[pltpu.VMEM((SLOTS, BLK, DH), jnp.bfloat16)] * GROUPS + [
            pltpu.VMEM((HLOC, NHEAD, TOK, WIDE), jnp.bfloat16),
            pltpu.VMEM((HLOC, NHEAD, TOK, WIDE), jnp.bfloat16),
            pltpu.VMEM((TOPK + 1, GRP * TOK, BLK), jnp.float32),
            pltpu.VMEM((NHEAD, TOPK + 1, GRP * TOK, BLK), jnp.bfloat16),
            pltpu.VMEM((NHEAD, 8, GRP * TOK), jnp.float32),
            pltpu.VMEM((TOPK + 1, DH, BLK), jnp.bfloat16),
            dma((GROUPS,)), dma((GROUPS,)),
            dma((HLOC,)), dma((HLOC,)),
            dma((GROUPS,)), dma((PIECES, 6)),
            dma((GROUPS,)), dma((GROUPS,)),
            dma((HLOC,)), dma((HLOC,)),
            dma((GROUPS + 2 * HLOC,)),
        ],
        compiler_params=pltpu.CompilerParams(
            collective_id=0, has_side_effects=True, vmem_limit_bytes=56 * 1024 * 1024),
        cost_estimate=pl.CostEstimate(
            flops=4 * BLK * HLOC * GRP * BLK * 4 * DH, bytes_accessed=4 * 1024 * 1024,
            transcendentals=HLOC * GRP * BLK * BLK * 4),
        name="window_attention",
    )(chosen, query, keys, values)


def solution(mesh):
    in_specs = (
        P(("seq", "head"), None),
        P(("seq", "head"), None),
        P(("seq", "head"), None),
        P("seq", "head", None),
    )
    return jax.shard_map(
        on_device, mesh=mesh, in_specs=in_specs, out_specs=P(("seq", "head"), None), check_vma=False
    )
```

```python
import math

import jax
import jax.numpy as jnp
from jax import lax
from jax.experimental import pallas as pl
from jax.experimental.pallas import tpu as pltpu
from jax.sharding import PartitionSpec as P

HQ = 32
HK = 8
DH = 128
BLK = 512
TOPK = 3
GRP = HQ // HK
NHEAD = 4
HLOC = HK // NHEAD
TOK = BLK // NHEAD
NX = 4
SLOTS = 13
GROUPS = 2 * HLOC
PARTS = 2
PIECES = GROUPS * PARTS
ROWS = BLK // PARTS
WIDE = GRP * DH
BAND = 256
BANDS = (TOPK + 1) * BLK // BAND
NEG = -1e30
RATE = math.log2(math.e) / math.sqrt(DH)
MESH = pl.DeviceIdType.MESH


def kernel(nseq, chosen, query, keys, values, out, kv0, kv1, kv2, kv3, qbuf, obuf, scores_a, scores_b, weights_a, weights_b, totals, flipped,
           own_send, own_recv, q_send, q_recv, win_send, win_recv, sib_send, sib_recv,
           out_send, out_recv, local_sem):
    kv = (kv0, kv1, kv2, kv3)
    nz = nseq // (2 * NX)
    seq = lax.axis_index("seq")
    y = lax.axis_index("head")
    core = lax.rem(seq, 2)
    x = lax.rem(seq // 2, NX)
    z = seq // (2 * NX)

    def at(zz, xx):
        return ((zz * NX + xx) * 2 + core, y)

    up = at(lax.rem(z + 1, nz), x)
    down = at(lax.rem(z + nz - 1, nz), x)
    right = at(z, lax.rem(x + 1, NX))
    left = at(z, lax.rem(x + NX - 1, NX))
    sibling = (seq + 1 - 2 * core, y)

    def partner(o):
        return (seq, lax.rem(y + o, NHEAD))

    barrier = pltpu.get_barrier_semaphore()
    for who in [up, down, right, left, sibling, partner(1), partner(2), partner(3)]:
        pl.semaphore_signal(barrier, inc=1, device_id=who, device_id_type=MESH)
    pl.semaphore_wait(barrier, 8)

    def columns(start, width):
        return pl.ds(pl.multiple_of(start, DH), width)

    def remote(src, dst, send, recv, to):
        return pltpu.make_async_remote_copy(
            src_ref=src, dst_ref=dst, send_sem=send, recv_sem=recv, device_id=to, device_id_type=MESH)

    own_rows = pl.ds(pl.multiple_of(y * TOK, TOK), TOK)

    def kv_source(g, to_y):
        return (keys, values)[g % 2].at[:, columns((to_y * HLOC + g // 2) * DH, DH)]

    def kv_copy(o, g):
        to = partner(o)
        return remote(kv_source(g, to[1]), kv[g].at[0, own_rows], own_send.at[g], own_recv.at[g], to)

    def kv_local(g):
        return pltpu.make_async_copy(kv_source(g, y), kv[g].at[0, own_rows], local_sem.at[g])

    def q_source(h, to_y):
        return query.at[:, columns((to_y * HLOC + h) * WIDE, WIDE)]

    def q_copy(o, h):
        to = partner(o)
        return remote(q_source(h, to[1]), qbuf.at[h, y], q_send.at[h], q_recv.at[h], to)

    def q_local(h):
        return pltpu.make_async_copy(q_source(h, y), qbuf.at[h, y], local_sem.at[GROUPS + h])

    def out_place(to_y, h):
        return out.at[:, columns((to_y * HLOC + h) * WIDE, WIDE)]

    def out_copy(o, h):
        to = partner(o)
        return remote(obuf.at[h, to[1]], out_place(y, h), out_send.at[h], out_recv.at[h], to)

    def out_local(h):
        return pltpu.make_async_copy(obuf.at[h, y], out_place(y, h), local_sem.at[GROUPS + HLOC + h])

    def three(ref, send, recv):
        return remote(ref, ref, send, recv, sibling)

    def kv_three(g):
        return three(kv[g].at[0, pl.ds(0, 3 * TOK)], own_send.at[g], own_recv.at[g])

    def q_three(h):
        return three(qbuf.at[h, pl.ds(0, 3)], q_send.at[h], q_recv.at[h])

    def out_three(h):
        return three(obuf.at[h, pl.ds(0, 3)], out_send.at[h], out_recv.at[h])

    def send_q(h):
        for o in (2, 1, 3):
            q_copy(o, h).start()
        q_local(h).start()

    def piece(m, slot):
        return kv[m // PARTS].at[slot, pl.ds((m % PARTS) * ROWS, ROWS)]

    def forward(m, to, r, into):
        remote(piece(m, 2 * r), piece(m, 2 * into),
               win_send.at[m // PARTS], win_recv.at[m, into - 1], to).start()

    def arrived(m, r):
        remote(piece(m, 2 * r), piece(m, 2 * r), win_send.at[m // PARTS], win_recv.at[m, r - 1], up).wait_recv()

    def share(m, r):
        g = m // PARTS

        def go():
            remote(kv[g].at[2 * r], kv[g].at[2 * r + 1 - 2 * core], sib_send.at[g], sib_recv.at[g], sibling).start()

        if m % PARTS < PARTS - 1:
            return
        if r == 0:
            pl.when(core == 0)(go)
        elif r == 6:
            pl.when(core == 1)(go)
        else:
            go()

    def when(cond, *args):
        pl.when(cond)(lambda: forward(*args))

    def lag0(m):
        if m % PARTS == 0:
            kv_three(m // PARTS).wait_recv()
            kv_local(m // PARTS).wait()
        forward(m, up, 0, 4)
        when(x < 3, m, right, 0, 1)
        when(x == 0, m, left, 0, 3)
        share(m, 0)

    def lag1(m):
        arrived(m, 4)
        when(x > 0, m, left, 4, 3)
        when(x == 3, m, right, 4, 1)
        when(x < 2, m, right, 4, 5)
        share(m, 4)

        @pl.when(x == 3)
        def _():
            arrived(m, 3)
            forward(m, left, 3, 2)
            share(m, 3)

        @pl.when(x > 0)
        def _():
            arrived(m, 1)
            when(x == 2, m, right, 1, 2)
            when(x == 3, m, up, 1, 5)
            share(m, 1)

    def lag2(m):
        @pl.when(x == 0)
        def _():
            arrived(m, 1)
            if m // PARTS == GROUPS - 1:
                forward(m, up, 1, 5)
            share(m, 1)

        @pl.when(x < 3)
        def _():
            arrived(m, 3)
            when(x == 0, m, left, 3, 6)
            when(x == 2, m, left, 3, 2)
            share(m, 3)

        @pl.when(x == 3)
        def _():
            arrived(m, 5)
            forward(m, right, 5, 2)
            share(m, 5)
            arrived(m, 2)
            share(m, 2)

        @pl.when(x == 2)
        def _():
            arrived(m, 2)
            forward(m, up, 2, 6)
            share(m, 2)

        @pl.when((x == 1) | (x == 2))
        def _():
            arrived(m, 5)
            share(m, 5)

    def lag3(m):
        @pl.when(x < 2)
        def _():
            arrived(m, 2)
            forward(m, up, 2, 6)
            share(m, 2)

        @pl.when(x >= 2)
        def _():
            arrived(m, 6)
            share(m, 6)

        if m // PARTS == GROUPS - 1:
            @pl.when(x == 0)
            def _():
                arrived(m, 5)
                share(m, 5)

    def lag4(m):
        @pl.when(x < 2)
        def _():
            arrived(m, 6)
            if m // PARTS < GROUPS - 1:
                when(x == 1, m, left, 6, 5)
            share(m, 6)

    def lag5(m):
        if m // PARTS == GROUPS - 1:
            return

        @pl.when(x == 0)
        def _():
            arrived(m, 5)
            share(m, 5)

    lags = [lag0, lag1, lag2, lag3, lag4, lag5]

    def step(n):
        for lag, event in enumerate(lags):
            if 0 <= n - lag < PIECES:
                event(n - lag)

    for g in range(GROUPS):
        for o in (2, 1, 3):
            kv_copy(o, g).start()
        kv_local(g).start()

    done = PARTS - 1 + len(lags) - 1
    for n in range(done + 1):
        step(n)
        if n == 1:
            send_q(0)
        if n == 4:
            send_q(1)

    def whole(g, slots=6):
        ref = kv[g].at[pl.ds(0, slots)]
        return remote(ref, ref, sib_send.at[g], sib_recv.at[g], sibling)

    def chunk(j):
        return lax.rem(y + j + 1, NHEAD)

    def picks(h):
        valid, slot = [None], [0]
        for t in range(TOPK):
            named = chosen[0, h, t]
            valid.append(named >= 0)
            slot.append(jnp.where(named >= 0, jnp.clip(seq - named, 0, SLOTS - 1), 0))
        return valid, slot

    behind = (lax.broadcasted_iota(jnp.int32, (BAND, TOK), 0)
              - lax.broadcasted_iota(jnp.int32, (BAND, TOK), 1))
    weights = (weights_a, weights_b)

    def queries(h, c):
        wide = qbuf[h, c]
        return jnp.concatenate([wide[:, g * DH:(g + 1) * DH] for g in range(GRP)], axis=0)

    def multiply(h, c, q, u, into, top):
        valid, slot = picks(h)
        t, half = u // 2, u % 2
        s = lax.dot_general(kv[2 * h][slot[t], half * BAND:(half + 1) * BAND], q, (((1,), (1,)), ((), ())),
                            preferred_element_type=jnp.float32)
        if t == 0:
            seen = behind <= c * TOK - u * BAND
            s = jnp.concatenate(
                [jnp.where(seen, s[:, g * TOK:(g + 1) * TOK], NEG) for g in range(GRP)], axis=1)
        into[u] = s
        high = jnp.max(s, axis=0, keepdims=True)
        if t > 0:
            high = jnp.where(valid[t], high, NEG)
        return high if top is None else jnp.maximum(top, high)

    def exponent(h, c, u, source, top, total):
        valid, _ = picks(h)
        shift = top if u < 2 else jnp.where(valid[u // 2], top, -NEG)
        p = jnp.exp2((source[u] - shift) * RATE)
        weights[h][c, u * BAND:(u + 1) * BAND] = p.astype(jnp.bfloat16)
        add = jnp.sum(p, axis=0, keepdims=True)
        return add if total is None else total + add

    def flip(h):
        _, slot = picks(h)
        for t in range(TOPK + 1):
            flipped[h, :, t * BLK:(t + 1) * BLK] = kv[2 * h + 1][slot[t]].T

    def attend(h, c, side):
        q0 = side * 2 * TOK
        acc = lax.dot_general(flipped[h], weights[h][c, :, q0:q0 + 2 * TOK], (((1,), (0,)), ((), ())),
                              preferred_element_type=jnp.float32)
        res = acc / totals[h, c, 0:1, q0:q0 + 2 * TOK]
        for g in range(2):
            obuf[h, c, :, q0 + g * DH:q0 + (g + 1) * DH] = res[:, g * TOK:(g + 1) * TOK].T.astype(jnp.bfloat16)

    def hand_out(h, j):
        o = lax.rem(j + 1, NHEAD)
        for k in (1, 2, 3):
            pl.when(o == k)(lambda: out_copy(k, h).start())
        pl.when(o == 0)(lambda: out_local(h).start())

    def weigh(h, j, source, top, into, other):
        c, later = chunk(j), chunk(j + 1)
        q = queries(h, later)
        total, ahead = None, None
        for u in range(BANDS):
            ahead = multiply(h, later, q, u, into, ahead)
            total = exponent(h, c, u, source, top, total)
            if other is not None and u % 4 == 3:
                attend(other, c, u // 4)
        totals[h, c] = jnp.broadcast_to(total, (8, GRP * TOK))
        return ahead

    def weigh_phase(h, other, steps):
        whole(2 * h).wait_recv()
        q_three(h).wait_recv()
        q_local(h).wait()
        if other is not None:
            whole(2 * other + 1).wait_recv()
            flip(other)
        q = queries(h, chunk(0))
        top = None
        for u in range(BANDS):
            top = multiply(h, chunk(0), q, u, scores_a, top)

        def after(jj, place):
            if other is not None:
                hand_out(other, 2 * jj + place)
            for at_jj, at_place, n in steps:
                if at_place == place:
                    pl.when(jj == at_jj)(lambda: step(n))

        def body(jj, top):
            top = weigh(h, 2 * jj, scores_a, top, scores_b, other)
            after(jj, 0)
            top = weigh(h, 2 * jj + 1, scores_b, top, scores_a, other)
            after(jj, 1)
            return top

        lax.fori_loop(0, NHEAD // 2, body, top)

    weigh_phase(0, None, [(0, 0, done + 1), (0, 1, done + 2), (1, 0, done + 3), (1, 1, done + 4)])
    weigh_phase(1, 0, [(0, 0, done + 5)])

    whole(2 * HLOC - 1).wait_recv()
    flip(HLOC - 1)

    def finish(j, _):
        for side in range(2):
            attend(HLOC - 1, chunk(j), side)
        hand_out(HLOC - 1, j)
        return 0

    lax.fori_loop(0, NHEAD, finish, 0)

    for g in range(GROUPS):
        kv_three(g).wait_send()
        whole(g).wait_send()

        def sent(slots):
            ref = kv[g].at[pl.ds(0, slots)]
            remote(ref, ref, win_send.at[g], sib_recv.at[g], up).wait_send()

        if g < GROUPS - 1:
            sent(6)
        else:
            pl.when(x == 0)(lambda: sent(7))
            pl.when(x == 1)(lambda: sent(5))
            pl.when(x > 1)(lambda: sent(6))
    for h in range(HLOC):
        q_three(h).wait_send()
        out_three(h).wait()
        out_local(h).wait()


def on_device(query, keys, values, chosen):
    nseq = lax.axis_size("seq")
    dma = pltpu.SemaphoreType.DMA
    any_spec = pl.BlockSpec(memory_space=pl.ANY)

    def body(*refs):
        kernel(nseq, *refs)

    return pl.pallas_call(
        body,
        out_shape=pltpu.VMEM(query.shape, jnp.bfloat16),
        in_specs=[pl.BlockSpec(memory_space=pltpu.SMEM), any_spec, any_spec, any_spec],
        out_specs=pl.BlockSpec(memory_space=pltpu.VMEM),
        scratch_shapes=[pltpu.VMEM((SLOTS, BLK, DH), jnp.bfloat16)] * GROUPS + [
            pltpu.VMEM((HLOC, NHEAD, TOK, WIDE), jnp.bfloat16),
            pltpu.VMEM((HLOC, NHEAD, TOK, WIDE), jnp.bfloat16),
            pltpu.VMEM((BANDS, BAND, GRP * TOK), jnp.float32),
            pltpu.VMEM((BANDS, BAND, GRP * TOK), jnp.float32),
            pltpu.VMEM((NHEAD, (TOPK + 1) * BLK, GRP * TOK), jnp.bfloat16),
            pltpu.VMEM((NHEAD, (TOPK + 1) * BLK, GRP * TOK), jnp.bfloat16),
            pltpu.VMEM((HLOC, NHEAD, 8, GRP * TOK), jnp.float32),
            pltpu.VMEM((HLOC, DH, (TOPK + 1) * BLK), jnp.bfloat16),
            dma((GROUPS,)), dma((GROUPS,)),
            dma((HLOC,)), dma((HLOC,)),
            dma((GROUPS,)), dma((PIECES, 6)),
            dma((GROUPS,)), dma((GROUPS,)),
            dma((HLOC,)), dma((HLOC,)),
            dma((GROUPS + 2 * HLOC,)),
        ],
        compiler_params=pltpu.CompilerParams(
            collective_id=0, has_side_effects=True, vmem_limit_bytes=56 * 1024 * 1024),
        cost_estimate=pl.CostEstimate(
            flops=4 * BLK * HLOC * GRP * BLK * 4 * DH, bytes_accessed=4 * 1024 * 1024,
            transcendentals=HLOC * GRP * BLK * BLK * 4),
        name="window_attention",
    )(chosen, query, keys, values)


def solution(mesh):
    in_specs = (
        P(("seq", "head"), None),
        P(("seq", "head"), None),
        P(("seq", "head"), None),
        P("seq", "head", None),
    )
    return jax.shard_map(
        on_device, mesh=mesh, in_specs=in_specs, out_specs=P(("seq", "head"), None), check_vma=False
    )
```

```python
import math

import jax
import jax.numpy as jnp
from jax import lax
from jax.experimental import pallas as pl
from jax.experimental.pallas import tpu as pltpu
from jax.sharding import PartitionSpec as P

HQ = 32
HK = 8
DH = 128
BLK = 512
TOPK = 3
GRP = HQ // HK
NHEAD = 4
HLOC = HK // NHEAD
TOK = BLK // NHEAD
NX = 4
SLOTS = 13
GROUPS = 2 * HLOC
PARTS = 2
PIECES = GROUPS * PARTS
ROWS = BLK // PARTS
WIDE = GRP * DH
NEG = -1e30
RATE = math.log2(math.e) / math.sqrt(DH)
MESH = pl.DeviceIdType.MESH


def kernel(nseq, chosen, query, keys, values, out, kv0, kv1, kv2, kv3, qbuf, obuf, scores, weights, totals, flipped, relay,
           own_send, own_recv, q_send, q_recv, win_send, win_recv, sib_send, sib_recv,
           out_send, out_recv, relay_recv, relay_send, local_sem):
    kv = (kv0, kv1, kv2, kv3)
    nz = nseq // (2 * NX)
    seq = lax.axis_index("seq")
    y = lax.axis_index("head")
    core = lax.rem(seq, 2)
    x = lax.rem(seq // 2, NX)
    z = seq // (2 * NX)

    def at(zz, xx):
        return ((zz * NX + xx) * 2 + core, y)

    up = at(lax.rem(z + 1, nz), x)
    down = at(lax.rem(z + nz - 1, nz), x)
    right = at(z, lax.rem(x + 1, NX))
    left = at(z, lax.rem(x + NX - 1, NX))
    sibling = (seq + 1 - 2 * core, y)

    def partner(o):
        return (seq, lax.rem(y + o, NHEAD))

    barrier = pltpu.get_barrier_semaphore()
    for who in [up, down, right, left, sibling, partner(1), partner(2), partner(3)]:
        pl.semaphore_signal(barrier, inc=1, device_id=who, device_id_type=MESH)
    pl.semaphore_wait(barrier, 8)

    def columns(start, width):
        return pl.ds(pl.multiple_of(start, DH), width)

    def remote(src, dst, send, recv, to):
        return pltpu.make_async_remote_copy(
            src_ref=src, dst_ref=dst, send_sem=send, recv_sem=recv, device_id=to, device_id_type=MESH)

    own_rows = pl.ds(pl.multiple_of(y * TOK, TOK), TOK)

    def kv_source(g, to_y):
        return (keys, values)[g % 2].at[:, columns((to_y * HLOC + g // 2) * DH, DH)]

    def kv_copy(o, g):
        to = partner(o)
        return remote(kv_source(g, to[1]), kv[g].at[0, own_rows], own_send.at[g], own_recv.at[g], to)

    def kv_local(g):
        return pltpu.make_async_copy(kv_source(g, y), kv[g].at[0, own_rows], local_sem.at[g])

    def q_source(h, to_y):
        return query.at[:, columns((to_y * HLOC + h) * WIDE, WIDE)]

    def q_copy(o, h):
        to = partner(o)
        return remote(q_source(h, to[1]), qbuf.at[h, y], q_send.at[h], q_recv.at[h], to)

    def q_local(h):
        return pltpu.make_async_copy(q_source(h, y), qbuf.at[h, y], local_sem.at[GROUPS + h])

    def out_place(to_y, h):
        return out.at[:, columns((to_y * HLOC + h) * WIDE, WIDE)]

    def out_copy(o, h):
        to = partner(o)
        return remote(obuf.at[h, to[1]], out_place(y, h), out_send.at[h], out_recv.at[h], to)

    def half(k):
        return pl.ds(k * TOK // 2, TOK // 2)

    def out_relay(h, k):
        return remote(obuf.at[h, partner(2)[1], half(k)], relay.at[h, k], out_send.at[h], relay_recv.at[h, k],
                      partner(1 + 2 * k))

    def out_pass(h, k):
        relay_in = relay.at[h, k]
        remote(relay_in, relay_in, out_send.at[h], relay_recv.at[h, k], sibling).wait_recv()
        origin = partner(3 - 2 * k)[1]
        remote(relay_in, out_place(origin, h).at[half(k)], relay_send.at[h], out_recv.at[h], partner(1 + 2 * k)).start()

    def pass_on(h):
        for k in range(2):
            out_pass(h, k)

    def out_local(h):
        return pltpu.make_async_copy(obuf.at[h, y], out_place(y, h), local_sem.at[GROUPS + HLOC + h])

    def three(ref, send, recv):
        return remote(ref, ref, send, recv, sibling)

    def kv_three(g):
        return three(kv[g].at[0, pl.ds(0, 3 * TOK)], own_send.at[g], own_recv.at[g])

    def q_three(h):
        return three(qbuf.at[h, pl.ds(0, 3)], q_send.at[h], q_recv.at[h])

    def out_three(h):
        return three(obuf.at[h, pl.ds(0, 3)], out_send.at[h], out_recv.at[h])

    def send_q(h):
        for o in (2, 1, 3):
            q_copy(o, h).start()
        q_local(h).start()

    def piece(m, slot):
        return kv[m // PARTS].at[slot, pl.ds((m % PARTS) * ROWS, ROWS)]

    def forward(m, to, r, into):
        remote(piece(m, 2 * r), piece(m, 2 * into),
               win_send.at[m // PARTS], win_recv.at[m, into - 1], to).start()

    def arrived(m, r):
        remote(piece(m, 2 * r), piece(m, 2 * r), win_send.at[m // PARTS], win_recv.at[m, r - 1], up).wait_recv()

    def share(m, r):
        g = m // PARTS

        def go():
            remote(kv[g].at[2 * r], kv[g].at[2 * r + 1 - 2 * core], sib_send.at[g], sib_recv.at[g], sibling).start()

        if m % PARTS < PARTS - 1:
            return
        if r == 0:
            pl.when(core == 0)(go)
        elif r == 6:
            pl.when(core == 1)(go)
        else:
            go()

    def when(cond, *args):
        pl.when(cond)(lambda: forward(*args))

    def lag0(m):
        if m % PARTS == 0:
            kv_three(m // PARTS).wait_recv()
            kv_local(m // PARTS).wait()
        forward(m, up, 0, 4)
        when(x < 3, m, right, 0, 1)
        when(x == 0, m, left, 0, 3)
        share(m, 0)

    def lag1(m):
        arrived(m, 4)
        when(x > 0, m, left, 4, 3)
        when(x == 3, m, right, 4, 1)
        when(x < 2, m, right, 4, 5)
        share(m, 4)

        @pl.when(x == 3)
        def _():
            arrived(m, 3)
            forward(m, left, 3, 2)
            share(m, 3)

        @pl.when(x > 0)
        def _():
            arrived(m, 1)
            when(x == 2, m, right, 1, 2)
            when(x == 3, m, up, 1, 5)
            share(m, 1)

    def lag2(m):
        @pl.when(x == 0)
        def _():
            arrived(m, 1)
            share(m, 1)

        @pl.when(x < 3)
        def _():
            arrived(m, 3)
            when(x == 0, m, left, 3, 6)
            when(x == 2, m, left, 3, 2)
            share(m, 3)

        @pl.when(x == 3)
        def _():
            arrived(m, 5)
            forward(m, right, 5, 2)
            share(m, 5)
            arrived(m, 2)
            share(m, 2)

        @pl.when(x == 2)
        def _():
            arrived(m, 2)
            forward(m, up, 2, 6)
            share(m, 2)

        @pl.when((x == 1) | (x == 2))
        def _():
            arrived(m, 5)
            share(m, 5)

    def lag3(m):
        @pl.when(x < 2)
        def _():
            arrived(m, 2)
            forward(m, up, 2, 6)
            share(m, 2)

        @pl.when(x >= 2)
        def _():
            arrived(m, 6)
            share(m, 6)

    def lag4(m):
        @pl.when(x < 2)
        def _():
            arrived(m, 6)
            when(x == 1, m, left, 6, 5)
            share(m, 6)

    def lag5(m):
        @pl.when(x == 0)
        def _():
            arrived(m, 5)
            share(m, 5)

    lags = [lag0, lag1, lag2, lag3, lag4, lag5]

    def step(n):
        for lag, event in enumerate(lags):
            if 0 <= n - lag < PIECES:
                event(n - lag)

    def send_kv(g):
        for o in (2, 1, 3):
            kv_copy(o, g).start()
        kv_local(g).start()

    send_kv(0)

    done = PARTS - 1 + len(lags) - 1
    for n in range(done + 1):
        step(n)
        if n == 0:
            send_kv(1)
        if n == 1:
            send_q(0)
        if n == 2:
            send_kv(2)
        if n == 3:
            send_kv(3)
        if n == 5:
            send_q(1)

    key_at = lax.broadcasted_iota(jnp.int32, (BLK, GRP * TOK), 0)
    token = lax.rem(lax.broadcasted_iota(jnp.int32, (BLK, GRP * TOK), 1), TOK)

    def whole(g):
        ref = kv[g].at[pl.ds(0, 6)]
        return remote(ref, ref, sib_send.at[g], sib_recv.at[g], sibling)

    def picks(h):
        valid, slot = [None], [0]
        for t in range(TOPK):
            pick = chosen[0, h, t]
            valid.append(pick >= 0)
            slot.append(jnp.where(pick >= 0, jnp.clip(seq - pick, 0, SLOTS - 1), 0))
        return valid, slot

    def weigh(h, c):
        wide = qbuf[h, c]
        q = jnp.concatenate([wide[:, g * DH:(g + 1) * DH] for g in range(GRP)], axis=0)
        valid, slot = picks(h)
        top = None
        for t in range(TOPK + 1):
            s = lax.dot_general(kv[2 * h][slot[t]], q, (((1,), (1,)), ((), ())),
                                preferred_element_type=jnp.float32)
            if t == 0:
                s = jnp.where(token + c * TOK >= key_at, s, NEG)
            scores[t] = s
            high = jnp.max(s, axis=0, keepdims=True)
            top = high if t == 0 else jnp.maximum(top, jnp.where(valid[t], high, NEG))
        total = None
        for t in range(TOPK + 1):
            shift = top if t == 0 else jnp.where(valid[t], top, -NEG)
            p = jnp.exp2((scores[t] - shift) * RATE)
            add = jnp.sum(p, axis=0, keepdims=True)
            weights[c, t] = p.astype(jnp.bfloat16)
            total = add if t == 0 else total + add
        totals[c] = jnp.broadcast_to(total, (8, GRP * TOK))

    def flip(h):
        _, slot = picks(h)
        for t in range(TOPK + 1):
            flipped[t] = kv[2 * h + 1][slot[t]].T

    def attend(h, c, o):
        acc = None
        for t in range(TOPK + 1):
            part = lax.dot_general(flipped[t], weights[c, t], (((1,), (0,)), ((), ())),
                                   preferred_element_type=jnp.float32)
            acc = part if t == 0 else acc + part
        res = acc / totals[c, 0:1]
        for g in range(GRP):
            obuf[h, c, :, g * DH:(g + 1) * DH] = res[:, g * TOK:(g + 1) * TOK].T.astype(jnp.bfloat16)
        for k in (1, 3):
            pl.when(o == k)(lambda: out_copy(k, h).start())

        @pl.when(o == 2)
        def _():
            for k in range(2):
                out_relay(h, k).start()

        pl.when(o == 0)(lambda: out_local(h).start())

    def phase(h, work, steps):
        def body(j, _):
            o = lax.rem(2 + 3 * j + 3 * (j // 2) + 2 * (j // 3), NHEAD)
            work(h, lax.rem(y + o, NHEAD), o)
            for after, then in steps:
                pl.when(j == after)(then)
            return 0

        lax.fori_loop(0, NHEAD, body, 0)

    def weigh_phase(h, steps):
        whole(2 * h).wait_recv()
        q_three(h).wait_recv()
        q_local(h).wait()
        phase(h, lambda h, c, o: weigh(h, c), steps)

    def attend_phase(h, steps):
        whole(2 * h + 1).wait_recv()
        flip(h)
        phase(h, attend, steps)

    weigh_phase(0, [(0, lambda: step(done + 1)), (2, lambda: step(done + 2))])
    attend_phase(0, [(1, lambda: step(done + 3)), (3, lambda: step(done + 4))])
    weigh_phase(1, [(0, lambda: step(done + 5)), (1, lambda: pass_on(0)), (2, lambda: step(done + 6))])
    attend_phase(1, [(2, lambda: pass_on(1))])

    for g in range(GROUPS):
        kv_three(g).wait_send()
        whole(g).wait_send()
        ref = kv[g].at[pl.ds(0, 6)]
        remote(ref, ref, win_send.at[g], sib_recv.at[g], up).wait_send()
    for h in range(HLOC):
        q_three(h).wait_send()
        out_three(h).wait()
        out_local(h).wait()
        three(relay.at[h], relay_send.at[h], out_recv.at[h]).wait_send()


def on_device(query, keys, values, chosen):
    nseq = lax.axis_size("seq")
    dma = pltpu.SemaphoreType.DMA
    any_spec = pl.BlockSpec(memory_space=pl.ANY)

    def body(*refs):
        kernel(nseq, *refs)

    return pl.pallas_call(
        body,
        out_shape=pltpu.VMEM(query.shape, jnp.bfloat16),
        in_specs=[pl.BlockSpec(memory_space=pltpu.SMEM), any_spec, any_spec, any_spec],
        out_specs=pl.BlockSpec(memory_space=pltpu.VMEM),
        scratch_shapes=[pltpu.VMEM((SLOTS, BLK, DH), jnp.bfloat16)] * GROUPS + [
            pltpu.VMEM((HLOC, NHEAD, TOK, WIDE), jnp.bfloat16),
            pltpu.VMEM((HLOC, NHEAD, TOK, WIDE), jnp.bfloat16),
            pltpu.VMEM((TOPK + 1, GRP * TOK, BLK), jnp.float32),
            pltpu.VMEM((NHEAD, TOPK + 1, GRP * TOK, BLK), jnp.bfloat16),
            pltpu.VMEM((NHEAD, 8, GRP * TOK), jnp.float32),
            pltpu.VMEM((TOPK + 1, DH, BLK), jnp.bfloat16),
            pltpu.VMEM((HLOC, 2, TOK // 2, WIDE), jnp.bfloat16),
            dma((GROUPS,)), dma((GROUPS,)),
            dma((HLOC,)), dma((HLOC,)),
            dma((GROUPS,)), dma((PIECES, 6)),
            dma((GROUPS,)), dma((GROUPS,)),
            dma((HLOC,)), dma((HLOC,)),
            dma((HLOC, 2)), dma((HLOC,)),
            dma((GROUPS + 2 * HLOC,)),
        ],
        compiler_params=pltpu.CompilerParams(
            collective_id=0, has_side_effects=True, vmem_limit_bytes=56 * 1024 * 1024),
        cost_estimate=pl.CostEstimate(
            flops=4 * BLK * HLOC * GRP * BLK * 4 * DH, bytes_accessed=4 * 1024 * 1024,
            transcendentals=HLOC * GRP * BLK * BLK * 4),
        name="window_attention",
    )(chosen, query, keys, values)


def solution(mesh):
    in_specs = (
        P(("seq", "head"), None),
        P(("seq", "head"), None),
        P(("seq", "head"), None),
        P("seq", "head", None),
    )
    return jax.shard_map(
        on_device, mesh=mesh, in_specs=in_specs, out_specs=P(("seq", "head"), None), check_vma=False
    )
```

```python
import math

import jax
import jax.numpy as jnp
from jax import lax
from jax.experimental import pallas as pl
from jax.experimental.pallas import tpu as pltpu
from jax.sharding import PartitionSpec as P

HQ = 32
HK = 8
DH = 128
BLK = 512
TOPK = 3
GRP = HQ // HK
NHEAD = 4
HLOC = HK // NHEAD
TOK = BLK // NHEAD
NX = 4
SLOTS = 13
GROUPS = 2 * HLOC
PARTS = 2
PIECES = GROUPS * PARTS
ROWS = BLK // PARTS
WIDE = GRP * DH
NEG = -1e30
RATE = math.log2(math.e) / math.sqrt(DH)
MESH = pl.DeviceIdType.MESH

ROUTES = {
    0: [
        (0, 0), (0, "Z", 0, 4), (0, "P", 0, 1), (0, "M", 0, 3), (2, 4),
        (2, "P", 4, 5), (4, 1), (4, "Z", 1, 5, 6, 8), (4, 3), (4, "M", 3, 6), (6, 2),
        (6, "Z", 2, 6), (9, 6), (10, 5),
    ],
    1: [
        (0, 0), (0, "Z", 0, 4), (0, "P", 0, 1), (2, 4), (2, "M", 4, 3),
        (2, "P", 4, 5), (2, 1), (4, 3), (4, 5), (6, 2),
        (6, "Z", 2, 6), (8, 6), (8, "M", 6, 5, 0, 6),
    ],
    2: [
        (0, 0), (0, "Z", 0, 4), (0, "P", 0, 1), (2, 4), (2, "M", 4, 3),
        (2, 1), (2, "P", 1, 2), (4, 3), (4, "M", 3, 2), (4, 2),
        (4, "Z", 2, 6), (4, 5), (6, 6),
    ],
    3: [
        (0, 0), (0, "Z", 0, 4), (2, 4), (2, "P", 4, 1), (2, "M", 4, 3),
        (2, 3), (2, "M", 3, 2), (2, 1), (2, "Z", 1, 5), (4, 5),
        (4, "P", 5, 2), (4, 2), (5, 6),
    ],
}
TICKS = 18
ITEM_TICKS = (12, 12, 13, 14, 14, 14, 15, 16, 16, 16, 17, 17, 17, 17, 17, 17)


def kernel(nseq, chosen, query, keys, values, out, kv, blocks, qbuf, obuf, scores, weights, totals, flipped,
           own_send, own_recv, q_send, q_recv, win_send, win_recv, sib_send, sib_recv,
           out_send, out_recv, local_sem):
    nz = nseq // (2 * NX)
    seq = lax.axis_index("seq")
    y = lax.axis_index("head")
    core = lax.rem(seq, 2)
    x = lax.rem(seq // 2, NX)
    z = seq // (2 * NX)

    def at(zz, xx):
        return ((zz * NX + xx) * 2 + core, y)

    up = at(lax.rem(z + 1, nz), x)
    down = at(lax.rem(z + nz - 1, nz), x)
    right = at(z, lax.rem(x + 1, NX))
    left = at(z, lax.rem(x + NX - 1, NX))
    sibling = (seq + 1 - 2 * core, y)

    def partner(o):
        return (seq, lax.rem(y + o, NHEAD))

    place = z * NX + x
    barrier = pltpu.get_barrier_semaphore()

    def greet(who):
        pl.semaphore_signal(barrier, inc=1, device_id=who, device_id_type=MESH)

    for who in [right, left, sibling, partner(1), partner(2), partner(3)]:
        greet(who)
    pl.when(z < nz - 1)(lambda: greet(up))
    pl.when(z > 0)(lambda: greet(down))
    edge = (z == 0) | (z == nz - 1)
    pl.when(edge)(lambda: pl.semaphore_wait(barrier, 7))
    pl.when(jnp.logical_not(edge))(lambda: pl.semaphore_wait(barrier, 8))

    def columns(start, width):
        return pl.ds(pl.multiple_of(start, DH), width)

    def remote(src, dst, send, recv, to):
        return pltpu.make_async_remote_copy(
            src_ref=src, dst_ref=dst, send_sem=send, recv_sem=recv, device_id=to, device_id_type=MESH)

    own_rows = pl.ds(pl.multiple_of(y * TOK, TOK), TOK)

    def kv_source(h, i, to_y):
        return (keys, values)[i].at[:, columns((to_y * HLOC + h) * DH, DH)]

    def kv_copy(o, h, i):
        to, g = partner(o), 2 * h + i
        return remote(kv_source(h, i, to[1]), kv.at[g, 0, own_rows], own_send.at[g], own_recv.at[g], to)

    def kv_local(h, i):
        return pltpu.make_async_copy(kv_source(h, i, y), kv.at[2 * h + i, 0, own_rows], local_sem.at[2 * h + i])

    def q_source(h, to_y):
        return query.at[:, columns((to_y * HLOC + h) * WIDE, WIDE)]

    def q_copy(o, h):
        to = partner(o)
        return remote(q_source(h, to[1]), qbuf.at[h, y], q_send.at[h], q_recv.at[h], to)

    def q_local(h):
        return pltpu.make_async_copy(q_source(h, y), qbuf.at[h, y], local_sem.at[GROUPS + h])

    def q_local_wait(h):
        pltpu.make_async_copy(qbuf.at[h, 0], qbuf.at[h, 0], local_sem.at[GROUPS + h]).wait()

    def out_place(to_y, h):
        return out.at[:, columns((to_y * HLOC + h) * WIDE, WIDE)]

    def out_copy(o, h):
        to = partner(o)
        return remote(obuf.at[h, to[1]], out_place(y, h), out_send.at[h], out_recv.at[h], to)

    def out_local(h):
        return pltpu.make_async_copy(obuf.at[h, y], out_place(y, h), local_sem.at[GROUPS + HLOC + h])

    def three(ref, send, recv):
        return remote(ref, ref, send, recv, sibling)

    def kv_three(g):
        return three(kv.at[g, 0, pl.ds(0, 3 * TOK)], own_send.at[g], own_recv.at[g])

    def kv_local_wait(g):
        ref = kv.at[g, 0, pl.ds(0, TOK)]
        pltpu.make_async_copy(ref, ref, local_sem.at[g]).wait()

    def q_three(h):
        return three(qbuf.at[h, pl.ds(0, 3)], q_send.at[h], q_recv.at[h])

    def out_three(h):
        return three(obuf.at[h, pl.ds(0, 3)], out_send.at[h], out_recv.at[h])

    def send_q(h):
        for o in (2, 1, 3):
            q_copy(o, h).start()
        q_local(h).start()

    def piece(m, slot):
        return kv.at[m // PARTS, slot, pl.ds(pl.multiple_of(lax.rem(m, PARTS) * ROWS, ROWS), ROWS)]

    def forward(m, to, r, into):
        remote(piece(m, 2 * r), piece(m, 2 * into),
               win_send.at[m // PARTS], win_recv.at[m, into - 1], to).start()

    def arrived(m, r):
        remote(piece(m, 2 * r), piece(m, 2 * r), win_send.at[m // PARTS], win_recv.at[m, r - 1], up).wait_recv()

    def share(m, r):
        g = m // PARTS

        def go():
            remote(kv.at[g, 2 * r], kv.at[g, 2 * r + 1 - 2 * core], sib_send.at[g], sib_recv.at[g], sibling).start()

        whole_slot = lax.rem(m, PARTS) == PARTS - 1
        if r == 0:
            whole_slot = whole_slot & (core == 0)
        elif r == 6:
            whole_slot = whole_slot & (core == 1)
        pl.when(whole_slot)(go)

    def own(m):
        @pl.when(lax.rem(m, PARTS) == 0)
        def _():
            kv_three(m // PARTS).wait_recv()
            kv_local_wait(m // PARTS)

    def event(m, entry):
        if len(entry) > 2:
            there = place >= entry[2]
            if entry[1] == "Z":
                there = there & (z < nz - 1)
            if len(entry) > 4:
                there = there & (m >= entry[4]) & (m < entry[5])
            to = {"Z": up, "P": right, "M": left}[entry[1]]
            pl.when(there)(lambda: forward(m, to, entry[2], entry[3]))
        else:
            if entry[1] == 0:
                own(m)
            else:
                pl.when(place >= entry[1])(lambda: arrived(m, entry[1]))
            share(m, entry[1])

    def step(n):
        for xx in range(NX):
            @pl.when(x == xx)
            def _():
                for lag in sorted({entry[0] for entry in ROUTES[xx]}):
                    m = n - lag

                    @pl.when((m >= 0) & (m < PIECES))
                    def _():
                        for entry in ROUTES[xx]:
                            if entry[0] == lag:
                                event(m, entry)

    def send_kv(h, _):
        for i in range(2):
            for o in (2, 1, 3):
                kv_copy(o, h, i).start()
            kv_local(h, i).start()
        return 0

    lax.fori_loop(0, HLOC, send_kv, 0)

    def whole(g, slots=6):
        ref = kv.at[g, pl.ds(0, slots)]
        return remote(ref, ref, sib_send.at[g], sib_recv.at[g], sibling)

    def picks(h):
        valid, slot = [None], [0]
        for t in range(TOPK):
            pick = chosen[0, h, t]
            valid.append(pick >= 0)
            slot.append(seq - pick)
        return valid, slot

    def collect(g):
        _, slot = picks(g // 2)

        def part(i, _):
            rows = pl.ds(pl.multiple_of(i * DH, DH), DH)
            block = kv[g, 0, rows]
            blocks[g % 2, 0, rows] = block
            found = [block] * TOPK
            for d in range(1, SLOTS):
                block = kv[g, d, rows]
                for t in range(TOPK):
                    found[t] = jnp.where(slot[t + 1] == d, block, found[t])
            for t in range(TOPK):
                blocks[g % 2, t + 1, rows] = found[t]
            return 0

        lax.fori_loop(0, BLK // DH, part, 0)

    behind = (lax.broadcasted_iota(jnp.int32, (BLK, TOK), 0)
              - lax.broadcasted_iota(jnp.int32, (BLK, TOK), 1))

    def weigh(h, j):
        @pl.when(j == 0)
        def _():
            whole(2 * h).wait_recv()
            q_three(h).wait_recv()
            q_local_wait(h)
            collect(2 * h)

        c = lax.rem(y + j + 1, NHEAD)
        wide = qbuf[h, c]
        q = jnp.concatenate([wide[:, g * DH:(g + 1) * DH] for g in range(GRP)], axis=0)
        valid, _ = picks(h)
        top = None
        for t in range(TOPK + 1):
            s = lax.dot_general(blocks[0, t], q, (((1,), (1,)), ((), ())), preferred_element_type=jnp.float32)
            if t == 0:
                seen = behind <= c * TOK
                s = jnp.concatenate(
                    [jnp.where(seen, s[:, g * TOK:(g + 1) * TOK], NEG) for g in range(GRP)], axis=1)
            scores[t] = s
            high = jnp.max(s, axis=0, keepdims=True)
            top = high if t == 0 else jnp.maximum(top, jnp.where(valid[t], high, NEG))
        total = None
        for t in range(TOPK + 1):
            shift = top if t == 0 else jnp.where(valid[t], top, -NEG)
            p = jnp.exp2((scores[t] - shift) * RATE)
            add = jnp.sum(p, axis=0, keepdims=True)
            weights[c, t] = p.astype(jnp.bfloat16)
            total = add if t == 0 else total + add
        totals[c] = jnp.broadcast_to(total, (8, GRP * TOK))

    def attend(h, j):
        @pl.when(j == 0)
        def _():
            whole(2 * h + 1).wait_recv()
            collect(2 * h + 1)
            for t in range(TOPK + 1):
                flipped[t] = blocks[1, t].T

        o = lax.rem(j + 1, NHEAD)
        c = lax.rem(y + o, NHEAD)
        acc = None
        for t in range(TOPK + 1):
            part = lax.dot_general(flipped[t], weights[c, t], (((1,), (0,)), ((), ())),
                                   preferred_element_type=jnp.float32)
            acc = part if t == 0 else acc + part
        res = acc / totals[c, 0:1]
        for g in range(GRP):
            obuf[h, c, :, g * DH:(g + 1) * DH] = res[:, g * TOK:(g + 1) * TOK].T.astype(jnp.bfloat16)
        for k in (1, 2, 3):
            pl.when(o == k)(lambda: out_copy(k, h).start())
        pl.when(o == 0)(lambda: out_local(h).start())

    def before(n):
        return sum((n + 63 - tick) // 64 for tick in ITEM_TICKS)

    def item(k, _):
        h, kind, j = k // 8, lax.rem(k // 4, 2), lax.rem(k, 4)
        pl.when(kind == 0)(lambda: weigh(h, j))
        pl.when(kind == 1)(lambda: attend(h, j))
        return 0

    def tick(n, _):
        step(n)
        pl.when((n == 3) | (n == 6))(lambda: send_q(n // 6))
        lax.fori_loop(before(n), before(n + 1), item, 0)
        return 0

    lax.fori_loop(0, TICKS, tick, 0)

    def sent(g, m):
        for xx in range(NX):
            for low, high in ((0, 1), (1, 2), (2, nz - 1), (nz - 1, nz)):
                count = 0
                for entry in ROUTES[xx]:
                    if len(entry) > 2 and low * NX + xx >= entry[2] and (entry[1] != "Z" or low < nz - 1):
                        count += len(entry) == 4 or entry[4] <= m < entry[5]
                if count == 0:
                    continue

                @pl.when((x == xx) & (z >= low) & (z < high))
                def _():
                    ref = kv.at[g, pl.ds(0, count)]
                    remote(ref, ref, win_send.at[g], sib_recv.at[g], right).wait_send()

    def finish(g, _):
        kv_three(g).wait_send()
        whole(g).wait_send()
        pl.when(g < GROUPS - 1)(lambda: sent(g, 0))
        pl.when(g == GROUPS - 1)(lambda: sent(g, PIECES - 1))
        return 0

    lax.fori_loop(0, GROUPS, finish, 0)
    for h in range(HLOC):
        q_three(h).wait_send()
        out_three(h).wait()
        out_local(h).wait()


def on_device(query, keys, values, chosen):
    nseq = lax.axis_size("seq")
    dma = pltpu.SemaphoreType.DMA
    any_spec = pl.BlockSpec(memory_space=pl.ANY)

    def body(*refs):
        kernel(nseq, *refs)

    return pl.pallas_call(
        body,
        out_shape=pltpu.VMEM(query.shape, jnp.bfloat16),
        in_specs=[pl.BlockSpec(memory_space=pltpu.SMEM), any_spec, any_spec, any_spec],
        out_specs=pl.BlockSpec(memory_space=pltpu.VMEM),
        scratch_shapes=[
            pltpu.VMEM((GROUPS, SLOTS, BLK, DH), jnp.bfloat16),
            pltpu.VMEM((2, TOPK + 1, BLK, DH), jnp.bfloat16),
            pltpu.VMEM((HLOC, NHEAD, TOK, WIDE), jnp.bfloat16),
            pltpu.VMEM((HLOC, NHEAD, TOK, WIDE), jnp.bfloat16),
            pltpu.VMEM((TOPK + 1, GRP * TOK, BLK), jnp.float32),
            pltpu.VMEM((NHEAD, TOPK + 1, GRP * TOK, BLK), jnp.bfloat16),
            pltpu.VMEM((NHEAD, 8, GRP * TOK), jnp.float32),
            pltpu.VMEM((TOPK + 1, DH, BLK), jnp.bfloat16),
            dma((GROUPS,)), dma((GROUPS,)),
            dma((HLOC,)), dma((HLOC,)),
            dma((GROUPS,)), dma((PIECES, 6)),
            dma((GROUPS,)), dma((GROUPS,)),
            dma((HLOC,)), dma((HLOC,)),
            dma((GROUPS + 2 * HLOC,)),
        ],
        compiler_params=pltpu.CompilerParams(
            collective_id=0, has_side_effects=True, vmem_limit_bytes=56 * 1024 * 1024),
        cost_estimate=pl.CostEstimate(
            flops=4 * BLK * HLOC * GRP * BLK * 4 * DH, bytes_accessed=4 * 1024 * 1024,
            transcendentals=HLOC * GRP * BLK * BLK * 4),
        name="window_attention",
    )(chosen, query, keys, values)


def solution(mesh):
    in_specs = (
        P(("seq", "head"), None),
        P(("seq", "head"), None),
        P(("seq", "head"), None),
        P("seq", "head", None),
    )
    return jax.shard_map(
        on_device, mesh=mesh, in_specs=in_specs, out_specs=P(("seq", "head"), None), check_vma=False
    )
```

```python
import math

import jax
import jax.numpy as jnp
from jax import lax
from jax.experimental import pallas as pl
from jax.experimental.pallas import tpu as pltpu
from jax.sharding import PartitionSpec as P

HQ = 32
HK = 8
DH = 128
BLK = 512
TOPK = 3
GRP = HQ // HK
NHEAD = 4
HLOC = HK // NHEAD
TOK = BLK // NHEAD
NX = 4
SLOTS = 13
GROUPS = 2 * HLOC
PARTS = 2
PIECES = GROUPS * PARTS
ROWS = BLK // PARTS
WIDE = GRP * DH
STRIP = 32
NEG = -1e30
RATE = math.log2(math.e) / math.sqrt(DH)
MESH = pl.DeviceIdType.MESH

ROUTES = {
    0: [
        (0, 0), (0, "Z", 0, 4), (0, "P", 0, 1), (0, "M", 0, 3), (2, 4),
        (2, "P", 4, 5), (4, 1), (4, "Z", 1, 5, 6, 8), (4, 3), (4, "M", 3, 6), (6, 2),
        (6, "Z", 2, 6), (9, 6), (10, 5),
    ],
    1: [
        (0, 0), (0, "Z", 0, 4), (0, "P", 0, 1), (2, 4), (2, "M", 4, 3),
        (2, "P", 4, 5), (2, 1), (4, 3), (4, 5), (6, 2),
        (6, "Z", 2, 6), (8, 6), (8, "M", 6, 5, 0, 6),
    ],
    2: [
        (0, 0), (0, "Z", 0, 4), (0, "P", 0, 1), (2, 4), (2, "M", 4, 3),
        (2, 1), (2, "P", 1, 2), (4, 3), (4, "M", 3, 2), (4, 2),
        (4, "Z", 2, 6), (4, 5), (6, 6),
    ],
    3: [
        (0, 0), (0, "Z", 0, 4), (2, 4), (2, "P", 4, 1), (2, "M", 4, 3),
        (2, 3), (2, "M", 3, 2), (2, 1), (2, "Z", 1, 5), (4, 5),
        (4, "P", 5, 2), (4, 2), (5, 6),
    ],
}
TICKS = 18
ITEM_TICKS = (12, 12, 13, 14, 14, 14, 15, 16, 16, 16, 17, 17, 17, 17, 17, 17)


def kernel(nseq, chosen, query, keys, values, out, kv, blocks, qbuf, obuf, scores, weights, totals, flipped, turned,
           own_send, own_recv, q_send, q_recv, win_send, win_recv, sib_send, sib_recv,
           out_send, out_recv, local_sem):
    nz = nseq // (2 * NX)
    seq = lax.axis_index("seq")
    y = lax.axis_index("head")
    core = lax.rem(seq, 2)
    x = lax.rem(seq // 2, NX)
    z = seq // (2 * NX)

    def at(zz, xx):
        return ((zz * NX + xx) * 2 + core, y)

    up = at(lax.rem(z + 1, nz), x)
    down = at(lax.rem(z + nz - 1, nz), x)
    right = at(z, lax.rem(x + 1, NX))
    left = at(z, lax.rem(x + NX - 1, NX))
    sibling = (seq + 1 - 2 * core, y)

    def partner(o):
        return (seq, lax.rem(y + o, NHEAD))

    place = z * NX + x
    barrier = pltpu.get_barrier_semaphore()

    def greet(who):
        pl.semaphore_signal(barrier, inc=1, device_id=who, device_id_type=MESH)

    for who in [right, left, sibling, partner(1), partner(2), partner(3)]:
        greet(who)
    pl.when(z < nz - 1)(lambda: greet(up))
    pl.when(z > 0)(lambda: greet(down))
    edge = (z == 0) | (z == nz - 1)
    pl.when(edge)(lambda: pl.semaphore_wait(barrier, 7))
    pl.when(jnp.logical_not(edge))(lambda: pl.semaphore_wait(barrier, 8))

    def columns(start, width):
        return pl.ds(pl.multiple_of(start, DH), width)

    def remote(src, dst, send, recv, to):
        return pltpu.make_async_remote_copy(
            src_ref=src, dst_ref=dst, send_sem=send, recv_sem=recv, device_id=to, device_id_type=MESH)

    own_rows = pl.ds(pl.multiple_of(y * TOK, TOK), TOK)

    def kv_source(h, i, to_y):
        return (keys, values)[i].at[:, columns((to_y * HLOC + h) * DH, DH)]

    def kv_copy(o, h, i):
        to, g = partner(o), 2 * h + i
        return remote(kv_source(h, i, to[1]), kv.at[g, 0, own_rows], own_send.at[g], own_recv.at[g], to)

    def kv_local(h, i):
        return pltpu.make_async_copy(kv_source(h, i, y), kv.at[2 * h + i, 0, own_rows], local_sem.at[2 * h + i])

    def q_source(h, to_y):
        return query.at[:, columns((to_y * HLOC + h) * WIDE, WIDE)]

    def q_copy(o, h):
        to = partner(o)
        return remote(q_source(h, to[1]), qbuf.at[h, y], q_send.at[h], q_recv.at[h], to)

    def q_local(h):
        return pltpu.make_async_copy(q_source(h, y), qbuf.at[h, y], local_sem.at[GROUPS + h])

    def q_local_wait(h):
        pltpu.make_async_copy(qbuf.at[h, 0], qbuf.at[h, 0], local_sem.at[GROUPS + h]).wait()

    def out_place(to_y, h):
        return out.at[:, columns((to_y * HLOC + h) * WIDE, WIDE)]

    def out_copy(o, h):
        to = partner(o)
        return remote(obuf.at[h, to[1]], out_place(y, h), out_send.at[h], out_recv.at[h], to)

    def out_local(h):
        return pltpu.make_async_copy(obuf.at[h, y], out_place(y, h), local_sem.at[GROUPS + HLOC + h])

    def three(ref, send, recv):
        return remote(ref, ref, send, recv, sibling)

    def kv_three(g):
        return three(kv.at[g, 0, pl.ds(0, 3 * TOK)], own_send.at[g], own_recv.at[g])

    def kv_local_wait(g):
        ref = kv.at[g, 0, pl.ds(0, TOK)]
        pltpu.make_async_copy(ref, ref, local_sem.at[g]).wait()

    def q_three(h):
        return three(qbuf.at[h, pl.ds(0, 3)], q_send.at[h], q_recv.at[h])

    def out_three(h):
        return three(obuf.at[h, pl.ds(0, 3)], out_send.at[h], out_recv.at[h])

    def send_q(h):
        for o in (2, 1, 3):
            q_copy(o, h).start()
        q_local(h).start()

    def piece(m, slot):
        return kv.at[m // PARTS, slot, pl.ds(pl.multiple_of(lax.rem(m, PARTS) * ROWS, ROWS), ROWS)]

    def forward(m, to, r, into):
        remote(piece(m, 2 * r), piece(m, 2 * into),
               win_send.at[m // PARTS], win_recv.at[m, into - 1], to).start()

    def arrived(m, r):
        remote(piece(m, 2 * r), piece(m, 2 * r), win_send.at[m // PARTS], win_recv.at[m, r - 1], up).wait_recv()

    def share(m, r):
        g = m // PARTS

        def go():
            remote(kv.at[g, 2 * r], kv.at[g, 2 * r + 1 - 2 * core], sib_send.at[g], sib_recv.at[g], sibling).start()

        whole_slot = lax.rem(m, PARTS) == PARTS - 1
        if r == 0:
            whole_slot = whole_slot & (core == 0)
        elif r == 6:
            whole_slot = whole_slot & (core == 1)
        pl.when(whole_slot)(go)

    def own(m):
        @pl.when(lax.rem(m, PARTS) == 0)
        def _():
            kv_three(m // PARTS).wait_recv()
            kv_local_wait(m // PARTS)

    def event(m, entry):
        if len(entry) > 2:
            there = place >= entry[2]
            if entry[1] == "Z":
                there = there & (z < nz - 1)
            if len(entry) > 4:
                there = there & (m >= entry[4]) & (m < entry[5])
            to = {"Z": up, "P": right, "M": left}[entry[1]]
            pl.when(there)(lambda: forward(m, to, entry[2], entry[3]))
        else:
            if entry[1] == 0:
                own(m)
            else:
                pl.when(place >= entry[1])(lambda: arrived(m, entry[1]))
            share(m, entry[1])

    def step(n):
        for xx in range(NX):
            @pl.when(x == xx)
            def _():
                for lag in sorted({entry[0] for entry in ROUTES[xx]}):
                    m = n - lag

                    @pl.when((m >= 0) & (m < PIECES))
                    def _():
                        for entry in ROUTES[xx]:
                            if entry[0] == lag:
                                event(m, entry)

    def send_kv(h, _):
        for i in range(2):
            for o in (2, 1, 3):
                kv_copy(o, h, i).start()
            kv_local(h, i).start()
        return 0

    lax.fori_loop(0, HLOC, send_kv, 0)

    def whole(g, slots=6):
        ref = kv.at[g, pl.ds(0, slots)]
        return remote(ref, ref, sib_send.at[g], sib_recv.at[g], sibling)

    def picks(h):
        valid, slot = [None], [0]
        for t in range(TOPK):
            pick = chosen[0, h, t]
            valid.append(pick >= 0)
            slot.append(seq - pick)
        return valid, slot

    def collect(g):
        _, slot = picks(g // 2)

        def part(i, _):
            rows = pl.ds(pl.multiple_of(i * DH, DH), DH)
            block = kv[g, 0, rows]
            blocks[g % 2, 0, rows] = block
            found = [block] * TOPK
            for d in range(1, SLOTS):
                block = kv[g, d, rows]
                for t in range(TOPK):
                    found[t] = jnp.where(slot[t + 1] == d, block, found[t])
            for t in range(TOPK):
                blocks[g % 2, t + 1, rows] = found[t]
            return 0

        lax.fori_loop(0, BLK // DH, part, 0)

    behind = (lax.broadcasted_iota(jnp.int32, (TOK, TOK), 0)
              - lax.broadcasted_iota(jnp.int32, (TOK, TOK), 1))

    def fold(op, start, rows):
        for i in range(0, rows.shape[0], 8):
            start = op(start, rows[i:i + 8])
        return start

    def weigh(h, j):
        @pl.when(j == 0)
        def _():
            whole(2 * h).wait_recv()
            q_three(h).wait_recv()
            q_local_wait(h)
            collect(2 * h)

        c = lax.rem(y + j + 1, NHEAD)
        for g in range(GRP):
            turned[:, g * TOK:(g + 1) * TOK] = qbuf[h, c, :, g * DH:(g + 1) * DH].T
        valid, _ = picks(h)
        top = None
        for t in range(TOPK + 1):
            high = jnp.full((8, GRP * TOK), NEG, jnp.float32)
            for i in range(BLK // TOK):
                s = jnp.dot(blocks[0, t, i * TOK:(i + 1) * TOK], turned[...], preferred_element_type=jnp.float32)
                if t == 0:
                    seen = behind <= (c - i) * TOK
                    s = jnp.concatenate(
                        [jnp.where(seen, s[:, g * TOK:(g + 1) * TOK], NEG) for g in range(GRP)], axis=1)
                scores[t, i * TOK:(i + 1) * TOK] = s
                high = fold(jnp.maximum, high, s)
            high = jnp.max(high, axis=0, keepdims=True)
            top = high if t == 0 else jnp.maximum(top, jnp.where(valid[t], high, NEG))
        total = jnp.zeros((8, GRP * TOK), jnp.float32)
        for t in range(TOPK + 1):
            shift = top if t == 0 else jnp.where(valid[t], top, -NEG)

            def band(i, total):
                rows = pl.ds(pl.multiple_of(i * STRIP, STRIP), STRIP)
                p = jnp.exp2((scores[t, rows] - shift) * RATE)
                weights[c, pl.ds(pl.multiple_of(t * BLK + i * STRIP, STRIP), STRIP)] = p.astype(jnp.bfloat16)
                return fold(jnp.add, total, p)

            total = lax.fori_loop(0, BLK // STRIP, band, total, unroll=4)
        totals[c] = jnp.broadcast_to(jnp.sum(total, axis=0, keepdims=True), (8, GRP * TOK))

    def attend(h, j):
        @pl.when(j == 0)
        def _():
            whole(2 * h + 1).wait_recv()
            collect(2 * h + 1)
            for t in range(TOPK + 1):
                flipped[:, t * BLK:(t + 1) * BLK] = blocks[1, t].T

        o = lax.rem(j + 1, NHEAD)
        c = lax.rem(y + o, NHEAD)
        for side in range(2):
            q0 = side * 2 * TOK
            acc = jnp.dot(flipped[...], weights[c, :, q0:q0 + 2 * TOK], preferred_element_type=jnp.float32)
            res = acc / totals[c, 0:1, q0:q0 + 2 * TOK]
            for g in range(2):
                obuf[h, c, :, q0 + g * DH:q0 + (g + 1) * DH] = res[:, g * TOK:(g + 1) * TOK].T.astype(jnp.bfloat16)
        for k in (1, 2, 3):
            pl.when(o == k)(lambda: out_copy(k, h).start())
        pl.when(o == 0)(lambda: out_local(h).start())

    def before(n):
        return sum((n + 63 - tick) // 64 for tick in ITEM_TICKS)

    def item(k, _):
        h, kind, j = k // 8, lax.rem(k // 4, 2), lax.rem(k, 4)
        pl.when(kind == 0)(lambda: weigh(h, j))
        pl.when(kind == 1)(lambda: attend(h, j))
        return 0

    def tick(n, _):
        step(n)
        pl.when((n == 3) | (n == 6))(lambda: send_q(n // 6))
        lax.fori_loop(before(n), before(n + 1), item, 0)
        return 0

    lax.fori_loop(0, TICKS, tick, 0)

    def sent(g, m):
        for xx in range(NX):
            for low, high in ((0, 1), (1, 2), (2, nz - 1), (nz - 1, nz)):
                count = 0
                for entry in ROUTES[xx]:
                    if len(entry) > 2 and low * NX + xx >= entry[2] and (entry[1] != "Z" or low < nz - 1):
                        count += len(entry) == 4 or entry[4] <= m < entry[5]
                if count == 0:
                    continue

                @pl.when((x == xx) & (z >= low) & (z < high))
                def _():
                    ref = kv.at[g, pl.ds(0, count)]
                    remote(ref, ref, win_send.at[g], sib_recv.at[g], right).wait_send()

    def finish(g, _):
        kv_three(g).wait_send()
        whole(g).wait_send()
        pl.when(g < GROUPS - 1)(lambda: sent(g, 0))
        pl.when(g == GROUPS - 1)(lambda: sent(g, PIECES - 1))
        return 0

    lax.fori_loop(0, GROUPS, finish, 0)
    for h in range(HLOC):
        q_three(h).wait_send()
        out_three(h).wait()
        out_local(h).wait()


def on_device(query, keys, values, chosen):
    nseq = lax.axis_size("seq")
    dma = pltpu.SemaphoreType.DMA
    any_spec = pl.BlockSpec(memory_space=pl.ANY)

    def body(*refs):
        kernel(nseq, *refs)

    return pl.pallas_call(
        body,
        out_shape=pltpu.VMEM(query.shape, jnp.bfloat16),
        in_specs=[pl.BlockSpec(memory_space=pltpu.SMEM), any_spec, any_spec, any_spec],
        out_specs=pl.BlockSpec(memory_space=pltpu.VMEM),
        scratch_shapes=[
            pltpu.VMEM((GROUPS, SLOTS, BLK, DH), jnp.bfloat16),
            pltpu.VMEM((2, TOPK + 1, BLK, DH), jnp.bfloat16),
            pltpu.VMEM((HLOC, NHEAD, TOK, WIDE), jnp.bfloat16),
            pltpu.VMEM((HLOC, NHEAD, TOK, WIDE), jnp.bfloat16),
            pltpu.VMEM((TOPK + 1, BLK, GRP * TOK), jnp.float32),
            pltpu.VMEM((NHEAD, (TOPK + 1) * BLK, GRP * TOK), jnp.bfloat16),
            pltpu.VMEM((NHEAD, 8, GRP * TOK), jnp.float32),
            pltpu.VMEM((DH, (TOPK + 1) * BLK), jnp.bfloat16),
            pltpu.VMEM((DH, GRP * TOK), jnp.bfloat16),
            dma((GROUPS,)), dma((GROUPS,)),
            dma((HLOC,)), dma((HLOC,)),
            dma((GROUPS,)), dma((PIECES, 6)),
            dma((GROUPS,)), dma((GROUPS,)),
            dma((HLOC,)), dma((HLOC,)),
            dma((GROUPS + 2 * HLOC,)),
        ],
        compiler_params=pltpu.CompilerParams(
            collective_id=0, has_side_effects=True, vmem_limit_bytes=56 * 1024 * 1024),
        cost_estimate=pl.CostEstimate(
            flops=4 * BLK * HLOC * GRP * BLK * 4 * DH, bytes_accessed=4 * 1024 * 1024,
            transcendentals=HLOC * GRP * BLK * BLK * 4),
        name="window_attention",
    )(chosen, query, keys, values)


def solution(mesh):
    in_specs = (
        P(("seq", "head"), None),
        P(("seq", "head"), None),
        P(("seq", "head"), None),
        P("seq", "head", None),
    )
    return jax.shard_map(
        on_device, mesh=mesh, in_specs=in_specs, out_specs=P(("seq", "head"), None), check_vma=False
    )
```

```python
import math

import jax
import jax.numpy as jnp
from jax import lax
from jax.experimental import pallas as pl
from jax.experimental.pallas import tpu as pltpu
from jax.sharding import PartitionSpec as P

HQ = 32
HK = 8
DH = 128
BLK = 512
TOPK = 3
GRP = HQ // HK
NHEAD = 4
HLOC = HK // NHEAD
TOK = BLK // NHEAD
NX = 4
SLOTS = 13
GROUPS = 2 * HLOC
PARTS = 2
PIECES = GROUPS * PARTS
ROWS = BLK // PARTS
WIDE = GRP * DH
STRIP = 32
NEG = -1e30
RATE = math.log2(math.e) / math.sqrt(DH)
MESH = pl.DeviceIdType.MESH

ROUTES = {
    0: [
        (0, 0), (0, "Z", 0, 4), (0, "P", 0, 1), (0, "M", 0, 3), (2, 4),
        (2, "P", 4, 5), (4, 1), (4, "Z", 1, 5, 6, 8), (4, 3), (4, "M", 3, 6), (6, 2),
        (6, "Z", 2, 6), (9, 6), (10, 5),
    ],
    1: [
        (0, 0), (0, "Z", 0, 4), (0, "P", 0, 1), (2, 4), (2, "M", 4, 3),
        (2, "P", 4, 5), (2, 1), (4, 3), (4, 5), (6, 2),
        (6, "Z", 2, 6), (8, 6), (8, "M", 6, 5, 0, 6),
    ],
    2: [
        (0, 0), (0, "Z", 0, 4), (0, "P", 0, 1), (2, 4), (2, "M", 4, 3),
        (2, 1), (2, "P", 1, 2), (4, 3), (4, "M", 3, 2), (4, 2),
        (4, "Z", 2, 6), (4, 5), (6, 6),
    ],
    3: [
        (0, 0), (0, "Z", 0, 4), (2, 4), (2, "P", 4, 1), (2, "M", 4, 3),
        (2, 3), (2, "M", 3, 2), (2, 1), (2, "Z", 1, 5), (4, 5),
        (4, "P", 5, 2), (4, 2), (5, 6),
    ],
}
TICKS = 18
ITEM_TICKS = (12, 12, 13, 14, 14, 14, 15, 16, 16, 16, 17, 17, 17, 17, 17, 17)


def kernel(nseq, chosen, query, keys, values, out, kv, blocks, qbuf, obuf, scores, weights, totals, flipped, turned,
           k_all, v_all, q_all, stage, q_relay, out_relay_buf,
           own_send, own_recv, q_send, q_recv, win_send, win_recv, sib_send, sib_recv,
           out_send, out_recv, q_relay_recv, q_relay_send, relay_recv, relay_send, local_sem):
    nz = nseq // (2 * NX)
    seq = lax.axis_index("seq")
    y = lax.axis_index("head")
    core = lax.rem(seq, 2)
    x = lax.rem(seq // 2, NX)
    z = seq // (2 * NX)

    def at(zz, xx):
        return ((zz * NX + xx) * 2 + core, y)

    up = at(lax.rem(z + 1, nz), x)
    down = at(lax.rem(z + nz - 1, nz), x)
    right = at(z, lax.rem(x + 1, NX))
    left = at(z, lax.rem(x + NX - 1, NX))
    sibling = (seq + 1 - 2 * core, y)

    def partner(o):
        return (seq, lax.rem(y + o, NHEAD))

    place = z * NX + x
    loads = [pltpu.make_async_copy(src, dst, local_sem.at[i])
             for i, (src, dst) in enumerate([(keys, k_all), (values, v_all), (query, q_all)])]
    for load in loads:
        load.start()

    barrier = pltpu.get_barrier_semaphore()

    def greet(who):
        pl.semaphore_signal(barrier, inc=1, device_id=who, device_id_type=MESH)

    for who in [right, left, sibling, partner(1), partner(2), partner(3)]:
        greet(who)
    pl.when(z < nz - 1)(lambda: greet(up))
    pl.when(z > 0)(lambda: greet(down))
    edge = (z == 0) | (z == nz - 1)
    pl.when(edge)(lambda: pl.semaphore_wait(barrier, 7))
    pl.when(jnp.logical_not(edge))(lambda: pl.semaphore_wait(barrier, 8))

    def columns(start, width):
        return pl.ds(pl.multiple_of(start, DH), width)

    def remote(src, dst, send, recv, to):
        return pltpu.make_async_remote_copy(
            src_ref=src, dst_ref=dst, send_sem=send, recv_sem=recv, device_id=to, device_id_type=MESH)

    own_rows = pl.ds(pl.multiple_of(y * TOK, TOK), TOK)

    def kv_copy(o, h):
        to = partner(o)
        return remote(stage.at[to[1] * HLOC + h], kv.at[pl.ds(2 * h, 2), 0, own_rows], own_send.at[h], own_recv.at[h], to)

    def half(k):
        return pl.ds(k * TOK // 2, TOK // 2)

    def q_source(h, to_y):
        return q_all.at[:, columns((to_y * HLOC + h) * WIDE, WIDE)]

    def q_copy(o, h):
        to = partner(o)
        return remote(q_source(h, to[1]), qbuf.at[h, y], q_send.at[h], q_recv.at[h], to)

    def q_via(h, k):
        return remote(q_source(h, partner(2)[1]).at[half(k)], q_relay.at[h, k], q_send.at[h], q_relay_recv.at[h, k],
                      partner(1 + 2 * k))

    def q_pass(h):
        for k in range(2):
            ref = q_relay.at[h, k]
            remote(ref, ref, q_send.at[h], q_relay_recv.at[h, k], sibling).wait_recv()
            remote(ref, qbuf.at[h, partner(3 - 2 * k)[1], half(k)], q_relay_send.at[h], q_recv.at[h],
                   partner(1 + 2 * k)).start()

    def q_local(h):
        return pltpu.make_async_copy(q_source(h, y), qbuf.at[h, y], local_sem.at[GROUPS + h])

    def q_local_wait(h):
        pltpu.make_async_copy(qbuf.at[h, 0], qbuf.at[h, 0], local_sem.at[GROUPS + h]).wait()

    def out_place(to_y, h):
        return out.at[:, columns((to_y * HLOC + h) * WIDE, WIDE)]

    def out_copy(o, h):
        to = partner(o)
        return remote(obuf.at[h, to[1]], out_place(y, h), out_send.at[h], out_recv.at[h], to)

    def out_local(h):
        return pltpu.make_async_copy(obuf.at[h, y], out_place(y, h), local_sem.at[GROUPS + HLOC + h])

    def three(ref, send, recv):
        return remote(ref, ref, send, recv, sibling)

    def kv_three(h):
        return three(kv.at[pl.ds(2 * h, 2), 0, pl.ds(0, 3 * TOK)], own_send.at[h], own_recv.at[h])

    def q_three(h):
        return three(qbuf.at[h, pl.ds(0, 3)], q_send.at[h], q_recv.at[h])

    def out_three(h):
        return three(obuf.at[h, pl.ds(0, 3)], out_send.at[h], out_recv.at[h])

    def send_q(h):
        for k in range(2):
            q_via(h, k).start()
        for o in (1, 3):
            q_copy(o, h).start()
        q_local(h).start()

    def out_via(h, k):
        return remote(obuf.at[h, partner(2)[1], half(k)], out_relay_buf.at[h, k], out_send.at[h], relay_recv.at[h, k],
                      partner(1 + 2 * k))

    def out_pass(h):
        for k in range(2):
            ref = out_relay_buf.at[h, k]
            remote(ref, ref, out_send.at[h], relay_recv.at[h, k], sibling).wait_recv()
            remote(ref, out_place(partner(3 - 2 * k)[1], h).at[half(k)], relay_send.at[h], out_recv.at[h],
                   partner(1 + 2 * k)).start()

    def piece(m, slot):
        return kv.at[m // PARTS, slot, pl.ds(pl.multiple_of(lax.rem(m, PARTS) * ROWS, ROWS), ROWS)]

    def forward(m, to, r, into):
        remote(piece(m, 2 * r), piece(m, 2 * into),
               win_send.at[m // PARTS], win_recv.at[m, into - 1], to).start()

    def arrived(m, r):
        remote(piece(m, 2 * r), piece(m, 2 * r), win_send.at[m // PARTS], win_recv.at[m, r - 1], up).wait_recv()

    def share(m, r):
        g = m // PARTS

        def go():
            remote(kv.at[g, 2 * r], kv.at[g, 2 * r + 1 - 2 * core], sib_send.at[g], sib_recv.at[g], sibling).start()

        whole_slot = lax.rem(m, PARTS) == PARTS - 1
        if r == 0:
            whole_slot = whole_slot & (core == 0)
        elif r == 6:
            whole_slot = whole_slot & (core == 1)
        pl.when(whole_slot)(go)

    def own(m):
        @pl.when(lax.rem(m, 2 * PARTS) == 0)
        def _():
            kv_three(m // (2 * PARTS)).wait_recv()

    def event(m, entry):
        if len(entry) > 2:
            there = place >= entry[2]
            if entry[1] == "Z":
                there = there & (z < nz - 1)
            if len(entry) > 4:
                there = there & (m >= entry[4]) & (m < entry[5])
            to = {"Z": up, "P": right, "M": left}[entry[1]]
            pl.when(there)(lambda: forward(m, to, entry[2], entry[3]))
        else:
            if entry[1] == 0:
                own(m)
            else:
                pl.when(place >= entry[1])(lambda: arrived(m, entry[1]))
            share(m, entry[1])

    def step(n):
        for xx in range(NX):
            @pl.when(x == xx)
            def _():
                for lag in sorted({entry[0] for entry in ROUTES[xx]}):
                    m = n - lag

                    @pl.when((m >= 0) & (m < PIECES))
                    def _():
                        for entry in ROUTES[xx]:
                            if entry[0] == lag:
                                event(m, entry)

    loads[0].wait()
    loads[1].wait()
    for head in range(HK):
        stage[head, 0] = k_all[:, head * DH:(head + 1) * DH]
        stage[head, 1] = v_all[:, head * DH:(head + 1) * DH]
    for h in range(HLOC):
        for o in (2, 1, 3):
            kv_copy(o, h).start()
        for i in range(2):
            kv[2 * h + i, 0, own_rows] = stage[y * HLOC + h, i]
    loads[2].wait()

    def whole(g, slots=6):
        ref = kv.at[g, pl.ds(0, slots)]
        return remote(ref, ref, sib_send.at[g], sib_recv.at[g], sibling)

    def picks(h):
        valid, slot = [None], [0]
        for t in range(TOPK):
            pick = chosen[0, h, t]
            valid.append(pick >= 0)
            slot.append(seq - pick)
        return valid, slot

    def collect(g):
        _, slot = picks(g // 2)

        def part(i, _):
            rows = pl.ds(pl.multiple_of(i * DH, DH), DH)
            block = kv[g, 0, rows]
            blocks[g % 2, 0, rows] = block
            found = [block] * TOPK
            for d in range(1, SLOTS):
                block = kv[g, d, rows]
                for t in range(TOPK):
                    found[t] = jnp.where(slot[t + 1] == d, block, found[t])
            for t in range(TOPK):
                blocks[g % 2, t + 1, rows] = found[t]
            return 0

        lax.fori_loop(0, BLK // DH, part, 0)

    behind = (lax.broadcasted_iota(jnp.int32, (TOK, TOK), 0)
              - lax.broadcasted_iota(jnp.int32, (TOK, TOK), 1))

    def fold(op, start, rows):
        for i in range(0, rows.shape[0], 8):
            start = op(start, rows[i:i + 8])
        return start

    def order(j):
        return lax.rem(2 + 3 * j + 3 * (j // 2) + 2 * (j // 3), NHEAD)

    def weigh(h, j):
        @pl.when(j == 0)
        def _():
            whole(2 * h).wait_recv()
            q_three(h).wait_recv()
            q_local_wait(h)
            collect(2 * h)

        c = lax.rem(y + order(j), NHEAD)
        for g in range(GRP):
            turned[:, g * TOK:(g + 1) * TOK] = qbuf[h, c, :, g * DH:(g + 1) * DH].T
        valid, _ = picks(h)
        top = None
        for t in range(TOPK + 1):
            high = jnp.full((8, GRP * TOK), NEG, jnp.float32)
            for i in range(BLK // TOK):
                s = jnp.dot(blocks[0, t, i * TOK:(i + 1) * TOK], turned[...], preferred_element_type=jnp.float32)
                if t == 0:
                    seen = behind <= (c - i) * TOK
                    s = jnp.concatenate(
                        [jnp.where(seen, s[:, g * TOK:(g + 1) * TOK], NEG) for g in range(GRP)], axis=1)
                scores[t, i * TOK:(i + 1) * TOK] = s
                high = fold(jnp.maximum, high, s)
            high = jnp.max(high, axis=0, keepdims=True)
            top = high if t == 0 else jnp.maximum(top, jnp.where(valid[t], high, NEG))
        total = jnp.zeros((8, GRP * TOK), jnp.float32)
        for t in range(TOPK + 1):
            shift = top if t == 0 else jnp.where(valid[t], top, -NEG)

            def band(i, total):
                rows = pl.ds(pl.multiple_of(i * STRIP, STRIP), STRIP)
                p = jnp.exp2((scores[t, rows] - shift) * RATE)
                weights[c, pl.ds(pl.multiple_of(t * BLK + i * STRIP, STRIP), STRIP)] = p.astype(jnp.bfloat16)
                return fold(jnp.add, total, p)

            total = lax.fori_loop(0, BLK // STRIP, band, total, unroll=4)
        totals[c] = jnp.broadcast_to(jnp.sum(total, axis=0, keepdims=True), (8, GRP * TOK))

    def attend(h, j):
        @pl.when(j == 0)
        def _():
            whole(2 * h + 1).wait_recv()
            collect(2 * h + 1)
            for t in range(TOPK + 1):
                flipped[:, t * BLK:(t + 1) * BLK] = blocks[1, t].T

        o = order(j)
        c = lax.rem(y + o, NHEAD)
        for side in range(2):
            q0 = side * 2 * TOK
            acc = jnp.dot(flipped[...], weights[c, :, q0:q0 + 2 * TOK], preferred_element_type=jnp.float32)
            res = acc / totals[c, 0:1, q0:q0 + 2 * TOK]
            for g in range(2):
                obuf[h, c, :, q0 + g * DH:q0 + (g + 1) * DH] = res[:, g * TOK:(g + 1) * TOK].T.astype(jnp.bfloat16)
        for k in (1, 3):
            pl.when(o == k)(lambda: out_copy(k, h).start())

        @pl.when(o == 2)
        def _():
            for k in range(2):
                out_via(h, k).start()

        pl.when(o == 0)(lambda: out_local(h).start())

    def before(n):
        return sum((n + 63 - tick) // 64 for tick in ITEM_TICKS)

    def item(k, _):
        h, kind, j = k // 8, lax.rem(k // 4, 2), lax.rem(k, 4)
        pl.when(kind == 0)(lambda: weigh(h, j))
        pl.when(kind == 1)(lambda: attend(h, j))
        pl.when((k == 9) | (k == 14))(lambda: out_pass(k // 14))
        return 0

    def tick(n, _):
        step(n)
        pl.when((n == 1) | (n == 2))(lambda: send_q(n // 2))
        pl.when((n == 4) | (n == 6))(lambda: q_pass(n // 6))
        lax.fori_loop(before(n), before(n + 1), item, 0)
        return 0

    lax.fori_loop(0, TICKS, tick, 0)

    def sent(g, m):
        for xx in range(NX):
            for low, high in ((0, 1), (1, 2), (2, nz - 1), (nz - 1, nz)):
                count = 0
                for entry in ROUTES[xx]:
                    if len(entry) > 2 and low * NX + xx >= entry[2] and (entry[1] != "Z" or low < nz - 1):
                        count += len(entry) == 4 or entry[4] <= m < entry[5]
                if count == 0:
                    continue

                @pl.when((x == xx) & (z >= low) & (z < high))
                def _():
                    ref = kv.at[g, pl.ds(0, count)]
                    remote(ref, ref, win_send.at[g], sib_recv.at[g], right).wait_send()

    def finish(g, _):
        whole(g).wait_send()
        pl.when(g < GROUPS - 1)(lambda: sent(g, 0))
        pl.when(g == GROUPS - 1)(lambda: sent(g, PIECES - 1))
        return 0

    lax.fori_loop(0, GROUPS, finish, 0)
    for h in range(HLOC):
        kv_three(h).wait_send()
        three(q_relay.at[h], q_relay_send.at[h], q_recv.at[h]).wait_send()
        three(out_relay_buf.at[h], relay_send.at[h], out_recv.at[h]).wait_send()
        q_three(h).wait_send()
        out_three(h).wait()
        out_local(h).wait()


def on_device(query, keys, values, chosen):
    nseq = lax.axis_size("seq")
    dma = pltpu.SemaphoreType.DMA
    any_spec = pl.BlockSpec(memory_space=pl.ANY)

    def body(*refs):
        kernel(nseq, *refs)

    return pl.pallas_call(
        body,
        out_shape=pltpu.VMEM(query.shape, jnp.bfloat16),
        in_specs=[pl.BlockSpec(memory_space=pltpu.SMEM), any_spec, any_spec, any_spec],
        out_specs=pl.BlockSpec(memory_space=pltpu.VMEM),
        scratch_shapes=[
            pltpu.VMEM((GROUPS, SLOTS, BLK, DH), jnp.bfloat16),
            pltpu.VMEM((2, TOPK + 1, BLK, DH), jnp.bfloat16),
            pltpu.VMEM((HLOC, NHEAD, TOK, WIDE), jnp.bfloat16),
            pltpu.VMEM((HLOC, NHEAD, TOK, WIDE), jnp.bfloat16),
            pltpu.VMEM((TOPK + 1, BLK, GRP * TOK), jnp.float32),
            pltpu.VMEM((NHEAD, (TOPK + 1) * BLK, GRP * TOK), jnp.bfloat16),
            pltpu.VMEM((NHEAD, 8, GRP * TOK), jnp.float32),
            pltpu.VMEM((DH, (TOPK + 1) * BLK), jnp.bfloat16),
            pltpu.VMEM((DH, GRP * TOK), jnp.bfloat16),
            pltpu.VMEM((TOK, HK * DH), jnp.bfloat16),
            pltpu.VMEM((TOK, HK * DH), jnp.bfloat16),
            pltpu.VMEM((TOK, HQ * DH), jnp.bfloat16),
            pltpu.VMEM((HK, 2, TOK, DH), jnp.bfloat16),
            pltpu.VMEM((HLOC, 2, TOK // 2, WIDE), jnp.bfloat16),
            pltpu.VMEM((HLOC, 2, TOK // 2, WIDE), jnp.bfloat16),
            dma((HLOC,)), dma((HLOC,)),
            dma((HLOC,)), dma((HLOC,)),
            dma((GROUPS,)), dma((PIECES, 6)),
            dma((GROUPS,)), dma((GROUPS,)),
            dma((HLOC,)), dma((HLOC,)),
            dma((HLOC, 2)), dma((HLOC,)),
            dma((HLOC, 2)), dma((HLOC,)),
            dma((GROUPS + 2 * HLOC,)),
        ],
        compiler_params=pltpu.CompilerParams(
            collective_id=0, has_side_effects=True, vmem_limit_bytes=56 * 1024 * 1024),
        cost_estimate=pl.CostEstimate(
            flops=4 * BLK * HLOC * GRP * BLK * 4 * DH, bytes_accessed=4 * 1024 * 1024,
            transcendentals=HLOC * GRP * BLK * BLK * 4),
        name="window_attention",
    )(chosen, query, keys, values)


def solution(mesh):
    in_specs = (
        P(("seq", "head"), None),
        P(("seq", "head"), None),
        P(("seq", "head"), None),
        P("seq", "head", None),
    )
    return jax.shard_map(
        on_device, mesh=mesh, in_specs=in_specs, out_specs=P(("seq", "head"), None), check_vma=False
    )
```

```python
import math

import jax
import jax.numpy as jnp
from jax import lax
from jax.experimental import pallas as pl
from jax.experimental.pallas import tpu as pltpu
from jax.sharding import PartitionSpec as P

HQ = 32
HK = 8
DH = 128
BLK = 512
TOPK = 3
GRP = HQ // HK
NHEAD = 4
HLOC = HK // NHEAD
TOK = BLK // NHEAD
NX = 4
SLOTS = 13
GROUPS = 2 * HLOC
PARTS = 2
PIECES = GROUPS * PARTS
ROWS = BLK // PARTS
WIDE = GRP * DH
STRIP = 32
NEG = -1e30
RATE = math.log2(math.e) / math.sqrt(DH)
MESH = pl.DeviceIdType.MESH

ROUTES = {
    0: [
        (0, 0), (0, "Z", 0, 4), (0, "P", 0, 1), (0, "M", 0, 3), (2, 4),
        (2, "P", 4, 5), (4, 1), (4, "Z", 1, 5, 6, 8), (4, 3), (4, "M", 3, 6), (6, 2),
        (6, "Z", 2, 6), (9, 6), (10, 5),
    ],
    1: [
        (0, 0), (0, "Z", 0, 4), (0, "P", 0, 1), (2, 4), (2, "M", 4, 3),
        (2, "P", 4, 5), (2, 1), (4, 3), (4, 5), (6, 2),
        (6, "Z", 2, 6), (8, 6), (8, "M", 6, 5, 0, 6),
    ],
    2: [
        (0, 0), (0, "Z", 0, 4), (0, "P", 0, 1), (2, 4), (2, "M", 4, 3),
        (2, 1), (2, "P", 1, 2), (4, 3), (4, "M", 3, 2), (4, 2),
        (4, "Z", 2, 6), (4, 5), (6, 6),
    ],
    3: [
        (0, 0), (0, "Z", 0, 4), (2, 4), (2, "P", 4, 1), (2, "M", 4, 3),
        (2, 3), (2, "M", 3, 2), (2, 1), (2, "Z", 1, 5), (4, 5),
        (4, "P", 5, 2), (4, 2), (5, 6),
    ],
}
TICKS = 18
ITEM_TICKS = (12, 12, 13, 14, 14, 14, 15, 16, 16, 16, 17, 17, 17, 17, 17, 17)


def kernel(nseq, chosen, query, keys, values, out, kv, blocks, qbuf, obuf, scores, weights, totals, flipped, turned,
           give, got, mine, theirs, asked, ask_send, ask_recv,
           own_send, own_recv, q_send, q_recv, win_send, win_recv, sib_send, sib_recv,
           out_send, out_recv, local_sem):
    nz = nseq // (2 * NX)
    seq = lax.axis_index("seq")
    y = lax.axis_index("head")
    core = lax.rem(seq, 2)
    x = lax.rem(seq // 2, NX)
    z = seq // (2 * NX)

    def at(zz, xx):
        return ((zz * NX + xx) * 2 + core, y)

    up = at(lax.rem(z + 1, nz), x)
    down = at(lax.rem(z + nz - 1, nz), x)
    right = at(z, lax.rem(x + 1, NX))
    left = at(z, lax.rem(x + NX - 1, NX))
    sibling = (seq + 1 - 2 * core, y)

    def partner(o):
        return (seq, lax.rem(y + o, NHEAD))

    place = z * NX + x
    barrier = pltpu.get_barrier_semaphore()

    def greet(who):
        pl.semaphore_signal(barrier, inc=1, device_id=who, device_id_type=MESH)

    for who in [right, left, sibling, partner(1), partner(2), partner(3)]:
        greet(who)
    pl.when(z < nz - 1)(lambda: greet(up))
    pl.when(z > 0)(lambda: greet(down))
    edge = (z == 0) | (z == nz - 1)
    pl.when(edge)(lambda: pl.semaphore_wait(barrier, 7))
    pl.when(jnp.logical_not(edge))(lambda: pl.semaphore_wait(barrier, 8))

    def columns(start, width):
        return pl.ds(pl.multiple_of(start, DH), width)

    def remote(src, dst, send, recv, to):
        return pltpu.make_async_remote_copy(
            src_ref=src, dst_ref=dst, send_sem=send, recv_sem=recv, device_id=to, device_id_type=MESH)

    own_rows = pl.ds(pl.multiple_of(y * TOK, TOK), TOK)

    def kv_source(h, i, to_y):
        return (keys, values)[i].at[:, columns((to_y * HLOC + h) * DH, DH)]

    def kv_copy(o, h, i):
        to, g = partner(o), 2 * h + i
        return remote(kv_source(h, i, to[1]), kv.at[g, 0, own_rows], own_send.at[g], own_recv.at[g], to)

    def kv_local(h, i):
        return pltpu.make_async_copy(kv_source(h, i, y), kv.at[2 * h + i, 0, own_rows], local_sem.at[2 * h + i])

    def q_source(h, to_y):
        return query.at[:, columns((to_y * HLOC + h) * WIDE, WIDE)]

    def q_copy(o, h):
        to = partner(o)
        return remote(q_source(h, to[1]), qbuf.at[h, y], q_send.at[h], q_recv.at[h], to)

    def q_local(h):
        return pltpu.make_async_copy(q_source(h, y), qbuf.at[h, y], local_sem.at[GROUPS + h])

    def q_local_wait(h):
        pltpu.make_async_copy(qbuf.at[h, 0], qbuf.at[h, 0], local_sem.at[GROUPS + h]).wait()

    def out_place(to_y, h):
        return out.at[:, columns((to_y * HLOC + h) * WIDE, WIDE)]

    def out_copy(o, h):
        to = partner(o)
        return remote(obuf.at[h, to[1]], out_place(y, h), out_send.at[h], out_recv.at[h], to)

    def out_local(h):
        return pltpu.make_async_copy(obuf.at[h, y], out_place(y, h), local_sem.at[GROUPS + HLOC + h])

    def three(ref, send, recv):
        return remote(ref, ref, send, recv, sibling)

    def kv_three(g):
        return three(kv.at[g, 0, pl.ds(0, 3 * TOK)], own_send.at[g], own_recv.at[g])

    def kv_local_wait(g):
        ref = kv.at[g, 0, pl.ds(0, TOK)]
        pltpu.make_async_copy(ref, ref, local_sem.at[g]).wait()

    def q_three(h):
        return three(qbuf.at[h, pl.ds(0, 3)], q_send.at[h], q_recv.at[h])

    def out_three(h):
        return three(obuf.at[h, pl.ds(0, 3)], out_send.at[h], out_recv.at[h])

    def send_q(h):
        for o in (2, 1, 3):
            q_copy(o, h).start()
        q_local(h).start()

    def piece(m, slot):
        return kv.at[m // PARTS, slot, pl.ds(pl.multiple_of(lax.rem(m, PARTS) * ROWS, ROWS), ROWS)]

    def forward(m, to, r, into):
        remote(piece(m, 2 * r), piece(m, 2 * into),
               win_send.at[m // PARTS], win_recv.at[m, into - 1], to).start()

    def arrived(m, r):
        remote(piece(m, 2 * r), piece(m, 2 * r), win_send.at[m // PARTS], win_recv.at[m, r - 1], up).wait_recv()

    def own(m):
        @pl.when(lax.rem(m, PARTS) == 0)
        def _():
            kv_three(m // PARTS).wait_recv()
            kv_local_wait(m // PARTS)

    def event(m, entry):
        if len(entry) > 2:
            there = place >= entry[2]
            if entry[1] == "Z":
                there = there & (z < nz - 1)
            if len(entry) > 4:
                there = there & (m >= entry[4]) & (m < entry[5])
            to = {"Z": up, "P": right, "M": left}[entry[1]]
            pl.when(there)(lambda: forward(m, to, entry[2], entry[3]))
        else:
            if entry[1] == 0:
                own(m)
            else:
                pl.when(place >= entry[1])(lambda: arrived(m, entry[1]))

    def step(n):
        for xx in range(NX):
            @pl.when(x == xx)
            def _():
                for lag in sorted({entry[0] for entry in ROUTES[xx]}):
                    m = n - lag

                    @pl.when((m >= 0) & (m < PIECES))
                    def _():
                        for entry in ROUTES[xx]:
                            if entry[0] == lag:
                                event(m, entry)

    def send_kv(h, _):
        for i in range(2):
            for o in (2, 1, 3):
                kv_copy(o, h, i).start()
            kv_local(h, i).start()
        return 0

    lax.fori_loop(0, HLOC, send_kv, 0)

    row = lax.broadcasted_iota(jnp.int32, (8, DH), 0)
    listed = jnp.zeros((8, DH), jnp.int32)
    for h in range(HLOC):
        for t in range(TOPK):
            listed = jnp.where(row == h * TOPK + t, chosen[0, h, t], listed)
    mine[...] = listed
    ask = remote(mine, theirs, ask_send.at[0], ask_recv.at[0], sibling)
    ask.start()
    ask.wait()
    read = pltpu.make_async_copy(theirs, asked, local_sem.at[GROUPS + 2 * HLOC])
    read.start()
    read.wait()

    def exchange(g):
        return remote(give.at[g], got.at[g], sib_send.at[g], sib_recv.at[g], sibling)

    def picks(h):
        return [None] + [chosen[0, h, t] >= 0 for t in range(TOPK)]

    def choose(g, named, rows, found):
        for r in range(SLOTS // 2 + 1):
            block = kv[g, 2 * r, rows]
            for t in range(TOPK):
                found[t] = jnp.where(named[t] == seq - 2 * r, block, found[t])
        return found

    def known(index):
        return jnp.where(index >= 0, index, -64)

    def part_rows(i):
        return pl.ds(pl.multiple_of(i * DH, DH), DH)

    def offer(g):
        named = [known(asked[(g // 2) * TOPK + t, 0]) for t in range(TOPK)]

        def part(i, _):
            rows = part_rows(i)
            found = choose(g, named, rows, [kv[g, 0, rows]] * TOPK)
            for t in range(TOPK):
                give[g, t, rows] = found[t]
            return 0

        lax.fori_loop(0, BLK // DH, part, 0)
        exchange(g).start()

    def collect(g):
        exchange(g).wait_recv()
        named = [known(chosen[0, g // 2, t]) for t in range(TOPK)]
        away = [(chosen[0, g // 2, t] >= 0) & (lax.rem(seq - named[t], 2) == 1) for t in range(TOPK)]

        def part(i, _):
            rows = part_rows(i)
            block = kv[g, 0, rows]
            blocks[g % 2, 0, rows] = block
            found = choose(g, named, rows, [block] * TOPK)
            for t in range(TOPK):
                blocks[g % 2, t + 1, rows] = jnp.where(away[t], got[g, t, rows], found[t])
            return 0

        lax.fori_loop(0, BLK // DH, part, 0)

    behind = (lax.broadcasted_iota(jnp.int32, (TOK, TOK), 0)
              - lax.broadcasted_iota(jnp.int32, (TOK, TOK), 1))

    def fold(op, start, rows):
        for i in range(0, rows.shape[0], 8):
            start = op(start, rows[i:i + 8])
        return start

    def weigh(h, j):
        @pl.when(j == 0)
        def _():
            q_three(h).wait_recv()
            q_local_wait(h)
            collect(2 * h)

        c = lax.rem(y + j + 1, NHEAD)
        for g in range(GRP):
            turned[:, g * TOK:(g + 1) * TOK] = qbuf[h, c, :, g * DH:(g + 1) * DH].T
        valid = picks(h)
        top = None
        for t in range(TOPK + 1):
            high = jnp.full((8, GRP * TOK), NEG, jnp.float32)
            for i in range(BLK // TOK):
                s = jnp.dot(blocks[0, t, i * TOK:(i + 1) * TOK], turned[...], preferred_element_type=jnp.float32)
                if t == 0:
                    seen = behind <= (c - i) * TOK
                    s = jnp.concatenate(
                        [jnp.where(seen, s[:, g * TOK:(g + 1) * TOK], NEG) for g in range(GRP)], axis=1)
                scores[t, i * TOK:(i + 1) * TOK] = s
                high = fold(jnp.maximum, high, s)
            high = jnp.max(high, axis=0, keepdims=True)
            top = high if t == 0 else jnp.maximum(top, jnp.where(valid[t], high, NEG))
        total = jnp.zeros((8, GRP * TOK), jnp.float32)
        for t in range(TOPK + 1):
            shift = top if t == 0 else jnp.where(valid[t], top, -NEG)

            def band(i, total):
                rows = pl.ds(pl.multiple_of(i * STRIP, STRIP), STRIP)
                p = jnp.exp2((scores[t, rows] - shift) * RATE)
                weights[c, pl.ds(pl.multiple_of(t * BLK + i * STRIP, STRIP), STRIP)] = p.astype(jnp.bfloat16)
                return fold(jnp.add, total, p)

            total = lax.fori_loop(0, BLK // STRIP, band, total, unroll=4)
        totals[c] = jnp.broadcast_to(jnp.sum(total, axis=0, keepdims=True), (8, GRP * TOK))

    def attend(h, j):
        @pl.when(j == 0)
        def _():
            collect(2 * h + 1)
            for t in range(TOPK + 1):
                flipped[:, t * BLK:(t + 1) * BLK] = blocks[1, t].T

        o = lax.rem(j + 1, NHEAD)
        c = lax.rem(y + o, NHEAD)
        for side in range(2):
            q0 = side * 2 * TOK
            acc = jnp.dot(flipped[...], weights[c, :, q0:q0 + 2 * TOK], preferred_element_type=jnp.float32)
            res = acc / totals[c, 0:1, q0:q0 + 2 * TOK]
            for g in range(2):
                obuf[h, c, :, q0 + g * DH:q0 + (g + 1) * DH] = res[:, g * TOK:(g + 1) * TOK].T.astype(jnp.bfloat16)
        for k in (1, 2, 3):
            pl.when(o == k)(lambda: out_copy(k, h).start())
        pl.when(o == 0)(lambda: out_local(h).start())

    def before(n):
        return sum((n + 63 - tick) // 64 for tick in ITEM_TICKS)

    def item(k, _):
        h, kind, j = k // 8, lax.rem(k // 4, 2), lax.rem(k, 4)
        pl.when(kind == 0)(lambda: weigh(h, j))
        pl.when(kind == 1)(lambda: attend(h, j))
        return 0

    def tick(n, _):
        step(n)
        last = n - (10 - 2 * x + x // 3)
        pl.when((last >= 0) & (last < PIECES) & (lax.rem(last, PARTS) == PARTS - 1))(lambda: offer(last // PARTS))
        pl.when((n == 3) | (n == 6))(lambda: send_q(n // 6))
        lax.fori_loop(before(n), before(n + 1), item, 0)
        return 0

    lax.fori_loop(0, TICKS, tick, 0)

    def sent(g, m):
        for xx in range(NX):
            for low, high in ((0, 1), (1, 2), (2, nz - 1), (nz - 1, nz)):
                count = 0
                for entry in ROUTES[xx]:
                    if len(entry) > 2 and low * NX + xx >= entry[2] and (entry[1] != "Z" or low < nz - 1):
                        count += len(entry) == 4 or entry[4] <= m < entry[5]
                if count == 0:
                    continue

                @pl.when((x == xx) & (z >= low) & (z < high))
                def _():
                    ref = kv.at[g, pl.ds(0, count)]
                    remote(ref, ref, win_send.at[g], sib_recv.at[g], right).wait_send()

    def finish(g, _):
        kv_three(g).wait_send()
        exchange(g).wait_send()
        pl.when(g < GROUPS - 1)(lambda: sent(g, 0))
        pl.when(g == GROUPS - 1)(lambda: sent(g, PIECES - 1))
        return 0

    lax.fori_loop(0, GROUPS, finish, 0)
    for h in range(HLOC):
        q_three(h).wait_send()
        out_three(h).wait()
        out_local(h).wait()


def on_device(query, keys, values, chosen):
    nseq = lax.axis_size("seq")
    dma = pltpu.SemaphoreType.DMA
    any_spec = pl.BlockSpec(memory_space=pl.ANY)

    def body(*refs):
        kernel(nseq, *refs)

    return pl.pallas_call(
        body,
        out_shape=pltpu.VMEM(query.shape, jnp.bfloat16),
        in_specs=[pl.BlockSpec(memory_space=pltpu.SMEM), any_spec, any_spec, any_spec],
        out_specs=pl.BlockSpec(memory_space=pltpu.VMEM),
        scratch_shapes=[
            pltpu.VMEM((GROUPS, SLOTS, BLK, DH), jnp.bfloat16),
            pltpu.VMEM((2, TOPK + 1, BLK, DH), jnp.bfloat16),
            pltpu.VMEM((HLOC, NHEAD, TOK, WIDE), jnp.bfloat16),
            pltpu.VMEM((HLOC, NHEAD, TOK, WIDE), jnp.bfloat16),
            pltpu.VMEM((TOPK + 1, BLK, GRP * TOK), jnp.float32),
            pltpu.VMEM((NHEAD, (TOPK + 1) * BLK, GRP * TOK), jnp.bfloat16),
            pltpu.VMEM((NHEAD, 8, GRP * TOK), jnp.float32),
            pltpu.VMEM((DH, (TOPK + 1) * BLK), jnp.bfloat16),
            pltpu.VMEM((DH, GRP * TOK), jnp.bfloat16),
            pltpu.VMEM((GROUPS, TOPK, BLK, DH), jnp.bfloat16),
            pltpu.VMEM((GROUPS, TOPK, BLK, DH), jnp.bfloat16),
            pltpu.VMEM((8, DH), jnp.int32),
            pltpu.VMEM((8, DH), jnp.int32),
            pltpu.SMEM((8, DH), jnp.int32),
            dma((1,)), dma((1,)),
            dma((GROUPS,)), dma((GROUPS,)),
            dma((HLOC,)), dma((HLOC,)),
            dma((GROUPS,)), dma((PIECES, 6)),
            dma((GROUPS,)), dma((GROUPS,)),
            dma((HLOC,)), dma((HLOC,)),
            dma((GROUPS + 2 * HLOC + 1,)),
        ],
        compiler_params=pltpu.CompilerParams(
            collective_id=0, has_side_effects=True, vmem_limit_bytes=56 * 1024 * 1024),
        cost_estimate=pl.CostEstimate(
            flops=4 * BLK * HLOC * GRP * BLK * 4 * DH, bytes_accessed=4 * 1024 * 1024,
            transcendentals=HLOC * GRP * BLK * BLK * 4),
        name="window_attention",
    )(chosen, query, keys, values)


def solution(mesh):
    in_specs = (
        P(("seq", "head"), None),
        P(("seq", "head"), None),
        P(("seq", "head"), None),
        P("seq", "head", None),
    )
    return jax.shard_map(
        on_device, mesh=mesh, in_specs=in_specs, out_specs=P(("seq", "head"), None), check_vma=False
    )
```

```python
import math

import jax
import jax.numpy as jnp
from jax import lax
from jax.experimental import pallas as pl
from jax.experimental.pallas import tpu as pltpu
from jax.sharding import PartitionSpec as P

HQ = 32
HK = 8
DH = 128
BLK = 512
TOPK = 3
GRP = HQ // HK
NHEAD = 4
HLOC = HK // NHEAD
TOK = BLK // NHEAD
NX = 4
SLOTS = 13
GROUPS = 2 * HLOC
PARTS = 2
PIECES = GROUPS * PARTS
ROWS = BLK // PARTS
WIDE = GRP * DH
STRIP = 32
NEG = -1e30
RATE = 1.0 / math.sqrt(DH)
MESH = pl.DeviceIdType.MESH

ROUTES = {
    0: [
        (0, 0), (0, "Z", 0, 4), (0, "P", 0, 1), (0, "M", 0, 3), (2, 4),
        (2, "P", 4, 5), (4, 1), (4, "Z", 1, 5), (4, 3), (4, "M", 3, 6),
        (6, 2), (6, "Z", 2, 6), (6, 5), (8, 6),
    ],
    1: [
        (0, 0), (0, "Z", 0, 4), (0, "P", 0, 1), (2, 4), (2, "M", 4, 3),
        (2, "P", 4, 5), (2, 1), (4, 3), (4, 5), (6, 2),
        (6, "Z", 2, 6), (8, 6),
    ],
    2: [
        (0, 0), (0, "Z", 0, 4), (0, "P", 0, 1), (2, 4), (2, "M", 4, 3),
        (2, 1), (2, "P", 1, 2), (4, 3), (4, "M", 3, 2), (4, 2),
        (4, "Z", 2, 6), (4, 5), (6, 6),
    ],
    3: [
        (0, 0), (0, "Z", 0, 4), (2, 4), (2, "P", 4, 1), (2, "M", 4, 3),
        (2, 3), (2, "M", 3, 2), (2, 1), (2, "Z", 1, 5), (4, 5),
        (4, "P", 5, 2), (4, 2), (5, 6),
    ],
}
TICKS = 16
ITEM_TICKS = (10, 10, 11, 12, 12, 12, 13, 14, 14, 14, 15, 15, 15, 15, 15, 15)


def kernel(nseq, chosen, query, keys, values, out, kv, blocks, qbuf, obuf, scores, weights, totals, flipped, turned,
           own_send, own_recv, q_send, q_recv, win_send, win_recv, sib_send, sib_recv,
           out_send, out_recv, local_sem):
    nz = nseq // (2 * NX)
    seq = lax.axis_index("seq")
    y = lax.axis_index("head")
    core = lax.rem(seq, 2)
    x = lax.rem(seq // 2, NX)
    z = seq // (2 * NX)

    def at(zz, xx):
        return ((zz * NX + xx) * 2 + core, y)

    up = at(lax.rem(z + 1, nz), x)
    down = at(lax.rem(z + nz - 1, nz), x)
    right = at(z, lax.rem(x + 1, NX))
    left = at(z, lax.rem(x + NX - 1, NX))
    sibling = (seq + 1 - 2 * core, y)

    def partner(o):
        return (seq, lax.rem(y + o, NHEAD))

    place = z * NX + x
    barrier = pltpu.get_barrier_semaphore()

    def greet(who):
        pl.semaphore_signal(barrier, inc=1, device_id=who, device_id_type=MESH)

    for who in [right, left, sibling, partner(1), partner(2), partner(3)]:
        greet(who)
    pl.when(z < nz - 1)(lambda: greet(up))
    pl.when(z > 0)(lambda: greet(down))
    edge = (z == 0) | (z == nz - 1)
    pl.when(edge)(lambda: pl.semaphore_wait(barrier, 7))
    pl.when(jnp.logical_not(edge))(lambda: pl.semaphore_wait(barrier, 8))

    def columns(start, width):
        return pl.ds(pl.multiple_of(start, DH), width)

    def remote(src, dst, send, recv, to):
        return pltpu.make_async_remote_copy(
            src_ref=src, dst_ref=dst, send_sem=send, recv_sem=recv, device_id=to, device_id_type=MESH)

    own_rows = pl.ds(pl.multiple_of(y * TOK, TOK), TOK)

    def kv_source(h, i, to_y):
        return (keys, values)[i].at[:, columns((to_y * HLOC + h) * DH, DH)]

    def kv_copy(o, h, i):
        to, g = partner(o), 2 * h + i
        return remote(kv_source(h, i, to[1]), kv.at[g, 0, own_rows], own_send.at[g], own_recv.at[g], to)

    def kv_local(h, i):
        return pltpu.make_async_copy(kv_source(h, i, y), kv.at[2 * h + i, 0, own_rows], local_sem.at[2 * h + i])

    def q_source(h, to_y):
        return query.at[:, columns((to_y * HLOC + h) * WIDE, WIDE)]

    def q_copy(o, h):
        to = partner(o)
        return remote(q_source(h, to[1]), qbuf.at[h, y], q_send.at[h], q_recv.at[h], to)

    def q_local(h):
        return pltpu.make_async_copy(q_source(h, y), qbuf.at[h, y], local_sem.at[GROUPS + h])

    def q_local_wait(h):
        pltpu.make_async_copy(qbuf.at[h, 0], qbuf.at[h, 0], local_sem.at[GROUPS + h]).wait()

    def out_place(to_y, h):
        return out.at[:, columns((to_y * HLOC + h) * WIDE, WIDE)]

    def out_copy(o, h):
        to = partner(o)
        return remote(obuf.at[h, to[1]], out_place(y, h), out_send.at[h], out_recv.at[h], to)

    def out_local(h):
        return pltpu.make_async_copy(obuf.at[h, y], out_place(y, h), local_sem.at[GROUPS + HLOC + h])

    def three(ref, send, recv):
        return remote(ref, ref, send, recv, sibling)

    def kv_three(g):
        return three(kv.at[g, 0, pl.ds(0, 3 * TOK)], own_send.at[g], own_recv.at[g])

    def kv_local_wait(g):
        ref = kv.at[g, 0, pl.ds(0, TOK)]
        pltpu.make_async_copy(ref, ref, local_sem.at[g]).wait()

    def q_three(h):
        return three(qbuf.at[h, pl.ds(0, 3)], q_send.at[h], q_recv.at[h])

    def out_three(h):
        return three(obuf.at[h, pl.ds(0, 3)], out_send.at[h], out_recv.at[h])

    def send_q(h):
        for o in (2, 1, 3):
            q_copy(o, h).start()
        q_local(h).start()

    def piece(m, slot):
        return kv.at[m // PARTS, slot, pl.ds(pl.multiple_of(lax.rem(m, PARTS) * ROWS, ROWS), ROWS)]

    def forward(m, to, r, into):
        remote(piece(m, 2 * r), piece(m, 2 * into),
               win_send.at[m // PARTS], win_recv.at[m, into - 1], to).start()

    def arrived(m, r):
        remote(piece(m, 2 * r), piece(m, 2 * r), win_send.at[m // PARTS], win_recv.at[m, r - 1], up).wait_recv()

    def share(m, r):
        g = m // PARTS

        def go():
            remote(kv.at[g, 2 * r], kv.at[g, 2 * r + 1 - 2 * core], sib_send.at[g], sib_recv.at[g], sibling).start()

        whole_slot = lax.rem(m, PARTS) == PARTS - 1
        if r == 0:
            whole_slot = whole_slot & (core == 0)
        elif r == 6:
            whole_slot = whole_slot & (core == 1)
        pl.when(whole_slot)(go)

    def own(m):
        @pl.when(lax.rem(m, PARTS) == 0)
        def _():
            kv_three(m // PARTS).wait_recv()
            kv_local_wait(m // PARTS)

    def event(m, entry):
        if len(entry) > 2:
            there = place >= entry[2]
            if entry[1] == "Z":
                there = there & (z < nz - 1)
            to = {"Z": up, "P": right, "M": left}[entry[1]]
            pl.when(there)(lambda: forward(m, to, entry[2], entry[3]))
        else:
            if entry[1] == 0:
                own(m)
            else:
                pl.when(place >= entry[1])(lambda: arrived(m, entry[1]))
            share(m, entry[1])

    def step(n):
        for xx in range(NX):
            @pl.when(x == xx)
            def _():
                for lag in sorted({entry[0] for entry in ROUTES[xx]}):
                    m = n - lag

                    @pl.when((m >= 0) & (m < PIECES))
                    def _():
                        for entry in ROUTES[xx]:
                            if entry[0] == lag:
                                event(m, entry)

    def send_kv(h, _):
        for i in range(2):
            for o in (2, 1, 3):
                kv_copy(o, h, i).start()
            kv_local(h, i).start()
        return 0

    lax.fori_loop(0, HLOC, send_kv, 0)

    def whole(g, slots=6):
        ref = kv.at[g, pl.ds(0, slots)]
        return remote(ref, ref, sib_send.at[g], sib_recv.at[g], sibling)

    def picks(h):
        valid, slot = [None], [0]
        for t in range(TOPK):
            pick = chosen[0, h, t]
            valid.append(pick >= 0)
            slot.append(seq - pick)
        return valid, slot

    def collect(g):
        _, slot = picks(g // 2)

        def part(i, _):
            rows = pl.ds(pl.multiple_of(i * DH, DH), DH)
            block = kv[g, 0, rows]
            blocks[g % 2, 0, rows] = block
            found = [block] * TOPK
            for d in range(1, SLOTS):
                block = kv[g, d, rows]
                for t in range(TOPK):
                    found[t] = jnp.where(slot[t + 1] == d, block, found[t])
            for t in range(TOPK):
                blocks[g % 2, t + 1, rows] = found[t]
            return 0

        lax.fori_loop(0, BLK // DH, part, 0)

    behind = (lax.broadcasted_iota(jnp.int32, (TOK, TOK), 0)
              - lax.broadcasted_iota(jnp.int32, (TOK, TOK), 1))

    def fold(op, start, rows):
        for i in range(0, rows.shape[0], 8):
            start = op(start, rows[i:i + 8])
        return start

    def weigh(h, j):
        @pl.when(j == 0)
        def _():
            whole(2 * h).wait_recv()
            q_three(h).wait_recv()
            q_local_wait(h)
            collect(2 * h)

        c = lax.rem(y + j + 1, NHEAD)
        for g in range(GRP):
            turned[:, g * TOK:(g + 1) * TOK] = qbuf[h, c, :, g * DH:(g + 1) * DH].T
        valid, _ = picks(h)
        top = None
        for t in range(TOPK + 1):
            high = jnp.full((8, GRP * TOK), NEG, jnp.float32)
            for i in range(BLK // TOK):
                s = jnp.dot(blocks[0, t, i * TOK:(i + 1) * TOK], turned[...], preferred_element_type=jnp.float32)
                if t == 0:
                    seen = behind <= (c - i) * TOK
                    s = jnp.concatenate(
                        [jnp.where(seen, s[:, g * TOK:(g + 1) * TOK], NEG) for g in range(GRP)], axis=1)
                scores[t, i * TOK:(i + 1) * TOK] = s
                high = fold(jnp.maximum, high, s)
            high = jnp.max(high, axis=0, keepdims=True)
            top = high if t == 0 else jnp.maximum(top, jnp.where(valid[t], high, NEG))
        total = jnp.zeros((8, GRP * TOK), jnp.float32)
        for t in range(TOPK + 1):
            shift = top if t == 0 else jnp.where(valid[t], top, -NEG)

            def band(i, total):
                rows = pl.ds(pl.multiple_of(i * STRIP, STRIP), STRIP)
                p = jnp.exp((scores[t, rows] - shift) * RATE)
                weights[c, pl.ds(pl.multiple_of(t * BLK + i * STRIP, STRIP), STRIP)] = p.astype(jnp.bfloat16)
                return fold(jnp.add, total, p)

            total = lax.fori_loop(0, BLK // STRIP, band, total, unroll=4)
        totals[c] = jnp.broadcast_to(jnp.sum(total, axis=0, keepdims=True), (8, GRP * TOK))

    def attend(h, j):
        @pl.when(j == 0)
        def _():
            whole(2 * h + 1).wait_recv()
            collect(2 * h + 1)
            for t in range(TOPK + 1):
                flipped[:, t * BLK:(t + 1) * BLK] = blocks[1, t].T

        o = lax.rem(j + 1, NHEAD)
        c = lax.rem(y + o, NHEAD)
        for side in range(2):
            q0 = side * 2 * TOK
            acc = jnp.dot(flipped[...], weights[c, :, q0:q0 + 2 * TOK], preferred_element_type=jnp.float32)
            res = acc / totals[c, 0:1, q0:q0 + 2 * TOK]
            for g in range(2):
                obuf[h, c, :, q0 + g * DH:q0 + (g + 1) * DH] = res[:, g * TOK:(g + 1) * TOK].T.astype(jnp.bfloat16)
        for k in (1, 2, 3):
            pl.when(o == k)(lambda: out_copy(k, h).start())
        pl.when(o == 0)(lambda: out_local(h).start())

    def before(n):
        return sum((n + 63 - tick) // 64 for tick in ITEM_TICKS)

    def item(k, _):
        h, kind, j = k // 8, lax.rem(k // 4, 2), lax.rem(k, 4)
        pl.when(kind == 0)(lambda: weigh(h, j))
        pl.when(kind == 1)(lambda: attend(h, j))
        return 0

    def tick(n, _):
        step(n)
        pl.when((n == 3) | (n == 6))(lambda: send_q(n // 6))
        lax.fori_loop(before(n), before(n + 1), item, 0)
        return 0

    lax.fori_loop(0, TICKS, tick, 0)

    def sent(g):
        for xx in range(NX):
            for low, high in ((0, 1), (1, 2), (2, nz - 1), (nz - 1, nz)):
                count = 0
                for entry in ROUTES[xx]:
                    if len(entry) > 2 and low * NX + xx >= entry[2] and (entry[1] != "Z" or low < nz - 1):
                        count += 1
                if count == 0:
                    continue

                @pl.when((x == xx) & (z >= low) & (z < high))
                def _():
                    ref = kv.at[g, pl.ds(0, count)]
                    remote(ref, ref, win_send.at[g], sib_recv.at[g], right).wait_send()

    def finish(g, _):
        kv_three(g).wait_send()
        whole(g).wait_send()
        sent(g)
        return 0

    lax.fori_loop(0, GROUPS, finish, 0)
    for h in range(HLOC):
        q_three(h).wait_send()
        out_three(h).wait()
        out_local(h).wait()


def on_device(query, keys, values, chosen):
    nseq = lax.axis_size("seq")
    dma = pltpu.SemaphoreType.DMA
    any_spec = pl.BlockSpec(memory_space=pl.ANY)

    def body(*refs):
        kernel(nseq, *refs)

    return pl.pallas_call(
        body,
        out_shape=pltpu.VMEM(query.shape, jnp.bfloat16),
        in_specs=[pl.BlockSpec(memory_space=pltpu.SMEM), any_spec, any_spec, any_spec],
        out_specs=pl.BlockSpec(memory_space=pltpu.VMEM),
        scratch_shapes=[
            pltpu.VMEM((GROUPS, SLOTS, BLK, DH), jnp.bfloat16),
            pltpu.VMEM((2, TOPK + 1, BLK, DH), jnp.bfloat16),
            pltpu.VMEM((HLOC, NHEAD, TOK, WIDE), jnp.bfloat16),
            pltpu.VMEM((HLOC, NHEAD, TOK, WIDE), jnp.bfloat16),
            pltpu.VMEM((TOPK + 1, BLK, GRP * TOK), jnp.float32),
            pltpu.VMEM((NHEAD, (TOPK + 1) * BLK, GRP * TOK), jnp.bfloat16),
            pltpu.VMEM((NHEAD, 8, GRP * TOK), jnp.float32),
            pltpu.VMEM((DH, (TOPK + 1) * BLK), jnp.bfloat16),
            pltpu.VMEM((DH, GRP * TOK), jnp.bfloat16),
            dma((GROUPS,)), dma((GROUPS,)),
            dma((HLOC,)), dma((HLOC,)),
            dma((GROUPS,)), dma((PIECES, 6)),
            dma((GROUPS,)), dma((GROUPS,)),
            dma((HLOC,)), dma((HLOC,)),
            dma((GROUPS + 2 * HLOC,)),
        ],
        compiler_params=pltpu.CompilerParams(
            collective_id=0, has_side_effects=True, vmem_limit_bytes=56 * 1024 * 1024),
        cost_estimate=pl.CostEstimate(
            flops=4 * BLK * HLOC * GRP * BLK * 4 * DH, bytes_accessed=4 * 1024 * 1024,
            transcendentals=HLOC * GRP * BLK * BLK * 4),
        name="window_attention",
    )(chosen, query, keys, values)


def solution(mesh):
    in_specs = (
        P(("seq", "head"), None),
        P(("seq", "head"), None),
        P(("seq", "head"), None),
        P("seq", "head", None),
    )
    return jax.shard_map(
        on_device, mesh=mesh, in_specs=in_specs, out_specs=P(("seq", "head"), None), check_vma=False
    )
```

```python
import math

import jax
import jax.numpy as jnp
from jax import lax
from jax.experimental import pallas as pl
from jax.experimental.pallas import tpu as pltpu
from jax.sharding import PartitionSpec as P

HQ = 32
HK = 8
DH = 128
BLK = 512
TOPK = 3
GRP = HQ // HK
NHEAD = 4
HLOC = HK // NHEAD
TOK = BLK // NHEAD
NX = 4
SLOTS = 13
GROUPS = 2 * HLOC
PARTS = 2
PIECES = GROUPS * PARTS
ROWS = BLK // PARTS
WIDE = GRP * DH
STRIP = 32
NEG = -1e30
RATE = 1.0 / math.sqrt(DH)
MESH = pl.DeviceIdType.MESH

ROUTES = {
    0: [
        (0, 0), (0, "Z", 0, 4), (0, "P", 0, 1), (0, "M", 0, 3), (2, 4),
        (2, "P", 4, 5), (4, 1), (4, "Z", 1, 5), (4, 3), (4, "M", 3, 6),
        (6, 2), (6, "Z", 2, 6), (6, 5), (8, 6),
    ],
    1: [
        (0, 0), (0, "Z", 0, 4), (0, "P", 0, 1), (2, 4), (2, "M", 4, 3),
        (2, "P", 4, 5), (2, 1), (4, 3), (4, 5), (6, 2),
        (6, "Z", 2, 6), (8, 6),
    ],
    2: [
        (0, 0), (0, "Z", 0, 4), (0, "P", 0, 1), (2, 4), (2, "M", 4, 3),
        (2, 1), (2, "P", 1, 2), (4, 3), (4, "M", 3, 2), (4, 2),
        (4, "Z", 2, 6), (4, 5), (6, 6),
    ],
    3: [
        (0, 0), (0, "Z", 0, 4), (2, 4), (2, "P", 4, 1), (2, "M", 4, 3),
        (2, 3), (2, "M", 3, 2), (2, 1), (2, "Z", 1, 5), (4, 5),
        (4, "P", 5, 2), (4, 2), (5, 6),
    ],
}
TICKS = 16
ITEM_TICKS = (9, 10, 10, 11, 11, 12, 12, 12, 13, 13, 14, 15, 15, 15, 15, 15)


def kernel(nseq, chosen, query, keys, values, out, kv, blocks, qbuf, obuf, scores, weights, totals, flipped, turned, relay,
           own_send, own_recv, q_send, q_recv, win_send, win_recv, sib_send, sib_recv,
           out_send, out_recv, relay_recv, relay_send, local_sem):
    nz = nseq // (2 * NX)
    seq = lax.axis_index("seq")
    y = lax.axis_index("head")
    core = lax.rem(seq, 2)
    x = lax.rem(seq // 2, NX)
    z = seq // (2 * NX)

    def at(zz, xx):
        return ((zz * NX + xx) * 2 + core, y)

    up = at(lax.rem(z + 1, nz), x)
    down = at(lax.rem(z + nz - 1, nz), x)
    right = at(z, lax.rem(x + 1, NX))
    left = at(z, lax.rem(x + NX - 1, NX))
    sibling = (seq + 1 - 2 * core, y)

    def partner(o):
        return (seq, lax.rem(y + o, NHEAD))

    place = z * NX + x
    barrier = pltpu.get_barrier_semaphore()

    def greet(who):
        pl.semaphore_signal(barrier, inc=1, device_id=who, device_id_type=MESH)

    for who in [right, left, sibling, partner(1), partner(2), partner(3)]:
        greet(who)
    pl.when(z < nz - 1)(lambda: greet(up))
    pl.when(z > 0)(lambda: greet(down))
    edge = (z == 0) | (z == nz - 1)
    pl.when(edge)(lambda: pl.semaphore_wait(barrier, 7))
    pl.when(jnp.logical_not(edge))(lambda: pl.semaphore_wait(barrier, 8))

    def columns(start, width):
        return pl.ds(pl.multiple_of(start, DH), width)

    def remote(src, dst, send, recv, to):
        return pltpu.make_async_remote_copy(
            src_ref=src, dst_ref=dst, send_sem=send, recv_sem=recv, device_id=to, device_id_type=MESH)

    own_rows = pl.ds(pl.multiple_of(y * TOK, TOK), TOK)

    def kv_source(h, i, to_y):
        return (keys, values)[i].at[:, columns((to_y * HLOC + h) * DH, DH)]

    def kv_copy(o, h, i):
        to, g = partner(o), 2 * h + i
        return remote(kv_source(h, i, to[1]), kv.at[g, 0, own_rows], own_send.at[g], own_recv.at[g], to)

    def kv_local(h, i):
        return pltpu.make_async_copy(kv_source(h, i, y), kv.at[2 * h + i, 0, own_rows], local_sem.at[2 * h + i])

    def q_source(h, to_y):
        return query.at[:, columns((to_y * HLOC + h) * WIDE, WIDE)]

    def q_copy(o, h):
        to = partner(o)
        return remote(q_source(h, to[1]), qbuf.at[h, y], q_send.at[h], q_recv.at[h], to)

    def q_local(h):
        return pltpu.make_async_copy(q_source(h, y), qbuf.at[h, y], local_sem.at[GROUPS + h])

    def q_local_wait(h):
        pltpu.make_async_copy(qbuf.at[h, 0], qbuf.at[h, 0], local_sem.at[GROUPS + h]).wait()

    def out_place(to_y, h):
        return out.at[:, columns((to_y * HLOC + h) * WIDE, WIDE)]

    def out_copy(o, h):
        to = partner(o)
        return remote(obuf.at[h, to[1]], out_place(y, h), out_send.at[h], out_recv.at[h], to)

    def out_local(h):
        return pltpu.make_async_copy(obuf.at[h, y], out_place(y, h), local_sem.at[GROUPS + HLOC + h])

    def three(ref, send, recv):
        return remote(ref, ref, send, recv, sibling)

    def kv_three(g):
        return three(kv.at[g, 0, pl.ds(0, 3 * TOK)], own_send.at[g], own_recv.at[g])

    def kv_local_wait(g):
        ref = kv.at[g, 0, pl.ds(0, TOK)]
        pltpu.make_async_copy(ref, ref, local_sem.at[g]).wait()

    def q_three(h):
        return three(qbuf.at[h, pl.ds(0, 3)], q_send.at[h], q_recv.at[h])

    def out_three(h):
        return three(obuf.at[h, pl.ds(0, 3)], out_send.at[h], out_recv.at[h])

    def send_q(h):
        for o in (2, 1, 3):
            q_copy(o, h).start()
        q_local(h).start()

    def half(k):
        return pl.ds(k * TOK // 2, TOK // 2)

    def out_via(h, k):
        return remote(obuf.at[h, partner(2)[1], half(k)], relay.at[h, k], out_send.at[h], relay_recv.at[h, k],
                      partner(1 + 2 * k))

    def out_pass(h):
        for k in range(2):
            ref = relay.at[h, k]
            remote(ref, ref, out_send.at[h], relay_recv.at[h, k], sibling).wait_recv()
            remote(ref, out_place(partner(3 - 2 * k)[1], h).at[half(k)], relay_send.at[h], out_recv.at[h],
                   partner(1 + 2 * k)).start()

    def piece(m, slot):
        return kv.at[m // PARTS, slot, pl.ds(pl.multiple_of(lax.rem(m, PARTS) * ROWS, ROWS), ROWS)]

    def forward(m, to, r, into):
        remote(piece(m, 2 * r), piece(m, 2 * into),
               win_send.at[m // PARTS], win_recv.at[m, into - 1], to).start()

    def arrived(m, r):
        remote(piece(m, 2 * r), piece(m, 2 * r), win_send.at[m // PARTS], win_recv.at[m, r - 1], up).wait_recv()

    def share(m, r):
        g = m // PARTS

        def go():
            remote(kv.at[g, 2 * r], kv.at[g, 2 * r + 1 - 2 * core], sib_send.at[g], sib_recv.at[g], sibling).start()

        whole_slot = lax.rem(m, PARTS) == PARTS - 1
        if r == 0:
            whole_slot = whole_slot & (core == 0)
        elif r == 6:
            whole_slot = whole_slot & (core == 1)
        pl.when(whole_slot)(go)

    def own(m):
        @pl.when(lax.rem(m, PARTS) == 0)
        def _():
            kv_three(m // PARTS).wait_recv()
            kv_local_wait(m // PARTS)

    def event(m, entry):
        if len(entry) > 2:
            there = place >= entry[2]
            if entry[1] == "Z":
                there = there & (z < nz - 1)
            to = {"Z": up, "P": right, "M": left}[entry[1]]
            pl.when(there)(lambda: forward(m, to, entry[2], entry[3]))
        else:
            if entry[1] == 0:
                own(m)
            else:
                pl.when(place >= entry[1])(lambda: arrived(m, entry[1]))
            share(m, entry[1])

    def step(n):
        for xx in range(NX):
            @pl.when(x == xx)
            def _():
                for lag in sorted({entry[0] for entry in ROUTES[xx]}):
                    m = n - lag

                    @pl.when((m >= 0) & (m < PIECES))
                    def _():
                        for entry in ROUTES[xx]:
                            if entry[0] == lag:
                                event(m, entry)

    def send_kv(h, _):
        for i in range(2):
            for o in (2, 1, 3):
                kv_copy(o, h, i).start()
            kv_local(h, i).start()
        return 0

    lax.fori_loop(0, HLOC, send_kv, 0)

    def whole(g, slots=6):
        ref = kv.at[g, pl.ds(0, slots)]
        return remote(ref, ref, sib_send.at[g], sib_recv.at[g], sibling)

    def picks(h):
        valid, slot = [None], [0]
        for t in range(TOPK):
            pick = chosen[0, h, t]
            valid.append(pick >= 0)
            slot.append(seq - pick)
        return valid, slot

    def collect(g):
        _, slot = picks(g // 2)

        def part(i, _):
            rows = pl.ds(pl.multiple_of(i * DH, DH), DH)
            block = kv[g, 0, rows]
            blocks[g % 2, 0, rows] = block
            found = [block] * TOPK
            for d in range(1, SLOTS):
                block = kv[g, d, rows]
                for t in range(TOPK):
                    found[t] = jnp.where(slot[t + 1] == d, block, found[t])
            for t in range(TOPK):
                blocks[g % 2, t + 1, rows] = found[t]
            return 0

        lax.fori_loop(0, BLK // DH, part, 0)

    behind = (lax.broadcasted_iota(jnp.int32, (TOK, TOK), 0)
              - lax.broadcasted_iota(jnp.int32, (TOK, TOK), 1))

    def fold(op, start, rows):
        for i in range(0, rows.shape[0], 8):
            start = op(start, rows[i:i + 8])
        return start

    def order(j):
        return lax.rem(2 + 3 * j + 3 * (j // 2) + 2 * (j // 3), NHEAD)

    def weigh(h, j):
        @pl.when(j == 0)
        def _():
            whole(2 * h).wait_recv()
            q_three(h).wait_recv()
            q_local_wait(h)
            collect(2 * h)

        c = lax.rem(y + order(j), NHEAD)
        for g in range(GRP):
            turned[:, g * TOK:(g + 1) * TOK] = qbuf[h, c, :, g * DH:(g + 1) * DH].T
        valid, _ = picks(h)
        top = None
        for t in range(TOPK + 1):
            high = jnp.full((8, GRP * TOK), NEG, jnp.float32)
            for i in range(BLK // TOK):
                s = jnp.dot(blocks[0, t, i * TOK:(i + 1) * TOK], turned[...], preferred_element_type=jnp.float32)
                if t == 0:
                    seen = behind <= (c - i) * TOK
                    s = jnp.concatenate(
                        [jnp.where(seen, s[:, g * TOK:(g + 1) * TOK], NEG) for g in range(GRP)], axis=1)
                scores[t, i * TOK:(i + 1) * TOK] = s
                high = fold(jnp.maximum, high, s)
            high = jnp.max(high, axis=0, keepdims=True)
            top = high if t == 0 else jnp.maximum(top, jnp.where(valid[t], high, NEG))
        total = jnp.zeros((8, GRP * TOK), jnp.float32)
        for t in range(TOPK + 1):
            shift = top if t == 0 else jnp.where(valid[t], top, -NEG)

            def band(i, total):
                rows = pl.ds(pl.multiple_of(i * STRIP, STRIP), STRIP)
                p = jnp.exp((scores[t, rows] - shift) * RATE)
                weights[c, pl.ds(pl.multiple_of(t * BLK + i * STRIP, STRIP), STRIP)] = p.astype(jnp.bfloat16)
                return fold(jnp.add, total, p)

            total = lax.fori_loop(0, BLK // STRIP, band, total, unroll=4)
        totals[c] = jnp.broadcast_to(jnp.sum(total, axis=0, keepdims=True), (8, GRP * TOK))

    def attend(h, j):
        @pl.when(j == 0)
        def _():
            whole(2 * h + 1).wait_recv()
            collect(2 * h + 1)
            for t in range(TOPK + 1):
                flipped[:, t * BLK:(t + 1) * BLK] = blocks[1, t].T

        o = order(j)
        c = lax.rem(y + o, NHEAD)
        for side in range(2):
            q0 = side * 2 * TOK
            acc = jnp.dot(flipped[...], weights[c, :, q0:q0 + 2 * TOK], preferred_element_type=jnp.float32)
            res = acc / totals[c, 0:1, q0:q0 + 2 * TOK]
            for g in range(2):
                obuf[h, c, :, q0 + g * DH:q0 + (g + 1) * DH] = res[:, g * TOK:(g + 1) * TOK].T.astype(jnp.bfloat16)
        for k in (1, 3):
            pl.when(o == k)(lambda: out_copy(k, h).start())

        @pl.when(o == 2)
        def _():
            for k in range(2):
                out_via(h, k).start()

        pl.when(o == 0)(lambda: out_local(h).start())

    def before(n):
        return sum((n + 63 - tick) // 64 for tick in ITEM_TICKS)

    def item(k, _):
        h, kind, j = k // 8, lax.rem(k // 4, 2), lax.rem(k, 4)
        pl.when(kind == 0)(lambda: weigh(h, j))
        pl.when(kind == 1)(lambda: attend(h, j))
        pl.when((k == 9) | (k == 15))(lambda: out_pass(k // 15))
        return 0

    def tick(n, _):
        step(n)
        pl.when((n == 3) | (n == 6))(lambda: send_q(n // 6))
        lax.fori_loop(before(n), before(n + 1), item, 0)
        return 0

    lax.fori_loop(0, TICKS, tick, 0)

    def sent(g):
        for xx in range(NX):
            for low, high in ((0, 1), (1, 2), (2, nz - 1), (nz - 1, nz)):
                count = 0
                for entry in ROUTES[xx]:
                    if len(entry) > 2 and low * NX + xx >= entry[2] and (entry[1] != "Z" or low < nz - 1):
                        count += 1
                if count == 0:
                    continue

                @pl.when((x == xx) & (z >= low) & (z < high))
                def _():
                    ref = kv.at[g, pl.ds(0, count)]
                    remote(ref, ref, win_send.at[g], sib_recv.at[g], right).wait_send()

    def finish(g, _):
        kv_three(g).wait_send()
        whole(g).wait_send()
        sent(g)
        return 0

    lax.fori_loop(0, GROUPS, finish, 0)
    for h in range(HLOC):
        q_three(h).wait_send()
        out_three(h).wait()
        three(relay.at[h], relay_send.at[h], out_recv.at[h]).wait_send()
        out_local(h).wait()


def on_device(query, keys, values, chosen):
    nseq = lax.axis_size("seq")
    dma = pltpu.SemaphoreType.DMA
    any_spec = pl.BlockSpec(memory_space=pl.ANY)

    def body(*refs):
        kernel(nseq, *refs)

    return pl.pallas_call(
        body,
        out_shape=pltpu.VMEM(query.shape, jnp.bfloat16),
        in_specs=[pl.BlockSpec(memory_space=pltpu.SMEM), any_spec, any_spec, any_spec],
        out_specs=pl.BlockSpec(memory_space=pltpu.VMEM),
        scratch_shapes=[
            pltpu.VMEM((GROUPS, SLOTS, BLK, DH), jnp.bfloat16),
            pltpu.VMEM((2, TOPK + 1, BLK, DH), jnp.bfloat16),
            pltpu.VMEM((HLOC, NHEAD, TOK, WIDE), jnp.bfloat16),
            pltpu.VMEM((HLOC, NHEAD, TOK, WIDE), jnp.bfloat16),
            pltpu.VMEM((TOPK + 1, BLK, GRP * TOK), jnp.float32),
            pltpu.VMEM((NHEAD, (TOPK + 1) * BLK, GRP * TOK), jnp.bfloat16),
            pltpu.VMEM((NHEAD, 8, GRP * TOK), jnp.float32),
            pltpu.VMEM((DH, (TOPK + 1) * BLK), jnp.bfloat16),
            pltpu.VMEM((DH, GRP * TOK), jnp.bfloat16),
            pltpu.VMEM((HLOC, 2, TOK // 2, WIDE), jnp.bfloat16),
            dma((GROUPS,)), dma((GROUPS,)),
            dma((HLOC,)), dma((HLOC,)),
            dma((GROUPS,)), dma((PIECES, 6)),
            dma((GROUPS,)), dma((GROUPS,)),
            dma((HLOC,)), dma((HLOC,)),
            dma((HLOC, 2)), dma((HLOC,)),
            dma((GROUPS + 2 * HLOC,)),
        ],
        compiler_params=pltpu.CompilerParams(
            collective_id=0, has_side_effects=True, vmem_limit_bytes=56 * 1024 * 1024),
        cost_estimate=pl.CostEstimate(
            flops=4 * BLK * HLOC * GRP * BLK * 4 * DH, bytes_accessed=4 * 1024 * 1024,
            transcendentals=HLOC * GRP * BLK * BLK * 4),
        name="window_attention",
    )(chosen, query, keys, values)


def solution(mesh):
    in_specs = (
        P(("seq", "head"), None),
        P(("seq", "head"), None),
        P(("seq", "head"), None),
        P("seq", "head", None),
    )
    return jax.shard_map(
        on_device, mesh=mesh, in_specs=in_specs, out_specs=P(("seq", "head"), None), check_vma=False
    )
```

```python
import math

import jax
import jax.numpy as jnp
from jax import lax
from jax.experimental import pallas as pl
from jax.experimental.pallas import tpu as pltpu
from jax.sharding import PartitionSpec as P

HQ = 32
HK = 8
DH = 128
BLK = 512
TOPK = 3
GRP = HQ // HK
NHEAD = 4
HLOC = HK // NHEAD
TOK = BLK // NHEAD
NX = 4
SLOTS = 13
GROUPS = 2 * HLOC
PARTS = 1
PIECES = GROUPS * PARTS
ROWS = BLK // PARTS
WIDE = GRP * DH
STRIP = 32
NEG = -1e30
RATE = 1.0 / math.sqrt(DH)
MESH = pl.DeviceIdType.MESH

ROUTES = {
    0: [
        (0, 0), (0, "Z", 0, 4), (0, "P", 0, 1), (0, "M", 0, 3), (1, 4),
        (1, "P", 4, 5), (2, 1), (2, "Z", 1, 5), (2, 3), (2, "M", 3, 6),
        (3, 2), (3, "Z", 2, 6), (3, 5), (4, 6),
    ],
    1: [
        (0, 0), (0, "Z", 0, 4), (0, "P", 0, 1), (1, 4), (1, "M", 4, 3),
        (1, "P", 4, 5), (1, 1), (2, 3), (2, 5), (3, 2),
        (3, "Z", 2, 6), (4, 6),
    ],
    2: [
        (0, 0), (0, "Z", 0, 4), (0, "P", 0, 1), (1, 4), (1, "M", 4, 3),
        (1, 1), (1, "P", 1, 2), (2, 3), (2, "M", 3, 2), (2, 2),
        (2, "Z", 2, 6), (2, 5), (3, 6),
    ],
    3: [
        (0, 0), (0, "Z", 0, 4), (1, 4), (1, "P", 4, 1), (1, "M", 4, 3),
        (1, 3), (1, "M", 3, 2), (1, 1), (1, "Z", 1, 5), (2, 5),
        (2, "P", 5, 2), (2, 2), (3, 6),
    ],
}
TICKS = 8
ITEM_TICKS = (4, 4, 4, 4, 5, 5, 5, 5, 6, 6, 6, 6, 7, 7, 7, 7)


def kernel(nseq, chosen, query, keys, values, out, kv, blocks, qbuf, obuf, scores, weights, totals, flipped, turned, relay,
           own_send, own_recv, q_send, q_recv, win_send, win_recv, sib_send, sib_recv,
           out_send, out_recv, relay_recv, relay_send, local_sem):
    nz = nseq // (2 * NX)
    seq = lax.axis_index("seq")
    y = lax.axis_index("head")
    core = lax.rem(seq, 2)
    x = lax.rem(seq // 2, NX)
    z = seq // (2 * NX)

    def at(zz, xx):
        return ((zz * NX + xx) * 2 + core, y)

    up = at(lax.rem(z + 1, nz), x)
    down = at(lax.rem(z + nz - 1, nz), x)
    right = at(z, lax.rem(x + 1, NX))
    left = at(z, lax.rem(x + NX - 1, NX))
    sibling = (seq + 1 - 2 * core, y)

    def partner(o):
        return (seq, lax.rem(y + o, NHEAD))

    place = z * NX + x
    barrier = pltpu.get_barrier_semaphore()

    def greet(who):
        pl.semaphore_signal(barrier, inc=1, device_id=who, device_id_type=MESH)

    for who in [right, left, sibling, partner(1), partner(2), partner(3)]:
        greet(who)
    pl.when(z < nz - 1)(lambda: greet(up))
    pl.when(z > 0)(lambda: greet(down))
    edge = (z == 0) | (z == nz - 1)
    pl.when(edge)(lambda: pl.semaphore_wait(barrier, 7))
    pl.when(jnp.logical_not(edge))(lambda: pl.semaphore_wait(barrier, 8))

    def columns(start, width):
        return pl.ds(pl.multiple_of(start, DH), width)

    def remote(src, dst, send, recv, to):
        return pltpu.make_async_remote_copy(
            src_ref=src, dst_ref=dst, send_sem=send, recv_sem=recv, device_id=to, device_id_type=MESH)

    own_rows = pl.ds(pl.multiple_of(y * TOK, TOK), TOK)

    def kv_source(h, i, to_y):
        return (keys, values)[i].at[:, columns((to_y * HLOC + h) * DH, DH)]

    def kv_copy(o, h, i):
        to, g = partner(o), 2 * h + i
        return remote(kv_source(h, i, to[1]), kv.at[g, 0, own_rows], own_send.at[g], own_recv.at[g], to)

    def kv_local(h, i):
        return pltpu.make_async_copy(kv_source(h, i, y), kv.at[2 * h + i, 0, own_rows], local_sem.at[2 * h + i])

    def q_source(h, to_y):
        return query.at[:, columns((to_y * HLOC + h) * WIDE, WIDE)]

    def q_copy(o, h):
        to = partner(o)
        return remote(q_source(h, to[1]), qbuf.at[h, y], q_send.at[h], q_recv.at[h], to)

    def q_local(h):
        return pltpu.make_async_copy(q_source(h, y), qbuf.at[h, y], local_sem.at[GROUPS + h])

    def q_local_wait(h):
        pltpu.make_async_copy(qbuf.at[h, 0], qbuf.at[h, 0], local_sem.at[GROUPS + h]).wait()

    def out_place(to_y, h):
        return out.at[:, columns((to_y * HLOC + h) * WIDE, WIDE)]

    def out_copy(o, h):
        to = partner(o)
        return remote(obuf.at[h, to[1]], out_place(y, h), out_send.at[h], out_recv.at[h], to)

    def out_local(h):
        return pltpu.make_async_copy(obuf.at[h, y], out_place(y, h), local_sem.at[GROUPS + HLOC + h])

    def three(ref, send, recv):
        return remote(ref, ref, send, recv, sibling)

    def kv_three(g):
        return three(kv.at[g, 0, pl.ds(0, 3 * TOK)], own_send.at[g], own_recv.at[g])

    def kv_local_wait(g):
        ref = kv.at[g, 0, pl.ds(0, TOK)]
        pltpu.make_async_copy(ref, ref, local_sem.at[g]).wait()

    def q_three(h):
        return three(qbuf.at[h, pl.ds(0, 3)], q_send.at[h], q_recv.at[h])

    def out_three(h):
        return three(obuf.at[h, pl.ds(0, 3)], out_send.at[h], out_recv.at[h])

    def send_q(h):
        for o in (2, 1, 3):
            q_copy(o, h).start()
        q_local(h).start()

    def half(k):
        return pl.ds(k * TOK // 2, TOK // 2)

    def out_via(h, k):
        return remote(obuf.at[h, partner(2)[1], half(k)], relay.at[h, k], out_send.at[h], relay_recv.at[h, k],
                      partner(1 + 2 * k))

    def out_pass(h):
        for k in range(2):
            ref = relay.at[h, k]
            remote(ref, ref, out_send.at[h], relay_recv.at[h, k], sibling).wait_recv()
            remote(ref, out_place(partner(3 - 2 * k)[1], h).at[half(k)], relay_send.at[h], out_recv.at[h],
                   partner(1 + 2 * k)).start()

    def piece(m, slot):
        return kv.at[m // PARTS, slot, pl.ds(pl.multiple_of(lax.rem(m, PARTS) * ROWS, ROWS), ROWS)]

    def forward(m, to, r, into):
        remote(piece(m, 2 * r), piece(m, 2 * into),
               win_send.at[m // PARTS], win_recv.at[m, into - 1], to).start()

    def arrived(m, r):
        remote(piece(m, 2 * r), piece(m, 2 * r), win_send.at[m // PARTS], win_recv.at[m, r - 1], up).wait_recv()

    def share(m, r):
        g = m // PARTS

        def go():
            remote(kv.at[g, 2 * r], kv.at[g, 2 * r + 1 - 2 * core], sib_send.at[g], sib_recv.at[g], sibling).start()

        whole_slot = lax.rem(m, PARTS) == PARTS - 1
        if r == 0:
            whole_slot = whole_slot & (core == 0)
        elif r == 6:
            whole_slot = whole_slot & (core == 1)
        pl.when(whole_slot)(go)

    def own(m):
        @pl.when(lax.rem(m, PARTS) == 0)
        def _():
            kv_three(m // PARTS).wait_recv()
            kv_local_wait(m // PARTS)

    def event(m, entry):
        if len(entry) > 2:
            there = place >= entry[2]
            if entry[1] == "Z":
                there = there & (z < nz - 1)
            to = {"Z": up, "P": right, "M": left}[entry[1]]
            pl.when(there)(lambda: forward(m, to, entry[2], entry[3]))
        else:
            if entry[1] == 0:
                own(m)
            else:
                pl.when(place >= entry[1])(lambda: arrived(m, entry[1]))
            share(m, entry[1])

    def step(n):
        for xx in range(NX):
            @pl.when(x == xx)
            def _():
                for lag in sorted({entry[0] for entry in ROUTES[xx]}):
                    m = n - lag

                    @pl.when((m >= 0) & (m < PIECES))
                    def _():
                        for entry in ROUTES[xx]:
                            if entry[0] == lag:
                                event(m, entry)

    def send_kv(h, _):
        for i in range(2):
            for o in (2, 1, 3):
                kv_copy(o, h, i).start()
            kv_local(h, i).start()
        return 0

    lax.fori_loop(0, HLOC, send_kv, 0)

    def whole(g, slots=6):
        ref = kv.at[g, pl.ds(0, slots)]
        return remote(ref, ref, sib_send.at[g], sib_recv.at[g], sibling)

    def picks(h):
        valid, slot = [None], [0]
        for t in range(TOPK):
            pick = chosen[0, h, t]
            valid.append(pick >= 0)
            slot.append(seq - pick)
        return valid, slot

    def collect(g):
        _, slot = picks(g // 2)

        def part(i, _):
            rows = pl.ds(pl.multiple_of(i * DH, DH), DH)
            block = kv[g, 0, rows]
            blocks[g % 2, 0, rows] = block
            found = [block] * TOPK
            for d in range(1, SLOTS):
                block = kv[g, d, rows]
                for t in range(TOPK):
                    found[t] = jnp.where(slot[t + 1] == d, block, found[t])
            for t in range(TOPK):
                blocks[g % 2, t + 1, rows] = found[t]
            return 0

        lax.fori_loop(0, BLK // DH, part, 0)

    behind = (lax.broadcasted_iota(jnp.int32, (TOK, TOK), 0)
              - lax.broadcasted_iota(jnp.int32, (TOK, TOK), 1))

    def fold(op, start, rows):
        for i in range(0, rows.shape[0], 8):
            start = op(start, rows[i:i + 8])
        return start

    def order(j):
        return lax.rem(2 + 3 * j + 3 * (j // 2) + 2 * (j // 3), NHEAD)

    def weigh(h, j):
        @pl.when(j == 0)
        def _():
            whole(2 * h).wait_recv()
            q_three(h).wait_recv()
            q_local_wait(h)
            collect(2 * h)

        c = lax.rem(y + order(j), NHEAD)
        for g in range(GRP):
            turned[:, g * TOK:(g + 1) * TOK] = qbuf[h, c, :, g * DH:(g + 1) * DH].T
        valid, _ = picks(h)
        top = None
        for t in range(TOPK + 1):
            high = jnp.full((8, GRP * TOK), NEG, jnp.float32)
            for i in range(BLK // TOK):
                s = jnp.dot(blocks[0, t, i * TOK:(i + 1) * TOK], turned[...], preferred_element_type=jnp.float32)
                if t == 0:
                    seen = behind <= (c - i) * TOK
                    s = jnp.concatenate(
                        [jnp.where(seen, s[:, g * TOK:(g + 1) * TOK], NEG) for g in range(GRP)], axis=1)
                scores[t, i * TOK:(i + 1) * TOK] = s
                high = fold(jnp.maximum, high, s)
            high = jnp.max(high, axis=0, keepdims=True)
            top = high if t == 0 else jnp.maximum(top, jnp.where(valid[t], high, NEG))
        total = jnp.zeros((8, GRP * TOK), jnp.float32)
        for t in range(TOPK + 1):
            shift = top if t == 0 else jnp.where(valid[t], top, -NEG)

            def band(i, total):
                rows = pl.ds(pl.multiple_of(i * STRIP, STRIP), STRIP)
                p = jnp.exp((scores[t, rows] - shift) * RATE)
                weights[c, pl.ds(pl.multiple_of(t * BLK + i * STRIP, STRIP), STRIP)] = p.astype(jnp.bfloat16)
                return fold(jnp.add, total, p)

            total = lax.fori_loop(0, BLK // STRIP, band, total, unroll=4)
        totals[c] = jnp.broadcast_to(jnp.sum(total, axis=0, keepdims=True), (8, GRP * TOK))

    def attend(h, j):
        @pl.when(j == 0)
        def _():
            whole(2 * h + 1).wait_recv()
            collect(2 * h + 1)
            for t in range(TOPK + 1):
                flipped[:, t * BLK:(t + 1) * BLK] = blocks[1, t].T

        o = order(j)
        c = lax.rem(y + o, NHEAD)
        for side in range(2):
            q0 = side * 2 * TOK
            acc = jnp.dot(flipped[...], weights[c, :, q0:q0 + 2 * TOK], preferred_element_type=jnp.float32)
            res = acc / totals[c, 0:1, q0:q0 + 2 * TOK]
            for g in range(2):
                obuf[h, c, :, q0 + g * DH:q0 + (g + 1) * DH] = res[:, g * TOK:(g + 1) * TOK].T.astype(jnp.bfloat16)
        for k in (1, 3):
            pl.when(o == k)(lambda: out_copy(k, h).start())

        @pl.when(o == 2)
        def _():
            for k in range(2):
                out_via(h, k).start()

        pl.when(o == 0)(lambda: out_local(h).start())

    def before(n):
        return sum((n + 63 - tick) // 64 for tick in ITEM_TICKS)

    def item(k, _):
        h, kind, j = k // 8, lax.rem(k // 4, 2), lax.rem(k, 4)
        pl.when(kind == 0)(lambda: weigh(h, j))
        pl.when(kind == 1)(lambda: attend(h, j))
        pl.when((k == 9) | (k == 15))(lambda: out_pass(k // 15))
        return 0

    def tick(n, _):
        step(n)
        pl.when((n == 1) | (n == 2))(lambda: send_q(n // 2))
        lax.fori_loop(before(n), before(n + 1), item, 0)
        return 0

    lax.fori_loop(0, TICKS, tick, 0)

    def sent(g):
        for xx in range(NX):
            for low, high in ((0, 1), (1, 2), (2, nz - 1), (nz - 1, nz)):
                count = 0
                for entry in ROUTES[xx]:
                    if len(entry) > 2 and low * NX + xx >= entry[2] and (entry[1] != "Z" or low < nz - 1):
                        count += 1
                if count == 0:
                    continue

                @pl.when((x == xx) & (z >= low) & (z < high))
                def _():
                    ref = kv.at[g, pl.ds(0, count)]
                    remote(ref, ref, win_send.at[g], sib_recv.at[g], right).wait_send()

    def finish(g, _):
        kv_three(g).wait_send()
        whole(g).wait_send()
        sent(g)
        return 0

    lax.fori_loop(0, GROUPS, finish, 0)
    for h in range(HLOC):
        q_three(h).wait_send()
        out_three(h).wait()
        three(relay.at[h], relay_send.at[h], out_recv.at[h]).wait_send()
        out_local(h).wait()


def on_device(query, keys, values, chosen):
    nseq = lax.axis_size("seq")
    dma = pltpu.SemaphoreType.DMA
    any_spec = pl.BlockSpec(memory_space=pl.ANY)

    def body(*refs):
        kernel(nseq, *refs)

    return pl.pallas_call(
        body,
        out_shape=pltpu.VMEM(query.shape, jnp.bfloat16),
        in_specs=[pl.BlockSpec(memory_space=pltpu.SMEM), any_spec, any_spec, any_spec],
        out_specs=pl.BlockSpec(memory_space=pltpu.VMEM),
        scratch_shapes=[
            pltpu.VMEM((GROUPS, SLOTS, BLK, DH), jnp.bfloat16),
            pltpu.VMEM((2, TOPK + 1, BLK, DH), jnp.bfloat16),
            pltpu.VMEM((HLOC, NHEAD, TOK, WIDE), jnp.bfloat16),
            pltpu.VMEM((HLOC, NHEAD, TOK, WIDE), jnp.bfloat16),
            pltpu.VMEM((TOPK + 1, BLK, GRP * TOK), jnp.float32),
            pltpu.VMEM((NHEAD, (TOPK + 1) * BLK, GRP * TOK), jnp.bfloat16),
            pltpu.VMEM((NHEAD, 8, GRP * TOK), jnp.float32),
            pltpu.VMEM((DH, (TOPK + 1) * BLK), jnp.bfloat16),
            pltpu.VMEM((DH, GRP * TOK), jnp.bfloat16),
            pltpu.VMEM((HLOC, 2, TOK // 2, WIDE), jnp.bfloat16),
            dma((GROUPS,)), dma((GROUPS,)),
            dma((HLOC,)), dma((HLOC,)),
            dma((GROUPS,)), dma((PIECES, 6)),
            dma((GROUPS,)), dma((GROUPS,)),
            dma((HLOC,)), dma((HLOC,)),
            dma((HLOC, 2)), dma((HLOC,)),
            dma((GROUPS + 2 * HLOC,)),
        ],
        compiler_params=pltpu.CompilerParams(
            collective_id=0, has_side_effects=True, vmem_limit_bytes=56 * 1024 * 1024),
        cost_estimate=pl.CostEstimate(
            flops=4 * BLK * HLOC * GRP * BLK * 4 * DH, bytes_accessed=4 * 1024 * 1024,
            transcendentals=HLOC * GRP * BLK * BLK * 4),
        name="window_attention",
    )(chosen, query, keys, values)


def solution(mesh):
    in_specs = (
        P(("seq", "head"), None),
        P(("seq", "head"), None),
        P(("seq", "head"), None),
        P("seq", "head", None),
    )
    return jax.shard_map(
        on_device, mesh=mesh, in_specs=in_specs, out_specs=P(("seq", "head"), None), check_vma=False
    )
```

```python
import math

import jax
import jax.numpy as jnp
from jax import lax
from jax.experimental import pallas as pl
from jax.experimental.pallas import tpu as pltpu
from jax.sharding import PartitionSpec as P

HQ = 32
HK = 8
DH = 128
BLK = 512
TOPK = 3
GRP = HQ // HK
NHEAD = 4
HLOC = HK // NHEAD
TOK = BLK // NHEAD
NX = 4
SLOTS = 13
GROUPS = 2 * HLOC
PARTS = 2
PIECES = GROUPS * PARTS
ROWS = BLK // PARTS
WIDE = GRP * DH
STRIP = 32
NEG = -1e30
RATE = 1.0 / math.sqrt(DH)
MESH = pl.DeviceIdType.MESH

ROUTES = {
    0: [
        (0, 0), (0, "Z", 0, 4), (0, "P", 0, 1), (0, "M", 0, 3), (2, 4),
        (2, "P", 4, 5), (4, 1), (4, "Z", 1, 5), (4, 3), (4, "M", 3, 6),
        (6, 2), (6, "Z", 2, 6), (6, 5), (8, 6),
    ],
    1: [
        (0, 0), (0, "Z", 0, 4), (0, "P", 0, 1), (2, 4), (2, "M", 4, 3),
        (2, "P", 4, 5), (2, 1), (4, 3), (4, 5), (6, 2),
        (6, "Z", 2, 6), (8, 6),
    ],
    2: [
        (0, 0), (0, "Z", 0, 4), (0, "P", 0, 1), (2, 4), (2, "M", 4, 3),
        (2, 1), (2, "P", 1, 2), (4, 3), (4, "M", 3, 2), (4, 2),
        (4, "Z", 2, 6), (4, 5), (6, 6),
    ],
    3: [
        (0, 0), (0, "Z", 0, 4), (2, 4), (2, "P", 4, 1), (2, "M", 4, 3),
        (2, 3), (2, "M", 3, 2), (2, 1), (2, "Z", 1, 5), (4, 5),
        (4, "P", 5, 2), (4, 2), (5, 6),
    ],
}
TICKS = 16
ITEM_TICKS = (9, 10, 10, 11, 11, 12, 12, 12, 13, 13, 14, 15, 15, 15, 15, 15)


def kernel(nseq, chosen, query, keys, values, out, kv, blocks, qbuf, obuf, scores, weights, totals, flipped, turned, relay,
           own_send, own_recv, q_send, q_recv, win_send, win_recv, sib_send, sib_recv,
           out_send, out_recv, relay_recv, relay_send, local_sem):
    nz = nseq // (2 * NX)
    seq = lax.axis_index("seq")
    y = lax.axis_index("head")
    core = lax.rem(seq, 2)
    x = lax.rem(seq // 2, NX)
    z = seq // (2 * NX)

    def at(zz, xx):
        return ((zz * NX + xx) * 2 + core, y)

    up = at(lax.rem(z + 1, nz), x)
    down = at(lax.rem(z + nz - 1, nz), x)
    right = at(z, lax.rem(x + 1, NX))
    left = at(z, lax.rem(x + NX - 1, NX))
    sibling = (seq + 1 - 2 * core, y)

    def partner(o):
        return (seq, lax.rem(y + o, NHEAD))

    place = z * NX + x
    barrier = pltpu.get_barrier_semaphore()

    def greet(who):
        pl.semaphore_signal(barrier, inc=1, device_id=who, device_id_type=MESH)

    for who in [right, left, sibling, partner(1), partner(2), partner(3)]:
        greet(who)
    pl.when(z < nz - 1)(lambda: greet(up))
    pl.when(z > 0)(lambda: greet(down))
    edge = (z == 0) | (z == nz - 1)
    pl.when(edge)(lambda: pl.semaphore_wait(barrier, 7))
    pl.when(jnp.logical_not(edge))(lambda: pl.semaphore_wait(barrier, 8))

    def columns(start, width):
        return pl.ds(pl.multiple_of(start, DH), width)

    def remote(src, dst, send, recv, to):
        return pltpu.make_async_remote_copy(
            src_ref=src, dst_ref=dst, send_sem=send, recv_sem=recv, device_id=to, device_id_type=MESH)

    own_rows = pl.ds(pl.multiple_of(y * TOK, TOK), TOK)

    def kv_source(h, i, to_y):
        return (keys, values)[i].at[:, columns((to_y * HLOC + h) * DH, DH)]

    def kv_copy(o, h, i):
        to, g = partner(o), 2 * h + i
        return remote(kv_source(h, i, to[1]), kv.at[g, 0, own_rows], own_send.at[g], own_recv.at[g], to)

    def kv_local(h, i):
        return pltpu.make_async_copy(kv_source(h, i, y), kv.at[2 * h + i, 0, own_rows], local_sem.at[2 * h + i])

    def q_source(h, to_y):
        return query.at[:, columns((to_y * HLOC + h) * WIDE, WIDE)]

    def q_copy(o, h):
        to = partner(o)
        return remote(q_source(h, to[1]), qbuf.at[h, y], q_send.at[h], q_recv.at[h], to)

    def q_local(h):
        return pltpu.make_async_copy(q_source(h, y), qbuf.at[h, y], local_sem.at[GROUPS + h])

    def q_local_wait(h):
        pltpu.make_async_copy(qbuf.at[h, 0], qbuf.at[h, 0], local_sem.at[GROUPS + h]).wait()

    def out_place(to_y, h):
        return out.at[:, columns((to_y * HLOC + h) * WIDE, WIDE)]

    def out_copy(o, h):
        to = partner(o)
        return remote(obuf.at[h, to[1]], out_place(y, h), out_send.at[h], out_recv.at[h], to)

    def out_local(h):
        return pltpu.make_async_copy(obuf.at[h, y], out_place(y, h), local_sem.at[GROUPS + HLOC + h])

    def three(ref, send, recv):
        return remote(ref, ref, send, recv, sibling)

    def kv_three(g):
        return three(kv.at[g, 0, pl.ds(0, 3 * TOK)], own_send.at[g], own_recv.at[g])

    def kv_local_wait(g):
        ref = kv.at[g, 0, pl.ds(0, TOK)]
        pltpu.make_async_copy(ref, ref, local_sem.at[g]).wait()

    def q_three(h):
        return three(qbuf.at[h, pl.ds(0, 3)], q_send.at[h], q_recv.at[h])

    def out_three(h):
        return three(obuf.at[h, pl.ds(0, 3)], out_send.at[h], out_recv.at[h])

    def send_q(h):
        for o in (2, 1, 3):
            q_copy(o, h).start()
        q_local(h).start()

    def half(k):
        return pl.ds(k * TOK // 2, TOK // 2)

    def out_via(h, k):
        return remote(obuf.at[h, partner(2)[1], half(k)], relay.at[h, k], out_send.at[h], relay_recv.at[h, k],
                      partner(1 + 2 * k))

    def out_pass(h):
        for k in range(2):
            ref = relay.at[h, k]
            remote(ref, ref, out_send.at[h], relay_recv.at[h, k], sibling).wait_recv()
            remote(ref, out_place(partner(3 - 2 * k)[1], h).at[half(k)], relay_send.at[h], out_recv.at[h],
                   partner(1 + 2 * k)).start()

    def piece(m, slot):
        return kv.at[m // PARTS, slot, pl.ds(pl.multiple_of(lax.rem(m, PARTS) * ROWS, ROWS), ROWS)]

    def forward(m, to, r, into):
        remote(piece(m, 2 * r), piece(m, 2 * into),
               win_send.at[m // PARTS], win_recv.at[m, into - 1], to).start()

    def arrived(m, r):
        remote(piece(m, 2 * r), piece(m, 2 * r), win_send.at[m // PARTS], win_recv.at[m, r - 1], up).wait_recv()

    def share(m, r):
        g = m // PARTS

        def go():
            remote(kv.at[g, 2 * r], kv.at[g, 2 * r + 1 - 2 * core], sib_send.at[g], sib_recv.at[g], sibling).start()

        whole_slot = lax.rem(m, PARTS) == PARTS - 1
        if r == 0:
            whole_slot = whole_slot & (core == 0)
        elif r == 6:
            whole_slot = whole_slot & (core == 1)
        pl.when(whole_slot)(go)

    def own(m):
        @pl.when(lax.rem(m, PARTS) == 0)
        def _():
            kv_three(m // PARTS).wait_recv()
            kv_local_wait(m // PARTS)

    def event(m, entry):
        if len(entry) > 2:
            there = place >= entry[2]
            if entry[1] == "Z":
                there = there & (z < nz - 1)
            to = {"Z": up, "P": right, "M": left}[entry[1]]
            pl.when(there)(lambda: forward(m, to, entry[2], entry[3]))
        else:
            if entry[1] == 0:
                own(m)
            else:
                pl.when(place >= entry[1])(lambda: arrived(m, entry[1]))
            share(m, entry[1])

    def step(n):
        for xx in range(NX):
            @pl.when(x == xx)
            def _():
                for lag in sorted({entry[0] for entry in ROUTES[xx]}):
                    m = n - lag

                    @pl.when((m >= 0) & (m < PIECES))
                    def _():
                        for entry in ROUTES[xx]:
                            if entry[0] == lag:
                                event(m, entry)

    def send_kv(h, i):
        for o in (2, 1, 3):
            kv_copy(o, h, i).start()
        kv_local(h, i).start()

    send_kv(0, 0)

    def whole(g, slots=6):
        ref = kv.at[g, pl.ds(0, slots)]
        return remote(ref, ref, sib_send.at[g], sib_recv.at[g], sibling)

    def picks(h):
        valid, slot = [None], [0]
        for t in range(TOPK):
            pick = chosen[0, h, t]
            valid.append(pick >= 0)
            slot.append(seq - pick)
        return valid, slot

    def collect(g):
        _, slot = picks(g // 2)

        def part(i, _):
            rows = pl.ds(pl.multiple_of(i * DH, DH), DH)
            block = kv[g, 0, rows]
            blocks[g % 2, 0, rows] = block
            found = [block] * TOPK
            for d in range(1, SLOTS):
                block = kv[g, d, rows]
                for t in range(TOPK):
                    found[t] = jnp.where(slot[t + 1] == d, block, found[t])
            for t in range(TOPK):
                blocks[g % 2, t + 1, rows] = found[t]
            return 0

        lax.fori_loop(0, BLK // DH, part, 0)

    behind = (lax.broadcasted_iota(jnp.int32, (TOK, TOK), 0)
              - lax.broadcasted_iota(jnp.int32, (TOK, TOK), 1))

    def fold(op, start, rows):
        for i in range(0, rows.shape[0], 8):
            start = op(start, rows[i:i + 8])
        return start

    def order(j):
        return lax.rem(2 + 3 * j + 3 * (j // 2) + 2 * (j // 3), NHEAD)

    def weigh(h, j):
        @pl.when(j == 0)
        def _():
            whole(2 * h).wait_recv()
            q_three(h).wait_recv()
            q_local_wait(h)
            collect(2 * h)

        c = lax.rem(y + order(j), NHEAD)
        for g in range(GRP):
            turned[:, g * TOK:(g + 1) * TOK] = qbuf[h, c, :, g * DH:(g + 1) * DH].T
        valid, _ = picks(h)
        top = None
        for t in range(TOPK + 1):
            high = jnp.full((8, GRP * TOK), NEG, jnp.float32)
            for i in range(BLK // TOK):
                s = jnp.dot(blocks[0, t, i * TOK:(i + 1) * TOK], turned[...], preferred_element_type=jnp.float32)
                if t == 0:
                    seen = behind <= (c - i) * TOK
                    s = jnp.concatenate(
                        [jnp.where(seen, s[:, g * TOK:(g + 1) * TOK], NEG) for g in range(GRP)], axis=1)
                scores[t, i * TOK:(i + 1) * TOK] = s
                high = fold(jnp.maximum, high, s)
            high = jnp.max(high, axis=0, keepdims=True)
            top = high if t == 0 else jnp.maximum(top, jnp.where(valid[t], high, NEG))
        total = jnp.zeros((8, GRP * TOK), jnp.float32)
        for t in range(TOPK + 1):
            shift = top if t == 0 else jnp.where(valid[t], top, -NEG)

            def band(i, total):
                rows = pl.ds(pl.multiple_of(i * STRIP, STRIP), STRIP)
                p = jnp.exp((scores[t, rows] - shift) * RATE)
                weights[c, pl.ds(pl.multiple_of(t * BLK + i * STRIP, STRIP), STRIP)] = p.astype(jnp.bfloat16)
                return fold(jnp.add, total, p)

            total = lax.fori_loop(0, BLK // STRIP, band, total, unroll=4)
        totals[c] = jnp.broadcast_to(jnp.sum(total, axis=0, keepdims=True), (8, GRP * TOK))

    def attend(h, j):
        @pl.when(j == 0)
        def _():
            whole(2 * h + 1).wait_recv()
            collect(2 * h + 1)
            for t in range(TOPK + 1):
                flipped[:, t * BLK:(t + 1) * BLK] = blocks[1, t].T

        o = order(j)
        c = lax.rem(y + o, NHEAD)
        for side in range(2):
            q0 = side * 2 * TOK
            acc = jnp.dot(flipped[...], weights[c, :, q0:q0 + 2 * TOK], preferred_element_type=jnp.float32)
            res = acc / totals[c, 0:1, q0:q0 + 2 * TOK]
            for g in range(2):
                obuf[h, c, :, q0 + g * DH:q0 + (g + 1) * DH] = res[:, g * TOK:(g + 1) * TOK].T.astype(jnp.bfloat16)
        for k in (1, 3):
            pl.when(o == k)(lambda: out_copy(k, h).start())

        @pl.when(o == 2)
        def _():
            for k in range(2):
                out_via(h, k).start()

        pl.when(o == 0)(lambda: out_local(h).start())

    def before(n):
        return sum((n + 63 - tick) // 64 for tick in ITEM_TICKS)

    def item(k, _):
        h, kind, j = k // 8, lax.rem(k // 4, 2), lax.rem(k, 4)
        pl.when(kind == 0)(lambda: weigh(h, j))
        pl.when(kind == 1)(lambda: attend(h, j))
        pl.when((k == 9) | (k == 15))(lambda: out_pass(k // 15))
        return 0

    def tick(n, _):
        step(n)
        pl.when(n == 0)(lambda: send_kv(0, 1))
        pl.when(n == 1)(lambda: send_kv(1, 0))
        pl.when(n == 2)(lambda: send_kv(1, 1))
        pl.when((n == 3) | (n == 6))(lambda: send_q(n // 6))
        lax.fori_loop(before(n), before(n + 1), item, 0)
        return 0

    lax.fori_loop(0, TICKS, tick, 0)

    def sent(g):
        for xx in range(NX):
            for low, high in ((0, 1), (1, 2), (2, nz - 1), (nz - 1, nz)):
                count = 0
                for entry in ROUTES[xx]:
                    if len(entry) > 2 and low * NX + xx >= entry[2] and (entry[1] != "Z" or low < nz - 1):
                        count += 1
                if count == 0:
                    continue

                @pl.when((x == xx) & (z >= low) & (z < high))
                def _():
                    ref = kv.at[g, pl.ds(0, count)]
                    remote(ref, ref, win_send.at[g], sib_recv.at[g], right).wait_send()

    def finish(g, _):
        kv_three(g).wait_send()
        whole(g).wait_send()
        sent(g)
        return 0

    lax.fori_loop(0, GROUPS, finish, 0)
    for h in range(HLOC):
        q_three(h).wait_send()
        out_three(h).wait()
        three(relay.at[h], relay_send.at[h], out_recv.at[h]).wait_send()
        out_local(h).wait()


def on_device(query, keys, values, chosen):
    nseq = lax.axis_size("seq")
    dma = pltpu.SemaphoreType.DMA
    any_spec = pl.BlockSpec(memory_space=pl.ANY)

    def body(*refs):
        kernel(nseq, *refs)

    return pl.pallas_call(
        body,
        out_shape=pltpu.VMEM(query.shape, jnp.bfloat16),
        in_specs=[pl.BlockSpec(memory_space=pltpu.SMEM), any_spec, any_spec, any_spec],
        out_specs=pl.BlockSpec(memory_space=pltpu.VMEM),
        scratch_shapes=[
            pltpu.VMEM((GROUPS, SLOTS, BLK, DH), jnp.bfloat16),
            pltpu.VMEM((2, TOPK + 1, BLK, DH), jnp.bfloat16),
            pltpu.VMEM((HLOC, NHEAD, TOK, WIDE), jnp.bfloat16),
            pltpu.VMEM((HLOC, NHEAD, TOK, WIDE), jnp.bfloat16),
            pltpu.VMEM((TOPK + 1, BLK, GRP * TOK), jnp.float32),
            pltpu.VMEM((NHEAD, (TOPK + 1) * BLK, GRP * TOK), jnp.bfloat16),
            pltpu.VMEM((NHEAD, 8, GRP * TOK), jnp.float32),
            pltpu.VMEM((DH, (TOPK + 1) * BLK), jnp.bfloat16),
            pltpu.VMEM((DH, GRP * TOK), jnp.bfloat16),
            pltpu.VMEM((HLOC, 2, TOK // 2, WIDE), jnp.bfloat16),
            dma((GROUPS,)), dma((GROUPS,)),
            dma((HLOC,)), dma((HLOC,)),
            dma((GROUPS,)), dma((PIECES, 6)),
            dma((GROUPS,)), dma((GROUPS,)),
            dma((HLOC,)), dma((HLOC,)),
            dma((HLOC, 2)), dma((HLOC,)),
            dma((GROUPS + 2 * HLOC,)),
        ],
        compiler_params=pltpu.CompilerParams(
            collective_id=0, has_side_effects=True, vmem_limit_bytes=56 * 1024 * 1024),
        cost_estimate=pl.CostEstimate(
            flops=4 * BLK * HLOC * GRP * BLK * 4 * DH, bytes_accessed=4 * 1024 * 1024,
            transcendentals=HLOC * GRP * BLK * BLK * 4),
        name="window_attention",
    )(chosen, query, keys, values)


def solution(mesh):
    in_specs = (
        P(("seq", "head"), None),
        P(("seq", "head"), None),
        P(("seq", "head"), None),
        P("seq", "head", None),
    )
    return jax.shard_map(
        on_device, mesh=mesh, in_specs=in_specs, out_specs=P(("seq", "head"), None), check_vma=False
    )
```

```python
import math

import jax
import jax.numpy as jnp
from jax import lax
from jax.experimental import pallas as pl
from jax.experimental.pallas import tpu as pltpu
from jax.sharding import PartitionSpec as P

HQ = 32
HK = 8
DH = 128
BLK = 512
TOPK = 3
GRP = HQ // HK
NHEAD = 4
HLOC = HK // NHEAD
TOK = BLK // NHEAD
NX = 4
SLOTS = 13
GROUPS = 2 * HLOC
PARTS = 2
PIECES = GROUPS * PARTS
ROWS = BLK // PARTS
WIDE = GRP * DH
STRIP = 32
NEG = -1e30
RATE = 1.0 / math.sqrt(DH)
MESH = pl.DeviceIdType.MESH

ROUTES = {
    0: [
        (0, 0), (0, "Z", 0, 4), (0, "P", 0, 1), (0, "M", 0, 3), (2, 4),
        (2, "P", 4, 5), (4, 1), (4, "Z", 1, 5), (4, 3), (4, "M", 3, 6),
        (6, 2), (6, "Z", 2, 6), (6, 5), (8, 6),
    ],
    1: [
        (0, 0), (0, "Z", 0, 4), (0, "P", 0, 1), (2, 4), (2, "M", 4, 3),
        (2, "P", 4, 5), (2, 1), (4, 3), (4, 5), (6, 2),
        (6, "Z", 2, 6), (8, 6),
    ],
    2: [
        (0, 0), (0, "Z", 0, 4), (0, "P", 0, 1), (2, 4), (2, "M", 4, 3),
        (2, 1), (2, "P", 1, 2), (4, 3), (4, "M", 3, 2), (4, 2),
        (4, "Z", 2, 6), (4, 5), (6, 6),
    ],
    3: [
        (0, 0), (0, "Z", 0, 4), (2, 4), (2, "P", 4, 1), (2, "M", 4, 3),
        (2, 3), (2, "M", 3, 2), (2, 1), (2, "Z", 1, 5), (4, 5),
        (4, "P", 5, 2), (4, 2), (5, 6),
    ],
}
TICKS = 16
ITEM_TICKS = (9, 10, 10, 11, 11, 12, 12, 12, 13, 13, 14, 15, 15, 15, 15, 15)


def kernel(nseq, chosen, query, keys, values, out, kv, blocks, qbuf, obuf, scores, weights, totals, flipped, turned, relay,
           own_send, own_recv, q_send, q_recv, win_send, win_recv, sib_send, sib_recv,
           out_send, out_recv, relay_recv, relay_send, local_sem):
    nz = nseq // (2 * NX)
    seq = lax.axis_index("seq")
    y = lax.axis_index("head")
    core = lax.rem(seq, 2)
    x = lax.rem(seq // 2, NX)
    z = seq // (2 * NX)

    def at(zz, xx):
        return ((zz * NX + xx) * 2 + core, y)

    up = at(lax.rem(z + 1, nz), x)
    down = at(lax.rem(z + nz - 1, nz), x)
    right = at(z, lax.rem(x + 1, NX))
    left = at(z, lax.rem(x + NX - 1, NX))
    sibling = (seq + 1 - 2 * core, y)

    def partner(o):
        return (seq, lax.rem(y + o, NHEAD))

    place = z * NX + x
    barrier = pltpu.get_barrier_semaphore()

    def greet(who):
        pl.semaphore_signal(barrier, inc=1, device_id=who, device_id_type=MESH)

    for who in [right, left, sibling, partner(1), partner(2), partner(3)]:
        greet(who)
    pl.when(z < nz - 1)(lambda: greet(up))
    pl.when(z > 0)(lambda: greet(down))
    edge = (z == 0) | (z == nz - 1)
    pl.when(edge)(lambda: pl.semaphore_wait(barrier, 7))
    pl.when(jnp.logical_not(edge))(lambda: pl.semaphore_wait(barrier, 8))

    def columns(start, width):
        return pl.ds(pl.multiple_of(start, DH), width)

    def remote(src, dst, send, recv, to):
        return pltpu.make_async_remote_copy(
            src_ref=src, dst_ref=dst, send_sem=send, recv_sem=recv, device_id=to, device_id_type=MESH)

    own_rows = pl.ds(pl.multiple_of(y * TOK, TOK), TOK)

    def kv_source(h, i, to_y):
        return (keys, values)[i].at[:, columns((to_y * HLOC + h) * DH, DH)]

    def kv_copy(o, h, i):
        to, g = partner(o), 2 * h + i
        return remote(kv_source(h, i, to[1]), kv.at[g, 0, own_rows], own_send.at[g], own_recv.at[g], to)

    def kv_local(h, i):
        return pltpu.make_async_copy(kv_source(h, i, y), kv.at[2 * h + i, 0, own_rows], local_sem.at[2 * h + i])

    def q_source(h, to_y):
        return query.at[:, columns((to_y * HLOC + h) * WIDE, WIDE)]

    def q_copy(o, h):
        to = partner(o)
        return remote(q_source(h, to[1]), qbuf.at[h, y], q_send.at[h], q_recv.at[h], to)

    def q_local(h):
        return pltpu.make_async_copy(q_source(h, y), qbuf.at[h, y], local_sem.at[GROUPS + h])

    def q_local_wait(h):
        pltpu.make_async_copy(qbuf.at[h, 0], qbuf.at[h, 0], local_sem.at[GROUPS + h]).wait()

    def out_place(to_y, h):
        return out.at[:, columns((to_y * HLOC + h) * WIDE, WIDE)]

    def out_copy(o, h):
        to = partner(o)
        return remote(obuf.at[h, to[1]], out_place(y, h), out_send.at[h], out_recv.at[h], to)

    def out_local(h):
        return pltpu.make_async_copy(obuf.at[h, y], out_place(y, h), local_sem.at[GROUPS + HLOC + h])

    def three(ref, send, recv):
        return remote(ref, ref, send, recv, sibling)

    def kv_three(g):
        return three(kv.at[g, 0, pl.ds(0, 3 * TOK)], own_send.at[g], own_recv.at[g])

    def kv_local_wait(g):
        ref = kv.at[g, 0, pl.ds(0, TOK)]
        pltpu.make_async_copy(ref, ref, local_sem.at[g]).wait()

    def q_three(h):
        return three(qbuf.at[h, pl.ds(0, 3)], q_send.at[h], q_recv.at[h])

    def out_three(h):
        return three(obuf.at[h, pl.ds(0, 3)], out_send.at[h], out_recv.at[h])

    def send_q(h):
        for o in (2, 1, 3):
            q_copy(o, h).start()
        q_local(h).start()

    def half(k):
        return pl.ds(k * TOK // 2, TOK // 2)

    def out_via(h, k):
        return remote(obuf.at[h, partner(2)[1], half(k)], relay.at[h, k], out_send.at[h], relay_recv.at[h, k],
                      partner(1 + 2 * k))

    def out_pass(h):
        for k in range(2):
            ref = relay.at[h, k]
            remote(ref, ref, out_send.at[h], relay_recv.at[h, k], sibling).wait_recv()
            remote(ref, out_place(partner(3 - 2 * k)[1], h).at[half(k)], relay_send.at[h], out_recv.at[h],
                   partner(1 + 2 * k)).start()

    def piece(m, slot):
        return kv.at[m // PARTS, slot, pl.ds(pl.multiple_of(lax.rem(m, PARTS) * ROWS, ROWS), ROWS)]

    def forward(m, to, r, into):
        remote(piece(m, 2 * r), piece(m, 2 * into),
               win_send.at[m // PARTS], win_recv.at[m, into - 1], to).start()

    def arrived(m, r):
        remote(piece(m, 2 * r), piece(m, 2 * r), win_send.at[m // PARTS], win_recv.at[m, r - 1], up).wait_recv()

    def share(m, r):
        g = m // PARTS

        def go():
            remote(kv.at[g, 2 * r], kv.at[g, 2 * r + 1 - 2 * core], sib_send.at[g], sib_recv.at[g], sibling).start()

        whole_slot = lax.rem(m, PARTS) == PARTS - 1
        if r == 0:
            whole_slot = whole_slot & (core == 0)
        elif r == 6:
            whole_slot = whole_slot & (core == 1)
        pl.when(whole_slot)(go)

    def own(m):
        @pl.when(lax.rem(m, PARTS) == 0)
        def _():
            kv_three(m // PARTS).wait_recv()
            kv_local_wait(m // PARTS)

    def event(m, entry):
        if len(entry) > 2:
            there = place >= entry[2]
            if entry[1] == "Z":
                there = there & (z < nz - 1)
            to = {"Z": up, "P": right, "M": left}[entry[1]]
            pl.when(there)(lambda: forward(m, to, entry[2], entry[3]))
        else:
            if entry[1] == 0:
                own(m)
            else:
                pl.when(place >= entry[1])(lambda: arrived(m, entry[1]))
            share(m, entry[1])

    def step(n):
        for xx in range(NX):
            @pl.when(x == xx)
            def _():
                for lag in sorted({entry[0] for entry in ROUTES[xx]}):
                    m = n - lag

                    @pl.when((m >= 0) & (m < PIECES))
                    def _():
                        for entry in ROUTES[xx]:
                            if entry[0] == lag:
                                event(m, entry)

    def send_kv(h, _):
        for i in range(2):
            for o in (2, 1, 3):
                kv_copy(o, h, i).start()
            kv_local(h, i).start()
        return 0

    lax.fori_loop(0, HLOC, send_kv, 0)

    def whole(g, slots=6):
        ref = kv.at[g, pl.ds(0, slots)]
        return remote(ref, ref, sib_send.at[g], sib_recv.at[g], sibling)

    def picks(h):
        valid, slot = [None], [0]
        for t in range(TOPK):
            pick = chosen[0, h, t]
            valid.append(pick >= 0)
            slot.append(seq - pick)
        return valid, slot

    def collect(g):
        _, slot = picks(g // 2)

        def part(i, _):
            rows = pl.ds(pl.multiple_of(i * DH, DH), DH)
            block = kv[g, 0, rows]
            blocks[g % 2, 0, rows] = block
            found = [block] * TOPK
            for d in range(1, SLOTS):
                block = kv[g, d, rows]
                for t in range(TOPK):
                    found[t] = jnp.where(slot[t + 1] == d, block, found[t])
            for t in range(TOPK):
                blocks[g % 2, t + 1, rows] = found[t]
            return 0

        lax.fori_loop(0, BLK // DH, part, 0)

    behind = (lax.broadcasted_iota(jnp.int32, (TOK, TOK), 0)
              - lax.broadcasted_iota(jnp.int32, (TOK, TOK), 1))

    def fold(op, start, rows):
        for i in range(0, rows.shape[0], 8):
            start = op(start, rows[i:i + 8])
        return start

    def order(j):
        return lax.rem(2 + 3 * j + 3 * (j // 2) + 2 * (j // 3), NHEAD)

    def weigh(h, j):
        @pl.when(j == 0)
        def _():
            whole(2 * h).wait_recv()
            q_three(h).wait_recv()
            q_local_wait(h)
            collect(2 * h)

        c = lax.rem(y + order(j), NHEAD)
        for g in range(GRP):
            turned[:, g * TOK:(g + 1) * TOK] = qbuf[h, c, :, g * DH:(g + 1) * DH].T
        valid, _ = picks(h)
        top = None
        for t in range(TOPK + 1):
            high = jnp.full((8, GRP * TOK), NEG, jnp.float32)
            for i in range(BLK // TOK):
                s = jnp.dot(blocks[0, t, i * TOK:(i + 1) * TOK], turned[...], preferred_element_type=jnp.float32)
                if t == 0:
                    seen = behind <= (c - i) * TOK
                    s = jnp.concatenate(
                        [jnp.where(seen, s[:, g * TOK:(g + 1) * TOK], NEG) for g in range(GRP)], axis=1)
                scores[t, i * TOK:(i + 1) * TOK] = s
                high = fold(jnp.maximum, high, s)
            high = jnp.max(high, axis=0, keepdims=True)
            top = high if t == 0 else jnp.maximum(top, jnp.where(valid[t], high, NEG))
        total = jnp.zeros((8, GRP * TOK), jnp.float32)
        for t in range(TOPK + 1):
            shift = top if t == 0 else jnp.where(valid[t], top, -NEG)

            def band(i, total):
                rows = pl.ds(pl.multiple_of(i * STRIP, STRIP), STRIP)
                p = jnp.exp((scores[t, rows] - shift) * RATE)
                weights[c, pl.ds(pl.multiple_of(t * BLK + i * STRIP, STRIP), STRIP)] = p.astype(jnp.bfloat16)
                return fold(jnp.add, total, p)

            total = lax.fori_loop(0, BLK // STRIP, band, total, unroll=4)
        totals[c] = jnp.broadcast_to(jnp.sum(total, axis=0, keepdims=True), (8, GRP * TOK))

    def attend(h, j):
        @pl.when(j == 0)
        def _():
            whole(2 * h + 1).wait_recv()
            collect(2 * h + 1)
            for t in range(TOPK + 1):
                flipped[:, t * BLK:(t + 1) * BLK] = blocks[1, t].T

        o = order(j)
        c = lax.rem(y + o, NHEAD)
        for side in range(2):
            q0 = side * 2 * TOK
            acc = jnp.dot(flipped[...], weights[c, :, q0:q0 + 2 * TOK], preferred_element_type=jnp.float32)
            res = acc / totals[c, 0:1, q0:q0 + 2 * TOK]
            for g in range(2):
                obuf[h, c, :, q0 + g * DH:q0 + (g + 1) * DH] = res[:, g * TOK:(g + 1) * TOK].T.astype(jnp.bfloat16)
        for k in (1, 3):
            pl.when(o == k)(lambda: out_copy(k, h).start())

        @pl.when(o == 2)
        def _():
            for k in range(2):
                out_via(h, k).start()

        pl.when(o == 0)(lambda: out_local(h).start())

    def before(n):
        return sum((n + 63 - tick) // 64 for tick in ITEM_TICKS)

    def item(k, _):
        h, kind, j = k // 8, lax.rem(k // 4, 2), lax.rem(k, 4)
        pl.when(kind == 0)(lambda: weigh(h, j))
        pl.when(kind == 1)(lambda: attend(h, j))
        pl.when((k == 9) | (k == 15))(lambda: out_pass(k // 15))
        return 0

    def tick(n, _):
        step(n)
        pl.when((n == 1) | (n == 3))(lambda: send_q(n // 3))
        lax.fori_loop(before(n), before(n + 1), item, 0)
        return 0

    lax.fori_loop(0, TICKS, tick, 0)

    def sent(g):
        for xx in range(NX):
            for low, high in ((0, 1), (1, 2), (2, nz - 1), (nz - 1, nz)):
                count = 0
                for entry in ROUTES[xx]:
                    if len(entry) > 2 and low * NX + xx >= entry[2] and (entry[1] != "Z" or low < nz - 1):
                        count += 1
                if count == 0:
                    continue

                @pl.when((x == xx) & (z >= low) & (z < high))
                def _():
                    ref = kv.at[g, pl.ds(0, count)]
                    remote(ref, ref, win_send.at[g], sib_recv.at[g], right).wait_send()

    def finish(g, _):
        kv_three(g).wait_send()
        whole(g).wait_send()
        sent(g)
        return 0

    lax.fori_loop(0, GROUPS, finish, 0)
    for h in range(HLOC):
        q_three(h).wait_send()
        out_three(h).wait()
        three(relay.at[h], relay_send.at[h], out_recv.at[h]).wait_send()
        out_local(h).wait()


def on_device(query, keys, values, chosen):
    nseq = lax.axis_size("seq")
    dma = pltpu.SemaphoreType.DMA
    any_spec = pl.BlockSpec(memory_space=pl.ANY)

    def body(*refs):
        kernel(nseq, *refs)

    return pl.pallas_call(
        body,
        out_shape=pltpu.VMEM(query.shape, jnp.bfloat16),
        in_specs=[pl.BlockSpec(memory_space=pltpu.SMEM), any_spec, any_spec, any_spec],
        out_specs=pl.BlockSpec(memory_space=pltpu.VMEM),
        scratch_shapes=[
            pltpu.VMEM((GROUPS, SLOTS, BLK, DH), jnp.bfloat16),
            pltpu.VMEM((2, TOPK + 1, BLK, DH), jnp.bfloat16),
            pltpu.VMEM((HLOC, NHEAD, TOK, WIDE), jnp.bfloat16),
            pltpu.VMEM((HLOC, NHEAD, TOK, WIDE), jnp.bfloat16),
            pltpu.VMEM((TOPK + 1, BLK, GRP * TOK), jnp.float32),
            pltpu.VMEM((NHEAD, (TOPK + 1) * BLK, GRP * TOK), jnp.bfloat16),
            pltpu.VMEM((NHEAD, 8, GRP * TOK), jnp.float32),
            pltpu.VMEM((DH, (TOPK + 1) * BLK), jnp.bfloat16),
            pltpu.VMEM((DH, GRP * TOK), jnp.bfloat16),
            pltpu.VMEM((HLOC, 2, TOK // 2, WIDE), jnp.bfloat16),
            dma((GROUPS,)), dma((GROUPS,)),
            dma((HLOC,)), dma((HLOC,)),
            dma((GROUPS,)), dma((PIECES, 6)),
            dma((GROUPS,)), dma((GROUPS,)),
            dma((HLOC,)), dma((HLOC,)),
            dma((HLOC, 2)), dma((HLOC,)),
            dma((GROUPS + 2 * HLOC,)),
        ],
        compiler_params=pltpu.CompilerParams(
            collective_id=0, has_side_effects=True, vmem_limit_bytes=56 * 1024 * 1024),
        cost_estimate=pl.CostEstimate(
            flops=4 * BLK * HLOC * GRP * BLK * 4 * DH, bytes_accessed=4 * 1024 * 1024,
            transcendentals=HLOC * GRP * BLK * BLK * 4),
        name="window_attention",
    )(chosen, query, keys, values)


def solution(mesh):
    in_specs = (
        P(("seq", "head"), None),
        P(("seq", "head"), None),
        P(("seq", "head"), None),
        P("seq", "head", None),
    )
    return jax.shard_map(
        on_device, mesh=mesh, in_specs=in_specs, out_specs=P(("seq", "head"), None), check_vma=False
    )
```
